32 devices in a mesh: member: 2 (over y), tile: 4 (over z), sub: 2 (over x), comp: 2 (over core).
Axes of the slice: x: 2, y: 2, z: 4, core: 2. Of those that a mesh axis runs over, the one named last changes fastest.
Arguments:
- air_exchanges: bfloat16 [4, 8, 131072], P(('member', 'comp'), None, ('tile', 'sub')), parts along dimension 0, may hold values from -6 to 6
- air_destination: int32 [2, 131072, 1], P('comp', ('tile', 'sub')), may hold values from 0 to 7, as said below
- diagonal_group_pointer: int32 [2, 4, 2, 64, 2], P('comp', 'tile', 'sub'), may hold values from 0 to 319
- interpolation_factors: bfloat16 [2, 4, 2, 64, 2, 128, 128], P('comp', 'tile', 'sub'), may hold values from -0.375 to 0.375
- marine_fields: float32 [4, 3, 256, 256], P(('member', 'comp'), None, 'tile', 'sub'), parts along dimension 0, may hold values from -6 to 6
- skin_warmth_anomaly: float32 [4, 256, 256], P(('member', 'comp'), 'tile', 'sub'), parts along dimension 0, may hold values from -6 to 6
- gravity_bathymetry: float32 [2, 256, 256], P('comp', 'tile', 'sub'), may hold values from 0.1 to 0.9
- marine_indicator: int32 [2, 256, 256], P('comp', 'tile', 'sub'), may hold values 0 or 1
Outputs:
- ocean_out: float32 [4, 3, 256, 256], P(('member', 'comp'), None, 'tile', 'sub'), parts along dimension 0
- atm_sst: float32 [4, 131072], P(('member', 'comp'), ('tile', 'sub')), parts along dimension 0
The draws below stay inside these ranges and needn't reach their ends.
There are 2 independent parts, one for each index of `member`. The reference program is written for one: setup_inputs(seed, part) draws one part's arguments, and reference() takes and returns one part's arrays. A program takes and returns all parts, laid end to end along the dimension named above; an argument that names none is the same for every part. Nothing has to cross between parts.
Inputs may be any that keep to these rules, and one draw needn't show every extreme that they name: `air_destination`: the ocean tile t * 2 + s that atmosphere column i intersects; with source = i // 16384, it is (source + o) mod 8 for some o with |o| <= 2. Among the 16384 columns of one device no tile is named more than 8192 times, and in every basin some device's columns name one tile exactly 8192 times.
All inputs are finite; a program needn't handle non-finite values. No bound on the sum of `marine_indicator` on one device may be relied on, other than what follows from the above.
Results may differ from the reference program's by a relative error of at most 0.0028.
Values may be sent and summed in bfloat16 or wider, within the bound.
No kernel may reach another device: no remote copies, remote signals or barrier semaphores. Data moves between devices by JAX's collectives and lax.ppermute only.
A program may use at most 128 MiB of HBM per device.

```python
import math
import jax
import jax.numpy as jnp
from jax import lax

NF = 8
ACOL = 16384
PARCEL_LATS = 64
PARCEL_LONGS = 128
RB = 128
BW = 2
NEIGHBOR_TILES = 5
SUBS = 8
SEA_REGIONS = 2
TILES = 8
CAP = 8192
ARRIVAL_GROUPS = 320
NRB = 64
ATOT = 131072
MERIDIONAL_CELLS = 256
ZONAL_CELLS = 256
N_TILE = 4
N_SUB = 2


def draw_air_destination(key, part):
    key = jax.random.fold_in(key, 11)
    key_centre, key_forced, key_weights, key_order = jax.random.split(key, 4)
    groups = SEA_REGIONS * TILES
    centre = jax.random.randint(key_centre, (groups,), ACOL // 4, CAP + 1)
    forced = jax.random.randint(key_forced, (SEA_REGIONS, 1), 0, TILES)
    is_forced = (jnp.arange(TILES, dtype=jnp.int32)[None, :] == forced).reshape(groups)
    centre = jnp.where(is_forced, CAP, centre).astype(jnp.int32)
    remain = ACOL - centre
    factor_matrix = jax.random.randint(key_weights, (groups, NEIGHBOR_TILES - 1), 1, 5)
    share = remain[:, None] * factor_matrix // jnp.sum(factor_matrix, axis=1, keepdims=True)
    share = share.at[:, 0].add(remain - jnp.sum(share, axis=1))
    counts = jnp.concatenate([share[:, :2], centre[:, None], share[:, 2:]], axis=1)
    ends = jnp.cumsum(counts, axis=1)
    position = jnp.arange(ACOL, dtype=jnp.int32)
    offsets = jnp.sum((position[None, :, None] >= ends[:, None, :]).astype(jnp.int32), axis=2)
    orders = jax.vmap(lambda single: jax.random.permutation(single, ACOL))(jax.random.split(key_order, groups))
    offsets = jnp.take_along_axis(offsets, orders, axis=1)
    owner = jnp.arange(groups, dtype=jnp.int32) % TILES
    tiles = jnp.mod(owner[:, None] + offsets - 2, TILES).astype(jnp.int32)
    return tiles.reshape(SEA_REGIONS, ATOT, 1)


def place_ends(entries, key, least, largest):
    longest = entries.shape.index(max(entries.shape))
    spots = []
    for shift in (0, 1):
        where = [jax.random.randint(jax.random.fold_in(key, axis), (), 0, length) for axis, length in enumerate(entries.shape)]
        where[longest] = (where[longest] + shift) % entries.shape[longest]
        spots.append(tuple(where))
    return entries.at[spots[0]].set(least).at[spots[1]].set(largest)


def block_levels(stream_key, dims, shards, low, top_value):
    factor_of, own = 1.0, jax.random.fold_in(stream_key, 6)
    for dim, shards_of in shards:
        heights = jnp.exp(jax.random.uniform(jax.random.fold_in(own, dim), (shards_of,), jnp.float32, low / len(shards), top_value / len(shards)))
        factor_of = factor_of * jnp.repeat(heights, dims[dim] // shards_of).reshape([-1 if axis == dim else 1 for axis in range(len(dims))])
    return factor_of


def noise(stream_key, dims, spread, limit, cuts=(), held_as=jnp.bfloat16):
    values = jax.random.normal(stream_key, dims, jnp.float32) * spread
    if len(cuts) > 0:
        values = block_levels(stream_key, dims, cuts, -0.22, 0.18) * values
    return jnp.clip(values, min=-limit, max=limit).astype(held_as)


def setup_inputs(seed: int = 0, part: int = 0) -> dict:
    key_of = jax.random.split(jax.random.key(seed), 9)
    part_splits = jax.random.split(jax.random.fold_in(key_of[8], part), 9)
    return {
        "air_exchanges": noise(part_splits[0], (SEA_REGIONS, NF, ATOT), 1.0, 6.0, ((0, 2), (2, 8))),
        "air_destination": draw_air_destination(jax.random.fold_in(key_of[8], 71), part),
        "diagonal_group_pointer": place_ends(jax.random.randint(key_of[2], (SEA_REGIONS, N_TILE, N_SUB, NRB, BW), 0, ARRIVAL_GROUPS), jax.random.fold_in(key_of[2], 1), 0, ARRIVAL_GROUPS - 1).astype(jnp.int32),
        "interpolation_factors": noise(key_of[3], (SEA_REGIONS, N_TILE, N_SUB, NRB, BW, RB, RB), (BW * RB) ** -0.5, 0.375, ((0, 2), (1, 4), (2, 2))),
        "marine_fields": noise(part_splits[4], (SEA_REGIONS, 3, MERIDIONAL_CELLS, ZONAL_CELLS), 1.0, 6.0, ((0, 2), (2, 4), (3, 2)), jnp.float32),
        "skin_warmth_anomaly": noise(part_splits[5], (SEA_REGIONS, MERIDIONAL_CELLS, ZONAL_CELLS), 1.0, 6.0, ((0, 2), (1, 4), (2, 2)), jnp.float32),
        "gravity_bathymetry": jnp.clip(jnp.exp(math.log(0.9) - 2.1972245 * jax.random.uniform(key_of[6], (SEA_REGIONS, MERIDIONAL_CELLS, ZONAL_CELLS), jnp.float32) ** block_levels(key_of[6], (SEA_REGIONS, MERIDIONAL_CELLS, ZONAL_CELLS), ((0, 2), (1, 4), (2, 2)), -0.2, 0.2)), 0.1, 0.9),
        "marine_indicator": place_ends((jax.random.randint(key_of[7], (SEA_REGIONS, MERIDIONAL_CELLS, ZONAL_CELLS), 0, 4) < 3).astype(jnp.int32), jax.random.fold_in(key_of[7], 1), 0, 1),
    }


def column_ranks(destination_listing, parcel_total):
    onehot = (destination_listing[:, None] == jnp.arange(parcel_total, dtype=jnp.int32)[None, :]).astype(jnp.int32)
    before = jnp.cumsum(onehot, axis=0) - onehot
    return lax.optimization_barrier(jnp.sum(before * onehot, axis=1)).astype(jnp.int32)

def difference_x(values):
    padded = jnp.pad(values, ((0, 0), (1, 1)))
    return 0.5 * (padded[:, 2:] - padded[:, :-2])

def difference_y(values):
    padded = jnp.pad(values, ((1, 1), (0, 0)))
    return 0.5 * (padded[2:, :] - padded[:-2, :])

def surface_forcing(fields):
    wind_speed = jnp.sqrt(fields[0] * fields[0] + fields[1] * fields[1] + 1.0)
    stress_x = 0.2 * wind_speed * fields[0]
    stress_y = 0.2 * wind_speed * fields[1]
    freshwater = 0.5 * (fields[3] - fields[2])
    thermal_forcing = fields[7] + fields[6] - fields[4] - fields[5]
    return (stress_x, stress_y, freshwater, thermal_forcing)

def barotropic_step(ocean_now, statics, coriolis):
    height, east_flow, north_flow = ocean_now
    liquid_indicator, depth_map, stress_x, stress_y, freshwater = statics
    height = liquid_indicator * (height - (difference_x(east_flow) + difference_y(north_flow)) + freshwater)
    slope_x = difference_x(height)
    slope_y = difference_y(height)
    new_east = liquid_indicator * (east_flow + coriolis * north_flow - depth_map * slope_x + stress_x)
    new_north = liquid_indicator * (north_flow - coriolis * east_flow - depth_map * slope_y + stress_y)
    return (height, new_east, new_north)

def remap_forward(received, narrow_longitudes, intersect_factor):
    blocks = received.reshape(received.shape[0], -1, intersect_factor.shape[2])[:, narrow_longitudes, :]
    result = jnp.einsum('kwab,fkwb->fka', intersect_factor.astype(jnp.float32), blocks.astype(jnp.float32))
    return result.reshape(received.shape[0], -1)

def backward_interpolation(departing_warmth, narrow_longitudes, intersect_factor, group_total):
    group_breadth = intersect_factor.shape[2]
    exchange_shares = jnp.einsum('ylub,yu->ylb', intersect_factor.astype(jnp.float32), departing_warmth.astype(jnp.float32).reshape(-1, group_breadth))
    select = (narrow_longitudes[:, :, None] == jnp.arange(group_total, dtype=jnp.int32)[None, None, :]).astype(jnp.float32)
    return jnp.einsum('kwc,kwb->cb', select, exchange_shares, precision=lax.Precision.HIGHEST).reshape(-1)

def reference(air_exchanges, air_destination, diagonal_group_pointer, interpolation_factors, marine_fields, skin_warmth_anomaly, gravity_bathymetry, marine_indicator):
    latitudes_each_parcel = MERIDIONAL_CELLS // PARCEL_LATS
    longitudes_each_parcel = ZONAL_CELLS // PARCEL_LONGS
    parcel_total = latitudes_each_parcel * longitudes_each_parcel
    coriolis = (0.1 + 0.2 * (jnp.arange(MERIDIONAL_CELLS, dtype=jnp.float32) + 0.5) / MERIDIONAL_CELLS)[:, None]
    source = jnp.arange(ATOT, dtype=jnp.int32) // ACOL
    marine_field_sets = []
    warmth_entries = []
    for drainage_region_number in range(SEA_REGIONS):
        destination_listing = air_destination[drainage_region_number, :, 0]
        offsets = jnp.mod(destination_listing - source + 2, parcel_total).astype(jnp.int32)
        ranking = lax.map(lambda route_block: column_ranks(route_block, parcel_total), destination_listing.reshape(parcel_total, ACOL)).reshape(ATOT)
        arrival_position = offsets * CAP + ranking
        received = jnp.zeros((NF, parcel_total, NEIGHBOR_TILES * CAP), jnp.bfloat16).at[:, destination_listing, arrival_position].set(air_exchanges[drainage_region_number])
        narrow_latitudes = diagonal_group_pointer[drainage_region_number].reshape(parcel_total, NRB, BW)
        factor_matrix = interpolation_factors[drainage_region_number].reshape(parcel_total, NRB, BW, RB, RB)
        remapped = lax.map(lambda compacted_latitudes: remap_forward(compacted_latitudes[0], compacted_latitudes[1], compacted_latitudes[2]), (jnp.moveaxis(received, 1, 0), narrow_latitudes, factor_matrix))
        remapped = remapped.reshape(latitudes_each_parcel, longitudes_each_parcel, NF, PARCEL_LATS, PARCEL_LONGS).transpose(2, 0, 3, 1, 4).reshape(NF, MERIDIONAL_CELLS, ZONAL_CELLS)
        stress_x, stress_y, freshwater, thermal_forcing = surface_forcing(remapped)
        liquid_indicator = marine_indicator[drainage_region_number].astype(jnp.float32)
        statics = (liquid_indicator, gravity_bathymetry[drainage_region_number], stress_x, stress_y, freshwater)
        ocean_now = (marine_fields[drainage_region_number, 0], marine_fields[drainage_region_number, 1], marine_fields[drainage_region_number, 2])
        for counter in range(SUBS):
            ocean_now = barotropic_step(ocean_now, statics, coriolis)
        marine_field_sets.append(jnp.stack(ocean_now))
        departing_warmth = lax.optimization_barrier((skin_warmth_anomaly[drainage_region_number] + 0.25 * liquid_indicator * thermal_forcing).astype(jnp.bfloat16))
        departing_warmth = departing_warmth.reshape(latitudes_each_parcel, PARCEL_LATS, longitudes_each_parcel, PARCEL_LONGS).transpose(0, 2, 1, 3).reshape(parcel_total, PARCEL_LATS * PARCEL_LONGS)
        sent_back_results = lax.map(lambda compacted_latitudes: backward_interpolation(compacted_latitudes[0], compacted_latitudes[1], compacted_latitudes[2], ARRIVAL_GROUPS), (departing_warmth, narrow_latitudes, factor_matrix))
        warmth_entries.append(sent_back_results[destination_listing, arrival_position])
    return (jnp.stack(marine_field_sets), jnp.stack(warmth_entries))
```

```python
import functools

import jax
import jax.numpy as jnp
from jax import lax
from jax.experimental import pallas as pl
from jax.experimental.pallas import tpu as pltpu
from jax.sharding import PartitionSpec as P

NEIGHBOR_TILES = 5
MIDDLE = NEIGHBOR_TILES // 2
SUBS = 8
LANES = 128
HALO = 2 * SUBS
FIELDS = 8
F32 = jnp.float32
BF16 = jnp.bfloat16
I32 = jnp.int32
VMEM_LIMIT = 48 * 1024 * 1024


def iota(shape, dim):
    return lax.broadcasted_iota(I32, shape, dim)


def dot(a, b):
    return jnp.dot(a, b, preferred_element_type=F32)


def dot_t(a, b):
    return lax.dot_general(a, b, (((1,), (1,)), ((), ())), preferred_element_type=F32)


def ones_where(mask):
    return jnp.where(mask, 1.0, 0.0).astype(BF16)


def offsets_of(destination, count_s, total):
    mine = lax.axis_index("tile") * count_s + lax.axis_index("sub")
    shifted = destination - mine + MIDDLE
    shifted = jnp.where(shifted < 0, shifted + total, shifted)
    return jnp.where(shifted >= total, shifted - total, shifted)


def ranks(offsets):
    rows = offsets.shape[0]
    r, c = iota((LANES, LANES), 0), iota((LANES, LANES), 1)
    before = ones_where(r < c)
    every = jnp.ones((LANES, LANES), BF16)
    earlier = ones_where(iota((rows, rows), 1) < iota((rows, rows), 0))
    result = []
    for o in range(NEIGHBOR_TILES):
        mask = offsets == o
        hot = ones_where(mask)
        inside = dot(hot, before)
        count = dot(hot, every)
        base = dot(earlier, count.astype(BF16))
        result.append((mask, hot, inside, count, base))
    return result


def route_kernel(
    count_s, total, dest_ref, x_ref, *rest
):
    outs = rest[:NEIGHBOR_TILES]
    comb, sorted_scr, place, pos_scr, vec, scal, sem = rest[NEIGHBOR_TILES:]
    blocks = dest_ref.shape[0]
    groups = outs[0].shape[0] // 4
    stride = (groups + 1) * 8
    offsets = offsets_of(dest_ref[...], count_s, total)
    parts = ranks(offsets)
    ones8 = jnp.ones((8, LANES), BF16)
    sub8 = iota((8, blocks), 0)
    before = ones_where(iota((blocks, blocks), 0) < iota((blocks, blocks), 1))
    start_t = jnp.zeros((8, blocks), F32)
    base_t = jnp.zeros((8, blocks), F32)
    starts_t = jnp.zeros((8, blocks), F32)
    start = jnp.zeros((blocks, LANES), F32)
    pos = jnp.zeros((blocks, LANES), F32)
    for o, (mask, hot, inside, count, base) in enumerate(parts):
        pos = jnp.where(mask, start + inside, pos)
        start = start + count
        count_t = dot_t(ones8, hot)
        base_row = dot(count_t.astype(BF16), before)
        base_t = jnp.where(sub8 == o, base_row, base_t)
        starts_t = jnp.where(sub8 == o, start_t, starts_t)
        start_t = start_t + count_t
    starts_t = jnp.where(sub8 == NEIGHBOR_TILES, start_t, starts_t)
    vec[0:8, :] = base_t.astype(I32)
    vec[8:16, :] = starts_t.astype(I32)
    copy = pltpu.make_async_copy(vec, scal, sem)
    copy.start()
    pos_scr[...] = pos.astype(I32)
    f, g = iota((8, 8), 1), jnp.bitwise_and(iota((8, 8), 0), 3)
    plus = ((g == 0) & (f == 0)) | ((g == 1) & (f == 1)) | ((g == 2) & (f == 3)) | ((g == 3) & (f >= 6))
    minus = ((g == 2) & (f == 2)) | ((g == 3) & ((f == 4) | (f == 5)))
    combine = (jnp.where(plus, 1.0, 0.0) - jnp.where(minus, 1.0, 0.0)).astype(BF16)
    comb[...] = dot(combine, x_ref[...]).astype(BF16)
    rows_id = iota((LANES, LANES), 0)

    def sort_step(i, carry):
        for u in range(8):
            b = i * 8 + u
            hot = ones_where(pos_scr[pl.ds(b, 1), :] == rows_id)
            columns = comb[:, pl.ds(pl.multiple_of(b * LANES, LANES), LANES)]
            sorted_scr[pl.ds(pl.multiple_of(b * 8, 8), 8), :] = dot_t(columns, hot)
        return carry

    lax.fori_loop(0, blocks // 8, sort_step, 0)
    copy.wait()
    lane = iota((8, LANES), 1)

    def place_step(i, current):
        current = list(current)
        for u in range(4):
            b = i * 4 + u
            values = sorted_scr[pl.ds(pl.multiple_of(b * 8, 8), 8), :]
            for o in range(NEIGHBOR_TILES):
                base = scal[o, b]
                first = scal[8 + o, b]
                length = scal[9 + o, b] - first
                at = jnp.bitwise_and(base, LANES - 1)
                turned = pltpu.roll(values, jnp.bitwise_and(at - first, LANES - 1), 1)
                merged = jnp.where(lane < at, current[o], turned)
                row = pl.multiple_of(o * stride + lax.shift_right_logical(base, 7) * 8, 8)
                place[pl.ds(row, 8), :] = merged
                current[o] = jnp.where(lane < at + length - LANES, turned, merged)
        return tuple(current)

    current = lax.fori_loop(
        0, blocks // 4, place_step, tuple(jnp.zeros((8, LANES), F32) for _ in range(NEIGHBOR_TILES))
    )
    pair_lane = jnp.where(iota((8, LANES), 0) < 4, lane, lane + LANES)
    upper = iota((groups // 2, 8, LANES), 1) < 4
    slot = iota((groups // 2, 8, LANES), 0) * (2 * LANES) + pair_lane[None]
    for o in range(NEIGHBOR_TILES):
        last = blocks - 1
        count = scal[o, last] + scal[9 + o, last] - scal[8 + o, last]
        row = pl.multiple_of(o * stride + lax.shift_right_logical(count, 7) * 8, 8)
        place[pl.ds(row, 8), :] = current[o]
        tiles = place[o * stride : o * stride + groups * 8, :].reshape(groups // 2, 2, 8, LANES)
        both = jnp.where(upper, tiles[:, 0], tiles[:, 1])
        both = jnp.where(slot < count, both, 0.0)
        outs[o][...] = both.reshape(groups * 4, LANES).astype(BF16)


def prepare_kernel(count_s, total, dest_ref, index_ref, code_ref, *hot_refs):
    blocks = dest_ref.shape[0]
    groups = hot_refs[0].shape[1]
    offsets = offsets_of(dest_ref[...], count_s, total)
    index = jnp.zeros((blocks, LANES), I32)
    code = jnp.zeros((blocks, LANES), I32)
    group_id = iota((blocks, groups), 1)
    for o, (mask, hot, inside, count, base) in enumerate(ranks(offsets)):
        base = base.astype(I32)
        rank = base + inside.astype(I32)
        first = lax.shift_right_logical(base, 7)
        index = jnp.where(mask, jnp.bitwise_and(rank, LANES - 1), index)
        code = jnp.where(mask, 2 * o + lax.shift_right_logical(rank, 7) - first, code)
        hot_refs[o][0:blocks, :] = ones_where(group_id == first[:, :groups])
        hot_refs[o][blocks:, :] = ones_where(group_id == first[:, :groups] + 1)
    index_ref[...] = index
    code_ref[...] = code


def packed_columns(fields, low):
    lane = iota(fields[0].shape, 1)
    packed = fields[0] if low else pltpu.roll(fields[0], HALO, 1)
    for i in range(1, FIELDS):
        turn = (i * HALO + (0 if low else HALO)) % LANES
        packed = jnp.where(
            lane >= i * HALO, pltpu.roll(fields[i], turn, 1) if turn else fields[i], packed
        )
    return packed


def remap_kernel(messages, ptr_ref, *rest):
    arrived = rest[:NEIGHBOR_TILES]
    (row_ref, w_ref, ocean_ref, skin_ref, depth_ref, mask_ref) = rest[NEIGHBOR_TILES : NEIGHBOR_TILES + 6]
    outs = rest[NEIGHBOR_TILES + 6 :]
    forcing_ref, own_ref = outs[:2]
    message_refs = outs[2 : 2 + len(messages)]
    slots, mapped, shares = outs[2 + len(messages) :]
    step = pl.program_id(0)
    per_step = w_ref.shape[0]
    size = arrived[0].shape[0]

    @pl.when(step == 0)
    def _():
        for o in range(NEIGHBOR_TILES):
            slots[o * size : (o + 1) * size, :] = arrived[o][...].astype(F32)
        slots[NEIGHBOR_TILES * size :, :] = jnp.zeros((8, LANES), F32)

    for j in range(per_step):
        k = step * per_step + j
        total = None
        for w in range(2):
            block = slots[pl.ds(ptr_ref[2 * k + w] * 4, 8), :].astype(BF16)
            product = dot_t(block, w_ref[j, w])
            total = product if total is None else total + product
        mapped[j * 8 : j * 8 + 8, :] = total
    u, v, p, h = (mapped[pl.ds(i, per_step, stride=8), :] for i in range(4))
    rows = pl.ds(pl.multiple_of(step * per_step, per_step), per_step)
    speed = jnp.sqrt(u * u + v * v + 1.0)
    forcing_ref[0, rows, :] = 0.2 * speed * u
    forcing_ref[1, rows, :] = 0.2 * speed * v
    forcing_ref[2, rows, :] = 0.5 * p
    sst = (skin_ref[rows, :] + 0.25 * mask_ref[rows, :].astype(F32) * h).astype(BF16).astype(F32)
    sub = iota((per_step, LANES), 0)
    for w in range(2):
        total = None
        for j in range(per_step):
            product = dot(jnp.where(sub == j, sst, 0.0).astype(BF16), w_ref[j, w])
            total = product if total is None else total + product
        shares[pl.ds(step * (2 * per_step) + w, per_step, stride=2), :] = total

    @pl.when(step == pl.num_programs(0) - 1)
    def _():
        count = shares.shape[0]
        every = shares[...]
        high = every.astype(BF16)
        low = (every - high.astype(F32)).astype(BF16)
        groups = own_ref.shape[0]
        returned = []
        for o in range(NEIGHBOR_TILES):
            hot = ones_where(iota((groups, count), 0) + o * groups == row_ref[...])
            returned.append((dot(hot, high) + dot(hot, low)).astype(BF16))
        own_ref[...] = returned[MIDDLE]
        fields = [ocean_ref[0], ocean_ref[1], ocean_ref[2], mask_ref[...].astype(F32), depth_ref[...]]
        fields += [forcing_ref[0], forcing_ref[1], forcing_ref[2]]
        high_columns = packed_columns(fields, False)
        low_columns = packed_columns(fields, True)
        tall = fields[0].shape[0]
        for (pairs, parts), out in zip(messages, message_refs):
            at = 0
            for kind, length in parts:
                if kind[0] == "ret":
                    value = returned[kind[1]]
                else:
                    _, dt, ds = kind
                    span = {1: slice(tall - HALO, tall), 0: slice(0, tall), -1: slice(0, HALO)}[dt]
                    if ds:
                        value = (high_columns if ds > 0 else low_columns)[span]
                    else:
                        value = jnp.concatenate([x[span] for x in fields], axis=0)
                    value = value.astype(BF16)
                out[at : at + length, :] = value
                at += length


def finish_kernel(messages, count_t, count_s, *rest):
    message_refs = rest[: len(messages)]
    own_ref, index_ref, code_ref = rest[len(messages) : len(messages) + 3]
    hot_refs = rest[len(messages) + 3 : len(messages) + 3 + NEIGHBOR_TILES]
    ocean_ref, depth_ref, mask_ref, forcing_ref, out_ref, warm_ref = rest[
        len(messages) + 3 + NEIGHBOR_TILES :
    ]
    t, s = lax.axis_index("tile"), lax.axis_index("sub")
    found = {("ret", MIDDLE): own_ref[...]}
    for (pairs, parts), ref in zip(messages, message_refs):
        at = 0
        for kind, length in parts:
            found[kind] = ref[at : at + length, :]
            at += length
    blocks = index_ref.shape[0]
    index = index_ref[...]
    code = code_ref[...]
    warm = jnp.zeros((blocks, LANES), F32)
    for o in range(NEIGHBOR_TILES):
        lines = dot(hot_refs[o][...], found[("ret", o)])
        for half in range(2):
            picked = jnp.take_along_axis(lines[half * blocks : (half + 1) * blocks], index, axis=1)
            warm = jnp.where(code == 2 * o + half, picked, warm)
    warm_ref[...] = warm

    tall = depth_ref.shape[0]
    full = tall + 2 * HALO

    def halo(dt, ds):
        ok = jnp.bool_(True)
        if dt == 1:
            ok &= t > 0
        if dt == -1:
            ok &= t < count_t - 1
        if ds == 1:
            ok &= s > 0
        if ds == -1:
            ok &= s < count_s - 1
        value = found[("halo", dt, ds)].astype(F32)
        return jnp.where(ok, value, 0.0)

    from_left = jnp.concatenate([halo(1, 1), halo(0, 1), halo(-1, 1)], axis=0)
    from_right = jnp.concatenate([halo(1, -1), halo(0, -1), halo(-1, -1)], axis=0)
    above, below = halo(1, 0), halo(-1, 0)
    lane = iota((full, LANES), 1)
    inner = [ocean_ref[0], ocean_ref[1], ocean_ref[2], mask_ref[...].astype(F32), depth_ref[...]]
    inner += [forcing_ref[0], forcing_ref[1], forcing_ref[2]]
    wide = []
    for i in range(FIELDS):
        rows = slice(i * HALO, (i + 1) * HALO)
        main = jnp.concatenate([above[rows], inner[i], below[rows]], axis=0)
        turn = (LANES - HALO - i * HALO) % LANES
        left = pltpu.roll(from_left, turn, 1) if turn else from_left
        turn = (LANES - i * HALO) % LANES
        right = pltpu.roll(from_right, turn, 1) if turn else from_right
        side = jnp.where(lane < HALO, right, jnp.where(lane >= LANES - HALO, left, 0.0))
        wide.append(jnp.concatenate([main, side], axis=1))
    eta, east, north, m, depth, stress_x, stress_y, fresh = wide
    row = iota((full, 2 * LANES), 0) + (t * tall - HALO)
    coriolis = 0.1 + 0.2 * (row.astype(F32) + 0.5) / (tall * count_t)

    def dx(a):
        return 0.5 * (pltpu.roll(a, 2 * LANES - 1, 1) - pltpu.roll(a, 1, 1))

    def dy(a):
        return 0.5 * (pltpu.roll(a, full - 1, 0) - pltpu.roll(a, 1, 0))

    for _ in range(SUBS):
        eta = m * (eta - (dx(east) + dy(north)) + fresh)
        new_east = m * (east + coriolis * north - depth * dx(eta) + stress_x)
        north = m * (north - coriolis * east - depth * dy(eta) + stress_y)
        east = new_east
    for i, a in enumerate((eta, east, north)):
        out_ref[i] = a[HALO : HALO + tall, :LANES]


def plan_messages(count_t, count_s, groups, tall):
    total = count_t * count_s
    by_distance = {}
    for o in range(NEIGHBOR_TILES):
        if o != MIDDLE:
            by_distance.setdefault(MIDDLE - o, []).append((("ret", o), groups))
    for dt in (-1, 0, 1):
        for ds in (-1, 0, 1):
            if dt or ds:
                length = tall if dt == 0 else (HALO if ds else HALO * FIELDS)
                by_distance.setdefault(dt * count_s + ds, []).append((("halo", dt, ds), length))
    messages, partial = [], []
    for distance, parts in sorted(by_distance.items()):
        if any(kind[0] == "ret" for kind, _ in parts):
            pairs = [(i, (i + distance) % total) for i in range(total)]
            messages.append((pairs, parts))
            continue
        pairs = []
        for (_, dt, ds), _ in parts:
            for t in range(count_t):
                for s in range(count_s):
                    if 0 <= t + dt < count_t and 0 <= s + ds < count_s:
                        pairs.append((t * count_s + s, (t + dt) * count_s + s + ds))
        for other in partial:
            if not {a for a, _ in pairs} & {a for a, _ in other[0]} and not (
                {b for _, b in pairs} & {b for _, b in other[0]}
            ):
                other[0].extend(pairs)
                other[1].extend(parts)
                break
        else:
            partial.append((pairs, list(parts)))
    return messages + partial


def shards(
    air_exchanges,
    air_destination,
    diagonal_group_pointer,
    interpolation_factors,
    marine_fields,
    skin_warmth_anomaly,
    gravity_bathymetry,
    marine_indicator,
):
    axes = ("tile", "sub")
    count_t, count_s = lax.axis_size("tile"), lax.axis_size("sub")
    total = count_t * count_s
    columns = air_destination.shape[1]
    blocks = columns // LANES
    groups = columns // 2 // LANES
    destination = air_destination.reshape(blocks, LANES)
    vmem = pl.BlockSpec(memory_space=pltpu.VMEM)
    params = pltpu.CompilerParams(vmem_limit_bytes=VMEM_LIMIT)
    outbound = pl.pallas_call(
        functools.partial(route_kernel, count_s, total),
        out_shape=[jax.ShapeDtypeStruct((groups * 4, LANES), BF16)] * NEIGHBOR_TILES,
        in_specs=[vmem, vmem],
        out_specs=[vmem] * NEIGHBOR_TILES,
        scratch_shapes=[
            pltpu.VMEM((8, columns), BF16),
            pltpu.VMEM((blocks * 8, LANES), F32),
            pltpu.VMEM((NEIGHBOR_TILES * (groups + 1) * 8, LANES), F32),
            pltpu.VMEM((blocks, LANES), I32),
            pltpu.VMEM((16, blocks), I32),
            pltpu.SMEM((16, blocks), I32),
            pltpu.SemaphoreType.DMA,
        ],
        compiler_params=params,
        name="route",
    )(destination, air_exchanges[0])
    arrived = list(outbound)
    for o in range(NEIGHBOR_TILES):
        if o != MIDDLE:
            pairs = [(i, (i + o - MIDDLE) % total) for i in range(total)]
            arrived[o] = lax.ppermute(outbound[o], axes, pairs)
    prepared = pl.pallas_call(
        functools.partial(prepare_kernel, count_s, total),
        out_shape=[jax.ShapeDtypeStruct((blocks, LANES), I32)] * 2
        + [jax.ShapeDtypeStruct((2 * blocks, groups), BF16)] * NEIGHBOR_TILES,
        in_specs=[vmem],
        out_specs=[vmem] * (2 + NEIGHBOR_TILES),
        compiler_params=params,
        cost_estimate=pl.CostEstimate(flops=2 * 15 * LANES**3, bytes_accessed=2**19, transcendentals=0),
        name="prepare",
    )(destination)

    pointers = diagonal_group_pointer.reshape(-1)
    weights = interpolation_factors[0, 0, 0]
    tall = skin_warmth_anomaly.shape[1]
    messages = plan_messages(count_t, count_s, groups, tall)
    lengths = [sum(n for _, n in parts) for _, parts in messages]
    row_blocks = weights.shape[0]
    per_step = 8
    whole = lambda shape: pl.BlockSpec(shape, lambda i, p: (0,) * len(shape))
    ocean, depth, mask = marine_fields[0], gravity_bathymetry[0], marine_indicator[0]
    outs = pl.pallas_call(
        functools.partial(remap_kernel, messages),
        out_shape=[
            jax.ShapeDtypeStruct((3, tall, LANES), F32),
            jax.ShapeDtypeStruct((groups, LANES), BF16),
        ]
        + [jax.ShapeDtypeStruct((n, LANES), BF16) for n in lengths],
        grid_spec=pltpu.PrefetchScalarGridSpec(
            num_scalar_prefetch=1,
            grid=(row_blocks // per_step,),
            in_specs=[whole((groups * 4, LANES))] * NEIGHBOR_TILES
            + [
                whole((1, 2 * row_blocks)),
                pl.BlockSpec((per_step, 2, LANES, LANES), lambda i, p: (i, 0, 0, 0)),
                whole((3, tall, LANES)),
                whole((tall, LANES)),
                whole((tall, LANES)),
                whole((tall, LANES)),
            ],
            out_specs=[whole((3, tall, LANES)), whole((groups, LANES))]
            + [whole((n, LANES)) for n in lengths],
            scratch_shapes=[
                pltpu.VMEM((NEIGHBOR_TILES * groups * 4 + 8, LANES), F32),
                pltpu.VMEM((per_step * 8, LANES), F32),
                pltpu.VMEM((2 * row_blocks, LANES), F32),
            ],
        ),
        compiler_params=params,
        name="remap",
    )(pointers, *arrived, pointers.reshape(1, -1), weights, ocean, skin_warmth_anomaly[0], depth, mask)
    forcing, own = outs[:2]
    received = [
        lax.ppermute(message, axes, pairs) for message, (pairs, _) in zip(outs[2:], messages)
    ]
    ocean_out, warm = pl.pallas_call(
        functools.partial(finish_kernel, messages, count_t, count_s),
        out_shape=[
            jax.ShapeDtypeStruct((3, tall, LANES), F32),
            jax.ShapeDtypeStruct((blocks, LANES), F32),
        ],
        in_specs=[vmem] * (len(messages) + 3 + NEIGHBOR_TILES + 4),
        out_specs=[vmem] * 2,
        compiler_params=params,
        name="finish",
    )(*received, own, *prepared, ocean, depth, mask, forcing)
    return ocean_out[None], warm.reshape(1, columns)


def solution(mesh):
    return jax.shard_map(
        shards,
        mesh=mesh,
        in_specs=(
            P(("member", "comp"), None, ("tile", "sub")),
            P("comp", ("tile", "sub"), None),
            P("comp", "tile", "sub", None, None),
            P("comp", "tile", "sub", None, None, None, None),
            P(("member", "comp"), None, "tile", "sub"),
            P(("member", "comp"), "tile", "sub"),
            P("comp", "tile", "sub"),
            P("comp", "tile", "sub"),
        ),
        out_specs=(
            P(("member", "comp"), None, "tile", "sub"),
            P(("member", "comp"), ("tile", "sub")),
        ),
        check_vma=False,
    )
```

```python
import functools

import jax
import jax.numpy as jnp
from jax import lax
from jax.experimental import pallas as pl
from jax.experimental.pallas import tpu as pltpu
from jax.sharding import PartitionSpec as P

NEIGHBOR_TILES = 5
MIDDLE = NEIGHBOR_TILES // 2
SUBS = 8
LANES = 128
HALO = 2 * SUBS
FIELDS = 8
F32 = jnp.float32
BF16 = jnp.bfloat16
I32 = jnp.int32
SORT_UNIT = 16
VMEM_LIMIT = 48 * 1024 * 1024


def iota(shape, dim):
    return lax.broadcasted_iota(I32, shape, dim)


def dot(a, b):
    return jnp.dot(a, b, preferred_element_type=F32)


def dot_t(a, b):
    return lax.dot_general(a, b, (((1,), (1,)), ((), ())), preferred_element_type=F32)


def ones_where(mask):
    return jnp.where(mask, 1.0, 0.0).astype(BF16)


def offsets_of(destination, count_s, total):
    mine = lax.axis_index("tile") * count_s + lax.axis_index("sub")
    shifted = destination - mine + MIDDLE
    shifted = jnp.where(shifted < 0, shifted + total, shifted)
    return jnp.where(shifted >= total, shifted - total, shifted)


def ranks(offsets):
    rows = offsets.shape[0]
    r, c = iota((LANES, LANES), 0), iota((LANES, LANES), 1)
    before = ones_where(r < c)
    every = jnp.ones((LANES, LANES), BF16)
    earlier = ones_where(iota((rows, rows), 1) < iota((rows, rows), 0))
    result = []
    for o in range(NEIGHBOR_TILES):
        mask = offsets == o
        hot = ones_where(mask)
        inside = dot(hot, before)
        count = dot(hot, every)
        base = dot(earlier, count.astype(BF16))
        result.append((mask, hot, inside, count, base))
    return result


def route_kernel(count_s, total, x_hbm, dest_hbm, *rest):
    staged = len(rest) - NEIGHBOR_TILES - 8
    sources, rest = rest[: staged // 2], rest[staged // 2 :]
    outs, dest_ref, rest = rest[:NEIGHBOR_TILES], rest[NEIGHBOR_TILES], rest[NEIGHBOR_TILES + 1 :]
    targets, rest = rest[: staged // 2], rest[staged // 2 :]
    x_ref, comb, place, pos_scr, vec, scal, sem = rest
    copies = [
        pltpu.make_async_copy(a, b, sem.at[i])
        for i, (a, b) in enumerate(
            zip((dest_hbm, x_hbm) + tuple(sources), (dest_ref, x_ref) + tuple(targets))
        )
    ]
    for copy in copies:
        copy.start()
    copies[0].wait()
    blocks = dest_ref.shape[0]
    unit = SORT_UNIT
    groups = outs[0].shape[0] // 4
    stride = (groups + 1) * 8
    offsets = offsets_of(dest_ref[...], count_s, total)
    ones8 = jnp.ones((8, LANES), BF16)
    sub8 = iota((8, blocks), 0)
    earlier = ones_where(iota((blocks, blocks), 0) < iota((blocks, blocks), 1))
    before = ones_where(iota((LANES, 2 * LANES), 0) < iota((LANES, 2 * LANES), 1))
    hots = [ones_where(offsets == o) for o in range(NEIGHBOR_TILES)]
    counts = jnp.zeros((8, blocks), F32)
    start_t = jnp.zeros((8, blocks), F32)
    starts = jnp.zeros((8, blocks), F32)
    for o, hot in enumerate(hots):
        count_t = dot_t(ones8, hot)
        counts = jnp.where(sub8 == o, count_t, counts)
        starts = jnp.where(sub8 == o, start_t, starts)
        start_t = start_t + count_t
    base = dot(counts.astype(BF16), earlier).astype(I32)
    counts, starts = counts.astype(I32), starts.astype(I32)
    at = jnp.bitwise_and(base, LANES - 1)
    vec[0:8, :] = sub8 * stride + lax.shift_right_logical(base, 7) * 8
    vec[8:16, :] = jnp.bitwise_and(at - starts, LANES - 1)
    vec[16:24, :] = at
    vec[24:32, :] = at + counts - LANES
    copy = pltpu.make_async_copy(vec, scal, sem.at[len(copies)])
    copy.start()
    start = jnp.zeros((blocks, LANES), F32)
    pos = jnp.zeros((blocks, LANES), F32)
    for o, hot in enumerate(hots):
        inside = dot(hot, before)
        pos = jnp.where(offsets == o, start + inside[:, :LANES], pos)
        start = start + inside[:, LANES:]
    pos_scr[...] = pos.astype(I32)
    f, g = iota((8, 8), 1), jnp.bitwise_and(iota((8, 8), 0), 3)
    plus = ((g == 0) & (f == 0)) | ((g == 1) & (f == 1)) | ((g == 2) & (f == 3)) | ((g == 3) & (f >= 6))
    minus = ((g == 2) & (f == 2)) | ((g == 3) & ((f == 4) | (f == 5)))
    combine = (jnp.where(plus, 1.0, 0.0) - jnp.where(minus, 1.0, 0.0)).astype(BF16)
    copies[1].wait()
    comb[...] = dot(combine, x_ref[...]).astype(BF16)

    lines = iota((LANES, LANES), 0)

    def sort_blocks(i):
        result = []
        for u in range(0, unit, 2):
            b = i * unit + u
            columns = comb[:, pl.ds(pl.multiple_of(b * LANES, 2 * LANES), 2 * LANES)].astype(F32)
            columns = jnp.concatenate([columns[:, :LANES], columns[:, LANES:]], axis=0).astype(BF16)
            hot = [ones_where(pos_scr[pl.ds(b + v, 1), :] == lines) for v in range(2)]
            both = dot_t(columns, jnp.concatenate(hot, axis=0))
            result += [both[:8, :LANES], both[8:, LANES:]]
        return result

    lane = iota((8, LANES), 1)

    def place_blocks(i, values, current):
        current = list(current)
        for u in range(unit):
            b = i * unit + u
            for o in range(NEIGHBOR_TILES):
                turned = pltpu.roll(values[u], scal[8 + o, b], 1)
                merged = jnp.where(lane < scal[16 + o, b], current[o], turned)
                place[pl.ds(pl.multiple_of(scal[o, b], 8), 8), :] = merged
                current[o] = jnp.where(lane < scal[24 + o, b], turned, merged)
        return current

    def step(i, carry):
        values = sort_blocks(i + 1)
        return tuple(place_blocks(i, carry[NEIGHBOR_TILES:], carry[:NEIGHBOR_TILES])) + tuple(values)

    steps = blocks // unit
    current = [jnp.zeros((8, LANES), F32) for _ in range(NEIGHBOR_TILES)]
    values = sort_blocks(0)
    copy.wait()
    carry = lax.fori_loop(0, steps - 1, step, tuple(current) + tuple(values))
    current = place_blocks(steps - 1, carry[NEIGHBOR_TILES:], carry[:NEIGHBOR_TILES])
    pair_lane = jnp.where(iota((8, LANES), 0) < 4, lane, lane + LANES)
    upper = iota((groups // 2, 8, LANES), 1) < 4
    slot = iota((groups // 2, 8, LANES), 0) * (2 * LANES) + pair_lane[None]
    last = blocks - 1
    for o in range(NEIGHBOR_TILES):
        row = scal[o, last] - o * stride
        count = row * (LANES // 8) + scal[24 + o, last] + LANES
        full = lax.shift_right_logical(count, 7) * 8 + o * stride
        place[pl.ds(pl.multiple_of(full, 8), 8), :] = current[o]
        tiles = place[o * stride : o * stride + groups * 8, :].reshape(groups // 2, 2, 8, LANES)
        both = jnp.where(upper, tiles[:, 0], tiles[:, 1])
        both = jnp.where(slot < count, both, 0.0)
        outs[o][...] = both.reshape(groups * 4, LANES).astype(BF16)
    for copy in copies[2:]:
        copy.wait()


def prepare_kernel(count_s, total, dest_ref, index_ref, code_ref, *hot_refs):
    blocks = dest_ref.shape[0]
    groups = hot_refs[0].shape[1]
    offsets = offsets_of(dest_ref[...], count_s, total)
    index = jnp.zeros((blocks, LANES), I32)
    code = jnp.zeros((blocks, LANES), I32)
    group_id = iota((blocks, groups), 1)
    for o, (mask, hot, inside, count, base) in enumerate(ranks(offsets)):
        base = base.astype(I32)
        rank = base + inside.astype(I32)
        first = lax.shift_right_logical(base, 7)
        index = jnp.where(mask, jnp.bitwise_and(rank, LANES - 1), index)
        code = jnp.where(mask, 2 * o + lax.shift_right_logical(rank, 7) - first, code)
        hot_refs[o][0:blocks, :] = ones_where(group_id == first[:, :groups])
        hot_refs[o][blocks:, :] = ones_where(group_id == first[:, :groups] + 1)
    index_ref[...] = index
    code_ref[...] = code


def packed_columns(fields, low):
    lane = iota(fields[0].shape, 1)
    packed = fields[0] if low else pltpu.roll(fields[0], HALO, 1)
    for i in range(1, FIELDS):
        turn = (i * HALO + (0 if low else HALO)) % LANES
        packed = jnp.where(
            lane >= i * HALO, pltpu.roll(fields[i], turn, 1) if turn else fields[i], packed
        )
    return packed


def remap_kernel(messages, *rest):
    arrived = rest[:NEIGHBOR_TILES]
    ptr_hbm, row_ref, w_ref, ocean_ref, skin_ref, depth_ref, mask_ref = rest[
        NEIGHBOR_TILES : NEIGHBOR_TILES + 7
    ]
    outs = rest[NEIGHBOR_TILES + 7 :]
    forcing_ref, own_ref = outs[:2]
    message_refs = outs[2 : 2 + len(messages)]
    slots, mapped, shares, ptr_ref, sem = outs[2 + len(messages) :]
    pointers = pltpu.make_async_copy(ptr_hbm, ptr_ref, sem)
    pointers.start()
    per_step = 8
    size = arrived[0].shape[0]
    for o in range(NEIGHBOR_TILES):
        slots[o * size : (o + 1) * size, :] = arrived[o][...].astype(F32)
    slots[NEIGHBOR_TILES * size :, :] = jnp.zeros((8, LANES), F32)
    pointers.wait()
    sub = iota((per_step, LANES), 0)

    def forward(step):
        for j in range(per_step):
            k = step * per_step + j
            both = [slots[pl.ds(ptr_ref[w, k] * 4, 8), :] for w in range(2)]
            both = jnp.concatenate(both, axis=0).astype(BF16)
            product = dot_t(both, w_ref[k].reshape(2 * LANES, LANES))
            mapped[pl.ds(k * 8, 8), :] = product[:8, :LANES] + product[8:, LANES:]

    def middle(step):
        rows = pl.ds(step * per_step, per_step)
        u, v, p, h = (mapped[pl.ds(step * per_step * 8 + i, per_step, stride=8), :] for i in range(4))
        speed = jnp.sqrt(u * u + v * v + 1.0)
        forcing_ref[0, rows, :] = 0.2 * speed * u
        forcing_ref[1, rows, :] = 0.2 * speed * v
        forcing_ref[2, rows, :] = 0.5 * p
        return (skin_ref[rows, :] + 0.25 * mask_ref[rows, :].astype(F32) * h).astype(BF16).astype(F32)

    def back(step, sst):
        left = []
        for j in range(per_step):
            only = jnp.where(sub == j, sst, 0.0)
            zero = jnp.zeros_like(only)
            left.append(jnp.concatenate([only, zero], axis=0).astype(BF16))
            left.append(jnp.concatenate([zero, only], axis=0).astype(BF16))
        left = jnp.concatenate(left, axis=1)
        right = w_ref[pl.ds(step * per_step, per_step)].reshape(per_step * 2 * LANES, LANES)
        total = dot(left, right)
        for w in range(2):
            rows = slice((w * steps + step) * per_step, (w * steps + step + 1) * per_step)
            shares[rows, :] = total[w * per_step : (w + 1) * per_step]

    steps = w_ref.shape[0] // per_step
    for i in range(steps):
        forward(i)
    for i in range(steps):
        back(i, middle(i))

    every = shares[...]
    high = every.astype(BF16)
    low = (every - high.astype(F32)).astype(BF16)
    split = jnp.concatenate([high, low], axis=1)
    count = shares.shape[0]
    groups = own_ref.shape[0]
    returned = []
    row = jnp.concatenate([row_ref[0:1, :], row_ref[1:2, :]], axis=1)
    for o in range(NEIGHBOR_TILES):
        hot = ones_where(iota((groups, count), 0) + o * groups == row)
        value = dot(hot, split)
        returned.append((value[:, :LANES] + value[:, LANES:]).astype(BF16))
    own_ref[...] = returned[MIDDLE]
    fields = [ocean_ref[0], ocean_ref[1], ocean_ref[2], mask_ref[...].astype(F32), depth_ref[...]]
    fields += [forcing_ref[0], forcing_ref[1], forcing_ref[2]]
    high_columns = packed_columns(fields, False)
    low_columns = packed_columns(fields, True)
    tall = fields[0].shape[0]
    for (pairs, parts), out in zip(messages, message_refs):
        at = 0
        for kind, length in parts:
            if kind[0] == "ret":
                value = returned[kind[1]]
            else:
                _, dt, ds = kind
                span = {1: slice(tall - HALO, tall), 0: slice(0, tall), -1: slice(0, HALO)}[dt]
                if ds:
                    value = (high_columns if ds > 0 else low_columns)[span]
                else:
                    value = jnp.concatenate([x[span] for x in fields], axis=0)
                value = value.astype(BF16)
            out[at : at + length, :] = value
            at += length


def finish_kernel(messages, count_t, count_s, *rest):
    message_refs = rest[: len(messages)]
    own_ref, index_ref, code_ref = rest[len(messages) : len(messages) + 3]
    hot_refs = rest[len(messages) + 3 : len(messages) + 3 + NEIGHBOR_TILES]
    ocean_ref, depth_ref, mask_ref, forcing_ref, out_ref, warm_ref = rest[
        len(messages) + 3 + NEIGHBOR_TILES :
    ]
    t, s = lax.axis_index("tile"), lax.axis_index("sub")
    found = {("ret", MIDDLE): own_ref[...]}
    for (pairs, parts), ref in zip(messages, message_refs):
        at = 0
        for kind, length in parts:
            found[kind] = ref[at : at + length, :]
            at += length
    blocks = index_ref.shape[0]
    index = index_ref[...]
    code = code_ref[...]
    warm = jnp.zeros((blocks, LANES), F32)
    for o in range(NEIGHBOR_TILES):
        lines = dot(hot_refs[o][...], found[("ret", o)])
        for half in range(2):
            picked = jnp.take_along_axis(lines[half * blocks : (half + 1) * blocks], index, axis=1)
            warm = jnp.where(code == 2 * o + half, picked, warm)
    warm_ref[...] = warm

    tall = depth_ref.shape[0]
    full = tall + 2 * HALO

    def halo(dt, ds):
        ok = jnp.bool_(True)
        if dt == 1:
            ok &= t > 0
        if dt == -1:
            ok &= t < count_t - 1
        if ds == 1:
            ok &= s > 0
        if ds == -1:
            ok &= s < count_s - 1
        value = found[("halo", dt, ds)].astype(F32)
        return jnp.where(ok, value, 0.0)

    from_left = jnp.concatenate([halo(1, 1), halo(0, 1), halo(-1, 1)], axis=0)
    from_right = jnp.concatenate([halo(1, -1), halo(0, -1), halo(-1, -1)], axis=0)
    above, below = halo(1, 0), halo(-1, 0)
    lane = iota((full, LANES), 1)
    inner = [ocean_ref[0], ocean_ref[1], ocean_ref[2], mask_ref[...].astype(F32), depth_ref[...]]
    inner += [forcing_ref[0], forcing_ref[1], forcing_ref[2]]
    wide = []
    for i in range(FIELDS):
        rows = slice(i * HALO, (i + 1) * HALO)
        main = jnp.concatenate([above[rows], inner[i], below[rows]], axis=0)
        turn = (LANES - HALO - i * HALO) % LANES
        left = pltpu.roll(from_left, turn, 1) if turn else from_left
        turn = (LANES - i * HALO) % LANES
        right = pltpu.roll(from_right, turn, 1) if turn else from_right
        side = jnp.where(lane < HALO, right, jnp.where(lane >= LANES - HALO, left, 0.0))
        wide.append(jnp.concatenate([main, side], axis=1))
    eta, east, north, m, depth, stress_x, stress_y, fresh = wide
    row = iota((full, 2 * LANES), 0) + (t * tall - HALO)
    coriolis = 0.1 + 0.2 * (row.astype(F32) + 0.5) / (tall * count_t)

    def dx(a):
        return 0.5 * (pltpu.roll(a, 2 * LANES - 1, 1) - pltpu.roll(a, 1, 1))

    def dy(a):
        return 0.5 * (pltpu.roll(a, full - 1, 0) - pltpu.roll(a, 1, 0))

    for _ in range(SUBS):
        eta = m * (eta - (dx(east) + dy(north)) + fresh)
        new_east = m * (east + coriolis * north - depth * dx(eta) + stress_x)
        north = m * (north - coriolis * east - depth * dy(eta) + stress_y)
        east = new_east
    for i, a in enumerate((eta, east, north)):
        out_ref[i] = a[HALO : HALO + tall, :LANES]


def plan_messages(count_t, count_s, groups, tall):
    total = count_t * count_s
    by_distance = {}
    for o in range(NEIGHBOR_TILES):
        if o != MIDDLE:
            by_distance.setdefault(MIDDLE - o, []).append((("ret", o), groups))
    for dt in (-1, 0, 1):
        for ds in (-1, 0, 1):
            if dt or ds:
                length = tall if dt == 0 else (HALO if ds else HALO * FIELDS)
                by_distance.setdefault(dt * count_s + ds, []).append((("halo", dt, ds), length))
    messages, partial = [], []
    for distance, parts in sorted(by_distance.items()):
        if any(kind[0] == "ret" for kind, _ in parts):
            pairs = [(i, (i + distance) % total) for i in range(total)]
            messages.append((pairs, parts))
            continue
        pairs = []
        for (_, dt, ds), _ in parts:
            for t in range(count_t):
                for s in range(count_s):
                    if 0 <= t + dt < count_t and 0 <= s + ds < count_s:
                        pairs.append((t * count_s + s, (t + dt) * count_s + s + ds))
        for other in partial:
            if not {a for a, _ in pairs} & {a for a, _ in other[0]} and not (
                {b for _, b in pairs} & {b for _, b in other[0]}
            ):
                other[0].extend(pairs)
                other[1].extend(parts)
                break
        else:
            partial.append((pairs, list(parts)))
    return messages + partial


def shards(
    air_exchanges,
    air_destination,
    diagonal_group_pointer,
    interpolation_factors,
    marine_fields,
    skin_warmth_anomaly,
    gravity_bathymetry,
    marine_indicator,
):
    axes = ("tile", "sub")
    count_t, count_s = lax.axis_size("tile"), lax.axis_size("sub")
    total = count_t * count_s
    columns = air_destination.shape[1]
    blocks = columns // LANES
    groups = columns // 2 // LANES
    destination = air_destination.reshape(blocks, LANES)
    vmem = pl.BlockSpec(memory_space=pltpu.VMEM)
    params = pltpu.CompilerParams(vmem_limit_bytes=VMEM_LIMIT)
    hbm = pl.BlockSpec(memory_space=pltpu.HBM)
    pointers = diagonal_group_pointer[0, 0, 0].T
    to_stage = (
        pointers,
        interpolation_factors[0, 0, 0],
        marine_fields[0],
        skin_warmth_anomaly[0],
        gravity_bathymetry[0],
        marine_indicator[0],
    )
    results = pl.pallas_call(
        functools.partial(route_kernel, count_s, total),
        out_shape=[jax.ShapeDtypeStruct((groups * 4, LANES), BF16)] * NEIGHBOR_TILES
        + [jax.ShapeDtypeStruct(a.shape, a.dtype) for a in (destination,) + to_stage],
        in_specs=[hbm] * (2 + len(to_stage)),
        out_specs=[vmem] * (NEIGHBOR_TILES + 1 + len(to_stage)),
        scratch_shapes=[
            pltpu.VMEM((8, columns), BF16),
            pltpu.VMEM((8, columns), BF16),
            pltpu.VMEM((NEIGHBOR_TILES * (groups + 1) * 8, LANES), F32),
            pltpu.VMEM((blocks, LANES), I32),
            pltpu.VMEM((32, blocks), I32),
            pltpu.SMEM((32, blocks), I32),
            pltpu.SemaphoreType.DMA((3 + len(to_stage),)),
        ],
        compiler_params=params,
        name="route",
    )(*(pltpu.with_memory_space_constraint(a, pltpu.HBM) for a in (air_exchanges[0], destination) + to_stage))
    outbound = results[:NEIGHBOR_TILES]
    destination, rows, weights, ocean, skin, depth, mask = results[NEIGHBOR_TILES:]
    arrived = list(outbound)
    for o in range(NEIGHBOR_TILES):
        if o != MIDDLE:
            pairs = [(i, (i + o - MIDDLE) % total) for i in range(total)]
            arrived[o] = lax.ppermute(outbound[o], axes, pairs)
    prepared = pl.pallas_call(
        functools.partial(prepare_kernel, count_s, total),
        out_shape=[jax.ShapeDtypeStruct((blocks, LANES), I32)] * 2
        + [jax.ShapeDtypeStruct((2 * blocks, groups), BF16)] * NEIGHBOR_TILES,
        in_specs=[vmem],
        out_specs=[vmem] * (2 + NEIGHBOR_TILES),
        compiler_params=params,
        cost_estimate=pl.CostEstimate(flops=2 * 15 * LANES**3, bytes_accessed=2**19, transcendentals=0),
        name="prepare",
    )(destination)

    tall = skin.shape[0]
    messages = plan_messages(count_t, count_s, groups, tall)
    lengths = [sum(n for _, n in parts) for _, parts in messages]
    row_blocks = weights.shape[0]
    outs = pl.pallas_call(
        functools.partial(remap_kernel, messages),
        out_shape=[
            jax.ShapeDtypeStruct((3, tall, LANES), F32),
            jax.ShapeDtypeStruct((groups, LANES), BF16),
        ]
        + [jax.ShapeDtypeStruct((n, LANES), BF16) for n in lengths],
        in_specs=[vmem] * NEIGHBOR_TILES + [hbm] + [vmem] * 6,
        out_specs=[vmem] * (2 + len(lengths)),
        scratch_shapes=[
            pltpu.VMEM((NEIGHBOR_TILES * groups * 4 + 8, LANES), F32),
            pltpu.VMEM((row_blocks * 8, LANES), F32),
            pltpu.VMEM((2 * row_blocks, LANES), F32),
            pltpu.SMEM(pointers.shape, I32),
            pltpu.SemaphoreType.DMA,
        ],
        compiler_params=params,
        name="remap",
    )(*arrived, pltpu.with_memory_space_constraint(pointers, pltpu.HBM), rows, weights, ocean, skin, depth, mask)
    forcing, own = outs[:2]
    received = [
        lax.ppermute(message, axes, pairs) for message, (pairs, _) in zip(outs[2:], messages)
    ]
    ocean_out, warm = pl.pallas_call(
        functools.partial(finish_kernel, messages, count_t, count_s),
        out_shape=[
            jax.ShapeDtypeStruct((3, tall, LANES), F32),
            jax.ShapeDtypeStruct((blocks, LANES), F32),
        ],
        in_specs=[vmem] * (len(messages) + 3 + NEIGHBOR_TILES + 4),
        out_specs=[vmem] * 2,
        compiler_params=params,
        name="finish",
    )(*received, own, *prepared, ocean, depth, mask, forcing)
    return ocean_out[None], warm.reshape(1, columns)


def solution(mesh):
    return jax.shard_map(
        shards,
        mesh=mesh,
        in_specs=(
            P(("member", "comp"), None, ("tile", "sub")),
            P("comp", ("tile", "sub"), None),
            P("comp", "tile", "sub", None, None),
            P("comp", "tile", "sub", None, None, None, None),
            P(("member", "comp"), None, "tile", "sub"),
            P(("member", "comp"), "tile", "sub"),
            P("comp", "tile", "sub"),
            P("comp", "tile", "sub"),
        ),
        out_specs=(
            P(("member", "comp"), None, "tile", "sub"),
            P(("member", "comp"), ("tile", "sub")),
        ),
        check_vma=False,
    )
```

```python
import functools

import jax
import jax.numpy as jnp
from jax import lax
from jax.experimental import pallas as pl
from jax.experimental.pallas import tpu as pltpu
from jax.sharding import PartitionSpec as P

NEIGHBOR_TILES = 5
MIDDLE = NEIGHBOR_TILES // 2
SUBS = 8
LANES = 128
HALO = 2 * SUBS
FIELDS = 8
F32 = jnp.float32
BF16 = jnp.bfloat16
I32 = jnp.int32
SORT_UNIT = 16
VMEM_LIMIT = 48 * 1024 * 1024


def iota(shape, dim):
    return lax.broadcasted_iota(I32, shape, dim)


def dot(a, b):
    return jnp.dot(a, b, preferred_element_type=F32)


def dot_t(a, b):
    return lax.dot_general(a, b, (((1,), (1,)), ((), ())), preferred_element_type=F32)


def position():
    return lax.axis_index("tile") * lax.axis_size("sub") + lax.axis_index("sub")


def pick(values):
    usual = max(sorted(set(values)), key=values.count)
    mine = position()
    result = jnp.int32(usual)
    for device, value in enumerate(values):
        if value != usual:
            result = jnp.where(mine == device, value, result)
    return result


def ones_where(mask):
    return jnp.where(mask, 1.0, 0.0).astype(BF16)


def offsets_of(destination, total):
    shifted = destination - position() + MIDDLE
    shifted = jnp.where(shifted < 0, shifted + total, shifted)
    return jnp.where(shifted >= total, shifted - total, shifted)


def ranks(offsets):
    rows = offsets.shape[0]
    r, c = iota((LANES, LANES), 0), iota((LANES, LANES), 1)
    before = ones_where(r < c)
    every = jnp.ones((LANES, LANES), BF16)
    earlier = ones_where(iota((rows, rows), 1) < iota((rows, rows), 0))
    result = []
    for o in range(NEIGHBOR_TILES):
        mask = offsets == o
        hot = ones_where(mask)
        inside = dot(hot, before)
        count = dot(hot, every)
        base = dot(earlier, count.astype(BF16))
        result.append((mask, hot, inside, count, base))
    return result


def route_kernel(sent, total, x_hbm, dest_hbm, *rest):
    staged = len(rest) - len(sent) - 8
    sources, rest = rest[: staged // 2], rest[staged // 2 :]
    outs, dest_ref, rest = rest[: len(sent)], rest[len(sent)], rest[len(sent) + 1 :]
    targets, rest = rest[: staged // 2], rest[staged // 2 :]
    x_ref, comb, place, pos_scr, vec, scal, sem = rest
    copies = [
        pltpu.make_async_copy(a, b, sem.at[i])
        for i, (a, b) in enumerate(
            zip((dest_hbm, x_hbm) + tuple(sources), (dest_ref, x_ref) + tuple(targets))
        )
    ]
    for copy in copies:
        copy.start()
    copies[0].wait()
    blocks = dest_ref.shape[0]
    unit = SORT_UNIT
    groups = outs[0].shape[0] // 4
    stride = (groups + 1) * 8
    offsets = offsets_of(dest_ref[...], total)
    ones8 = jnp.ones((8, LANES), BF16)
    sub8 = iota((8, blocks), 0)
    earlier = ones_where(iota((blocks, blocks), 0) < iota((blocks, blocks), 1))
    before = ones_where(iota((LANES, 2 * LANES), 0) < iota((LANES, 2 * LANES), 1))
    hots = [ones_where(offsets == o) for o in range(NEIGHBOR_TILES)]
    counts = jnp.zeros((8, blocks), F32)
    start_t = jnp.zeros((8, blocks), F32)
    starts = jnp.zeros((8, blocks), F32)
    for o, hot in enumerate(hots):
        count_t = dot_t(ones8, hot)
        counts = jnp.where(sub8 == o, count_t, counts)
        starts = jnp.where(sub8 == o, start_t, starts)
        start_t = start_t + count_t
    base = dot(counts.astype(BF16), earlier).astype(I32)
    counts, starts = counts.astype(I32), starts.astype(I32)
    at = jnp.bitwise_and(base, LANES - 1)
    vec[0:8, :] = sub8 * stride + lax.shift_right_logical(base, 7) * 8
    vec[8:16, :] = jnp.bitwise_and(at - starts, LANES - 1)
    vec[16:24, :] = at
    vec[24:32, :] = at + counts - LANES
    copy = pltpu.make_async_copy(vec, scal, sem.at[len(copies)])
    copy.start()
    start = jnp.zeros((blocks, LANES), F32)
    pos = jnp.zeros((blocks, LANES), F32)
    for o, hot in enumerate(hots):
        inside = dot(hot, before)
        pos = jnp.where(offsets == o, start + inside[:, :LANES], pos)
        start = start + inside[:, LANES:]
    pos_scr[...] = pos.astype(I32)
    f, g = iota((8, 8), 1), jnp.bitwise_and(iota((8, 8), 0), 3)
    plus = ((g == 0) & (f == 0)) | ((g == 1) & (f == 1)) | ((g == 2) & (f == 3)) | ((g == 3) & (f >= 6))
    minus = ((g == 2) & (f == 2)) | ((g == 3) & ((f == 4) | (f == 5)))
    combine = (jnp.where(plus, 1.0, 0.0) - jnp.where(minus, 1.0, 0.0)).astype(BF16)
    copies[1].wait()
    comb[...] = dot(combine, x_ref[...]).astype(BF16)

    lines = iota((LANES, LANES), 0)

    def sort_blocks(i):
        result = []
        for u in range(0, unit, 2):
            b = i * unit + u
            columns = comb[:, pl.ds(pl.multiple_of(b * LANES, 2 * LANES), 2 * LANES)].astype(F32)
            columns = jnp.concatenate([columns[:, :LANES], columns[:, LANES:]], axis=0).astype(BF16)
            hot = [ones_where(pos_scr[pl.ds(b + v, 1), :] == lines) for v in range(2)]
            both = dot_t(columns, jnp.concatenate(hot, axis=0))
            result += [both[:8, :LANES], both[8:, LANES:]]
        return result

    lane = iota((8, LANES), 1)

    def place_blocks(i, values, current):
        current = list(current)
        for u in range(unit):
            b = i * unit + u
            for o in range(NEIGHBOR_TILES):
                turned = pltpu.roll(values[u], scal[8 + o, b], 1)
                merged = jnp.where(lane < scal[16 + o, b], current[o], turned)
                place[pl.ds(pl.multiple_of(scal[o, b], 8), 8), :] = merged
                current[o] = jnp.where(lane < scal[24 + o, b], turned, merged)
        return current

    def step(i, carry):
        values = sort_blocks(i + 1)
        return tuple(place_blocks(i, carry[NEIGHBOR_TILES:], carry[:NEIGHBOR_TILES])) + tuple(values)

    steps = blocks // unit
    current = [jnp.zeros((8, LANES), F32) for _ in range(NEIGHBOR_TILES)]
    values = sort_blocks(0)
    copy.wait()
    carry = lax.fori_loop(0, steps - 1, step, tuple(current) + tuple(values))
    current = place_blocks(steps - 1, carry[NEIGHBOR_TILES:], carry[:NEIGHBOR_TILES])
    pair_lane = jnp.where(iota((8, LANES), 0) < 4, lane, lane + LANES)
    upper = iota((groups // 2, 8, LANES), 1) < 4
    slot = iota((groups // 2, 8, LANES), 0) * (2 * LANES) + pair_lane[None]
    last = blocks - 1

    def length(o):
        return (scal[o, last] - o * stride) * (LANES // 8) + scal[24 + o, last] + LANES

    for o in range(NEIGHBOR_TILES):
        full = lax.shift_right_logical(length(o), 7) * 8 + o * stride
        place[pl.ds(pl.multiple_of(full, 8), 8), :] = current[o]
    for offset, out in zip(sent, outs):
        o = pick(offset)
        tiles = place[pl.ds(pl.multiple_of(o * stride, 8), groups * 8), :]
        tiles = tiles.reshape(groups // 2, 2, 8, LANES)
        both = jnp.where(upper, tiles[:, 0], tiles[:, 1])
        both = jnp.where(slot < length(o), both, 0.0)
        out[...] = both.reshape(groups * 4, LANES).astype(BF16)
    for copy in copies[2:]:
        copy.wait()


def prepare_kernel(total, dest_ref, row_ref, blocks_ref, index_ref, code_ref, *hot_refs):
    blocks = dest_ref.shape[0]
    groups = hot_refs[0].shape[1]
    offsets = offsets_of(dest_ref[...], total)
    index = jnp.zeros((blocks, LANES), I32)
    code = jnp.zeros((blocks, LANES), I32)
    group_id = iota((blocks, groups), 1)
    for o, (mask, hot, inside, count, base) in enumerate(ranks(offsets)):
        base = base.astype(I32)
        rank = base + inside.astype(I32)
        first = lax.shift_right_logical(base, 7)
        index = jnp.where(mask, jnp.bitwise_and(rank, LANES - 1), index)
        code = jnp.where(mask, 2 * o + lax.shift_right_logical(rank, 7) - first, code)
        hot_refs[o][0:blocks, :] = ones_where(group_id == first[:, :groups])
        hot_refs[o][blocks:, :] = ones_where(group_id == first[:, :groups] + 1)
    index_ref[...] = index
    code_ref[...] = code
    row = jnp.concatenate([row_ref[0:1, :], row_ref[1:2, :]], axis=1)
    blocks_ref[...] = ones_where(iota(blocks_ref.shape, 0) == row)


def packed_columns(fields, low):
    lane = iota(fields[0].shape, 1)
    packed = fields[0] if low else pltpu.roll(fields[0], HALO, 1)
    for i in range(1, FIELDS):
        turn = (i * HALO + (0 if low else HALO)) % LANES
        packed = jnp.where(
            lane >= i * HALO, pltpu.roll(fields[i], turn, 1) if turn else fields[i], packed
        )
    return packed


def remap_kernel(came, returns, edges, *rest):
    arrived, rest = rest[: len(came)], rest[len(came) :]
    ptr_hbm, hot_ref, w_ref, ocean_ref, skin_ref, depth_ref, mask_ref = rest[:7]
    forcing_ref, own_ref = rest[7:9]
    message_refs = rest[9 : 9 + len(returns)]
    slots, mapped, shares, homebound, bank, ptr_ref, sem = rest[9 + len(returns) :]
    pointers = pltpu.make_async_copy(ptr_hbm, ptr_ref, sem)
    pointers.start()
    per_step = 8
    size = arrived[0].shape[0]
    for offset, block in zip(came, arrived):
        o = pick(offset)
        slots[pl.ds(pl.multiple_of(o * size, size), size), :] = block[...].astype(F32)
    slots[NEIGHBOR_TILES * size :, :] = jnp.zeros((8, LANES), F32)
    pointers.wait()
    sub = iota((per_step, LANES), 0)

    def forward(step):
        for j in range(per_step):
            k = step * per_step + j
            both = [slots[pl.ds(ptr_ref[w, k] * 4, 8), :] for w in range(2)]
            both = jnp.concatenate(both, axis=0).astype(BF16)
            product = dot_t(both, w_ref[k].reshape(2 * LANES, LANES))
            mapped[pl.ds(k * 8, 8), :] = product[:8, :LANES] + product[8:, LANES:]

    def middle(step):
        rows = pl.ds(step * per_step, per_step)
        u, v, p, h = (mapped[pl.ds(step * per_step * 8 + i, per_step, stride=8), :] for i in range(4))
        speed = jnp.sqrt(u * u + v * v + 1.0)
        forcing_ref[0, rows, :] = 0.2 * speed * u
        forcing_ref[1, rows, :] = 0.2 * speed * v
        forcing_ref[2, rows, :] = 0.5 * p
        return (skin_ref[rows, :] + 0.25 * mask_ref[rows, :].astype(F32) * h).astype(BF16).astype(F32)

    def back(step, sst):
        left = []
        for j in range(per_step):
            only = jnp.where(sub == j, sst, 0.0)
            zero = jnp.zeros_like(only)
            left.append(jnp.concatenate([only, zero], axis=0).astype(BF16))
            left.append(jnp.concatenate([zero, only], axis=0).astype(BF16))
        left = jnp.concatenate(left, axis=1)
        right = w_ref[pl.ds(step * per_step, per_step)].reshape(per_step * 2 * LANES, LANES)
        total = dot(left, right)
        for w in range(2):
            rows = slice((w * steps + step) * per_step, (w * steps + step + 1) * per_step)
            shares[rows, :] = total[w * per_step : (w + 1) * per_step]

    steps = w_ref.shape[0] // per_step
    for i in range(steps):
        forward(i)
    for i in range(steps):
        back(i, middle(i))

    every = shares[...]
    high = every.astype(BF16)
    low = (every - high.astype(F32)).astype(BF16)
    split = jnp.concatenate([high, low], axis=1)
    groups = own_ref.shape[0]
    value = dot(hot_ref[...], split)
    returned = (value[:, :LANES] + value[:, LANES:]).astype(BF16)
    homebound[...] = returned
    own_ref[...] = returned[MIDDLE * groups : (MIDDLE + 1) * groups]
    fields = [ocean_ref[0], ocean_ref[1], ocean_ref[2], mask_ref[...].astype(F32), depth_ref[...]]
    fields += [forcing_ref[0], forcing_ref[1], forcing_ref[2]]
    tall = fields[0].shape[0]
    rows = HALO * FIELDS
    bank[0:rows, :] = jnp.concatenate([x[tall - HALO :] for x in fields], axis=0).astype(BF16)
    bank[rows : 2 * rows, :] = jnp.concatenate([x[:HALO] for x in fields], axis=0).astype(BF16)
    bank[2 * rows : 2 * rows + tall, :] = packed_columns(fields, False).astype(BF16)
    bank[2 * rows + tall : 2 * rows + 2 * tall, :] = packed_columns(fields, True).astype(BF16)
    bank[2 * rows + 2 * tall :, :] = jnp.zeros((rows, LANES), BF16)
    for offset, edge, out in zip(returns, edges, message_refs):
        first = pl.multiple_of(pick(offset) * groups, 16)
        out[0:groups, :] = homebound[pl.ds(first, groups), :]
        first = pl.multiple_of(pick(edge), 16)
        out[groups:, :] = bank[pl.ds(first, rows), :]


def finish_kernel(sources, halos, count_t, count_s, messages, *rest):
    message_refs, rest = rest[:messages], rest[messages:]
    own_ref, index_ref, code_ref = rest[:3]
    hot_refs, rest = rest[3 : 3 + NEIGHBOR_TILES], rest[3 + NEIGHBOR_TILES :]
    ocean_ref, depth_ref, mask_ref, forcing_ref, out_ref, warm_ref, inbox = rest
    t, s = lax.axis_index("tile"), lax.axis_index("sub")
    size = message_refs[0].shape[0]
    groups = own_ref.shape[0]
    for i, ref in enumerate(message_refs):
        inbox[i * size : (i + 1) * size, :] = ref[...]
    blocks = index_ref.shape[0]
    index = index_ref[...]
    code = code_ref[...]
    warm = jnp.zeros((blocks, LANES), F32)
    for o in range(NEIGHBOR_TILES):
        if o == MIDDLE:
            value = own_ref[...]
        else:
            value = inbox[pl.ds(pl.multiple_of(pick(sources[o]) * size, 16), groups), :]
        lines = dot(hot_refs[o][...], value)
        for half in range(2):
            picked = jnp.take_along_axis(lines[half * blocks : (half + 1) * blocks], index, axis=1)
            warm = jnp.where(code == 2 * o + half, picked, warm)
    warm_ref[...] = warm

    tall = depth_ref.shape[0]
    full = tall + 2 * HALO

    def halo(dt, ds):
        ok = jnp.bool_(True)
        if dt == 1:
            ok &= t > 0
        if dt == -1:
            ok &= t < count_t - 1
        if ds == 1:
            ok &= s > 0
        if ds == -1:
            ok &= s < count_s - 1
        rows = tall if dt == 0 else (HALO if ds else HALO * FIELDS)
        first = pl.multiple_of(pick(halos[dt, ds]) * size + groups, 16)
        value = inbox[pl.ds(first, rows), :].astype(F32)
        return jnp.where(ok, value, 0.0)

    from_left = jnp.concatenate([halo(1, 1), halo(0, 1), halo(-1, 1)], axis=0)
    from_right = jnp.concatenate([halo(1, -1), halo(0, -1), halo(-1, -1)], axis=0)
    above, below = halo(1, 0), halo(-1, 0)
    lane = iota((full, LANES), 1)
    inner = [ocean_ref[0], ocean_ref[1], ocean_ref[2], mask_ref[...].astype(F32), depth_ref[...]]
    inner += [forcing_ref[0], forcing_ref[1], forcing_ref[2]]
    wide = []
    for i in range(FIELDS):
        rows = slice(i * HALO, (i + 1) * HALO)
        main = jnp.concatenate([above[rows], inner[i], below[rows]], axis=0)
        turn = (LANES - HALO - i * HALO) % LANES
        left = pltpu.roll(from_left, turn, 1) if turn else from_left
        turn = (LANES - i * HALO) % LANES
        right = pltpu.roll(from_right, turn, 1) if turn else from_right
        side = jnp.where(lane < HALO, right, jnp.where(lane >= LANES - HALO, left, 0.0))
        wide.append(jnp.concatenate([main, side], axis=1))
    eta, east, north, m, depth, stress_x, stress_y, fresh = wide
    row = iota((full, 2 * LANES), 0) + (t * tall - HALO)
    coriolis = 0.1 + 0.2 * (row.astype(F32) + 0.5) / (tall * count_t)

    def dx(a):
        return 0.5 * (pltpu.roll(a, 2 * LANES - 1, 1) - pltpu.roll(a, 1, 1))

    def dy(a):
        return 0.5 * (pltpu.roll(a, full - 1, 0) - pltpu.roll(a, 1, 0))

    for _ in range(SUBS):
        eta = m * (eta - (dx(east) + dy(north)) + fresh)
        new_east = m * (east + coriolis * north - depth * dx(eta) + stress_x)
        north = m * (north - coriolis * east - depth * dy(eta) + stress_y)
        east = new_east
    for i, a in enumerate((eta, east, north)):
        out_ref[i] = a[HALO : HALO + tall, :LANES]


SCHEDULES = {
    (4, 2): (
        [
            [1, 3, 4, 2, 6, 7, 0, 5],
            [7, 2, 1, 5, 3, 6, 4, 0],
            [6, 7, 0, 4, 2, 3, 5, 1],
            [2, 0, 3, 1, 5, 4, 7, 6],
        ],
        [
            [3, 7, 1, 4, 2, 6, 0, 5],
            [7, 2, 4, 5, 6, 3, -1, 0],
            [6, 3, 5, 0, 7, 2, 4, 1],
            [2, -1, 0, 1, 3, 7, 5, 4],
            [1, 0, 3, 2, 5, 4, 7, 6],
        ],
    ),
}


def schedule(count_t, count_s):
    total = count_t * count_s
    if (count_t, count_s) in SCHEDULES:
        return SCHEDULES[count_t, count_s]
    rings = [
        [(i + distance) % total for i in range(total)]
        for distance in range(-MIDDLE, MIDDLE + 1)
        if distance
    ]
    others = []
    for dt in (-1, 1):
        for ds in (-1, 0, 1):
            if MIDDLE < abs(dt * count_s + ds):
                targets = [-1] * total
                for device in range(total):
                    t, s = device // count_s + dt, device % count_s + ds
                    if 0 <= t < count_t and 0 <= s < count_s:
                        targets[device] = t * count_s + s
                others.append(targets)
    return rings, rings + others


def plan(count_t, count_s, groups, tall):
    total = count_t * count_s
    outward, homeward = schedule(count_t, count_s)

    def offset(a, b):
        o = (b - a + MIDDLE) % total
        return o if o < NEIGHBOR_TILES else -1

    def step(a, b):
        dt, ds = b // count_s - a // count_s, b % count_s - a % count_s
        return (dt, ds) if abs(dt) <= 1 and abs(ds) <= 1 else None

    def senders(targets):
        return [targets.index(d) if d in targets else -1 for d in range(total)]

    rows = HALO * FIELDS
    start = {(1, 0): 0, (-1, 0): rows}
    for ds, first in ((1, 2 * rows), (-1, 2 * rows + tall)):
        start[0, ds] = start[-1, ds] = first
        start[1, ds] = first + tall - HALO
    result = {"outward": outward, "homeward": homeward}
    result["sent"] = [[offset(a, b) for a, b in enumerate(p)] for p in outward]
    result["sent"].insert(0, [MIDDLE] * total)
    result["came"] = [[offset(a, b) for b, a in enumerate(senders(p))] for p in outward]
    result["came"].insert(0, [MIDDLE] * total)
    result["returns"] = [
        [max(offset(b, a), 0) if b >= 0 else 0 for a, b in enumerate(p)] for p in homeward
    ]
    result["edges"] = [
        [start[step(a, b)] if b >= 0 and step(a, b) else 0 for a, b in enumerate(p)] for p in homeward
    ]
    sources = [[0] * total for _ in range(NEIGHBOR_TILES)]
    halos = {(dt, ds): [0] * total for dt in (-1, 0, 1) for ds in (-1, 0, 1)}
    for i, p in enumerate(homeward):
        for a, b in enumerate(p):
            if b >= 0:
                if offset(b, a) >= 0:
                    sources[offset(b, a)][b] = i
                if step(a, b):
                    halos[step(a, b)][b] = i
    result["sources"], result["halos"] = sources, halos
    return result


def shards(
    air_exchanges,
    air_destination,
    diagonal_group_pointer,
    interpolation_factors,
    marine_fields,
    skin_warmth_anomaly,
    gravity_bathymetry,
    marine_indicator,
):
    axes = ("tile", "sub")
    count_t, count_s = lax.axis_size("tile"), lax.axis_size("sub")
    total = count_t * count_s
    columns = air_destination.shape[1]
    blocks = columns // LANES
    groups = columns // 2 // LANES
    destination = air_destination.reshape(blocks, LANES)
    vmem = pl.BlockSpec(memory_space=pltpu.VMEM)
    params = pltpu.CompilerParams(vmem_limit_bytes=VMEM_LIMIT)
    hbm = pl.BlockSpec(memory_space=pltpu.HBM)
    pointers = diagonal_group_pointer[0, 0, 0].T
    to_stage = (
        pointers,
        interpolation_factors[0, 0, 0],
        marine_fields[0],
        skin_warmth_anomaly[0],
        gravity_bathymetry[0],
        marine_indicator[0],
    )
    tall = skin_warmth_anomaly.shape[1]
    moves = plan(count_t, count_s, groups, tall)
    sends = len(moves["sent"])
    results = pl.pallas_call(
        functools.partial(route_kernel, moves["sent"], total),
        out_shape=[jax.ShapeDtypeStruct((groups * 4, LANES), BF16)] * sends
        + [jax.ShapeDtypeStruct(a.shape, a.dtype) for a in (destination,) + to_stage],
        in_specs=[hbm] * (2 + len(to_stage)),
        out_specs=[vmem] * (sends + 1 + len(to_stage)),
        scratch_shapes=[
            pltpu.VMEM((8, columns), BF16),
            pltpu.VMEM((8, columns), BF16),
            pltpu.VMEM((NEIGHBOR_TILES * (groups + 1) * 8, LANES), F32),
            pltpu.VMEM((blocks, LANES), I32),
            pltpu.VMEM((32, blocks), I32),
            pltpu.SMEM((32, blocks), I32),
            pltpu.SemaphoreType.DMA((3 + len(to_stage),)),
        ],
        compiler_params=params,
        name="route",
    )(*(pltpu.with_memory_space_constraint(a, pltpu.HBM) for a in (air_exchanges[0], destination) + to_stage))
    destination, rows, weights, ocean, skin, depth, mask = results[sends:]

    def send(array, targets):
        return lax.ppermute(array, axes, [(a, b) for a, b in enumerate(targets) if b >= 0])

    arrived = [results[0]] + [send(a, p) for a, p in zip(results[1:], moves["outward"])]
    prepared = pl.pallas_call(
        functools.partial(prepare_kernel, total),
        out_shape=[jax.ShapeDtypeStruct((NEIGHBOR_TILES * groups, LANES), BF16)]
        + [jax.ShapeDtypeStruct((blocks, LANES), I32)] * 2
        + [jax.ShapeDtypeStruct((2 * blocks, groups), BF16)] * NEIGHBOR_TILES,
        in_specs=[vmem] * 2,
        out_specs=[vmem] * (3 + NEIGHBOR_TILES),
        compiler_params=params,
        cost_estimate=pl.CostEstimate(flops=2 * 15 * LANES**3, bytes_accessed=2**19, transcendentals=0),
        name="prepare",
    )(destination, rows)
    returns = len(moves["returns"])
    message = (groups + HALO * FIELDS, LANES)
    row_blocks = weights.shape[0]
    outs = pl.pallas_call(
        functools.partial(remap_kernel, moves["came"], moves["returns"], moves["edges"]),
        out_shape=[
            jax.ShapeDtypeStruct((3, tall, LANES), F32),
            jax.ShapeDtypeStruct((groups, LANES), BF16),
        ]
        + [jax.ShapeDtypeStruct(message, BF16)] * returns,
        in_specs=[vmem] * sends + [hbm] + [vmem] * 6,
        out_specs=[vmem] * (2 + returns),
        scratch_shapes=[
            pltpu.VMEM((NEIGHBOR_TILES * groups * 4 + 8, LANES), F32),
            pltpu.VMEM((row_blocks * 8, LANES), F32),
            pltpu.VMEM((2 * row_blocks, LANES), F32),
            pltpu.VMEM((NEIGHBOR_TILES * groups, LANES), BF16),
            pltpu.VMEM((3 * HALO * FIELDS + 2 * tall, LANES), BF16),
            pltpu.SMEM(pointers.shape, I32),
            pltpu.SemaphoreType.DMA,
        ],
        compiler_params=params,
        name="remap",
    )(*arrived, pltpu.with_memory_space_constraint(pointers, pltpu.HBM), prepared[0], weights, ocean, skin, depth, mask)
    forcing, own = outs[:2]
    received = [send(a, p) for a, p in zip(outs[2:], moves["homeward"])]
    ocean_out, warm = pl.pallas_call(
        functools.partial(
            finish_kernel, moves["sources"], moves["halos"], count_t, count_s, returns
        ),
        out_shape=[
            jax.ShapeDtypeStruct((3, tall, LANES), F32),
            jax.ShapeDtypeStruct((blocks, LANES), F32),
        ],
        in_specs=[vmem] * (returns + 3 + NEIGHBOR_TILES + 4),
        out_specs=[vmem] * 2,
        scratch_shapes=[pltpu.VMEM((returns * message[0], LANES), BF16)],
        compiler_params=params,
        name="finish",
    )(*received, own, *prepared[1:], ocean, depth, mask, forcing)
    return ocean_out[None], warm.reshape(1, columns)


def solution(mesh):
    return jax.shard_map(
        shards,
        mesh=mesh,
        in_specs=(
            P(("member", "comp"), None, ("tile", "sub")),
            P("comp", ("tile", "sub"), None),
            P("comp", "tile", "sub", None, None),
            P("comp", "tile", "sub", None, None, None, None),
            P(("member", "comp"), None, "tile", "sub"),
            P(("member", "comp"), "tile", "sub"),
            P("comp", "tile", "sub"),
            P("comp", "tile", "sub"),
        ),
        out_specs=(
            P(("member", "comp"), None, "tile", "sub"),
            P(("member", "comp"), ("tile", "sub")),
        ),
        check_vma=False,
    )
```

```python
import functools

import jax
import jax.numpy as jnp
from jax import lax
from jax.experimental import pallas as pl
from jax.experimental.pallas import tpu as pltpu
from jax.sharding import PartitionSpec as P

NEIGHBOR_TILES = 5
MIDDLE = NEIGHBOR_TILES // 2
SUBS = 8
LANES = 128
HALO = 2 * SUBS
FIELDS = 8
F32 = jnp.float32
BF16 = jnp.bfloat16
I32 = jnp.int32
SORT_UNIT = 16
VMEM_LIMIT = 48 * 1024 * 1024


def iota(shape, dim):
    return lax.broadcasted_iota(I32, shape, dim)


def dot(a, b):
    return jnp.dot(a, b, preferred_element_type=F32)


def dot_t(a, b):
    return lax.dot_general(a, b, (((1,), (1,)), ((), ())), preferred_element_type=F32)


def position():
    return lax.axis_index("tile") * lax.axis_size("sub") + lax.axis_index("sub")


def pick(values):
    usual = max(sorted(set(values)), key=values.count)
    mine = position()
    result = jnp.int32(usual)
    for device, value in enumerate(values):
        if value != usual:
            result = jnp.where(mine == device, value, result)
    return result


def ones_where(mask):
    return jnp.where(mask, 1.0, 0.0).astype(BF16)


def offsets_of(destination, total):
    shifted = destination - position() + MIDDLE
    shifted = jnp.where(shifted < 0, shifted + total, shifted)
    return jnp.where(shifted >= total, shifted - total, shifted)


def ranks(offsets):
    rows = offsets.shape[0]
    r, c = iota((LANES, LANES), 0), iota((LANES, LANES), 1)
    before = ones_where(r < c)
    every = jnp.ones((LANES, LANES), BF16)
    earlier = ones_where(iota((rows, rows), 1) < iota((rows, rows), 0))
    result = []
    for o in range(NEIGHBOR_TILES):
        mask = offsets == o
        hot = ones_where(mask)
        inside = dot(hot, before)
        count = dot(hot, every)
        base = dot(earlier, count.astype(BF16))
        result.append((mask, hot, inside, count, base))
    return result


def route_kernel(sent, total, x_hbm, dest_hbm, *rest):
    staged = len(rest) - len(sent) - 8
    sources, rest = rest[: staged // 2], rest[staged // 2 :]
    outs, dest_ref, rest = rest[: len(sent)], rest[len(sent)], rest[len(sent) + 1 :]
    targets, rest = rest[: staged // 2], rest[staged // 2 :]
    x_ref, comb, place, pos_scr, vec, scal, sem = rest
    copies = [
        pltpu.make_async_copy(a, b, sem.at[i])
        for i, (a, b) in enumerate(
            zip((dest_hbm, x_hbm) + tuple(sources), (dest_ref, x_ref) + tuple(targets))
        )
    ]
    for copy in copies:
        copy.start()
    copies[0].wait()
    blocks = dest_ref.shape[0]
    unit = SORT_UNIT
    groups = outs[0].shape[0] // 4
    stride = (groups + 1) * 8
    offsets = offsets_of(dest_ref[...], total)
    ones8 = jnp.ones((8, LANES), BF16)
    sub8 = iota((8, blocks), 0)
    earlier = ones_where(iota((blocks, blocks), 0) < iota((blocks, blocks), 1))
    before = ones_where(iota((LANES, 2 * LANES), 0) < iota((LANES, 2 * LANES), 1))
    hots = [ones_where(offsets == o) for o in range(NEIGHBOR_TILES)]
    counts = jnp.zeros((8, blocks), F32)
    start_t = jnp.zeros((8, blocks), F32)
    starts = jnp.zeros((8, blocks), F32)
    for o, hot in enumerate(hots):
        count_t = dot_t(ones8, hot)
        counts = jnp.where(sub8 == o, count_t, counts)
        starts = jnp.where(sub8 == o, start_t, starts)
        start_t = start_t + count_t
    base = dot(counts.astype(BF16), earlier).astype(I32)
    counts, starts = counts.astype(I32), starts.astype(I32)
    at = jnp.bitwise_and(base, LANES - 1)
    vec[0:8, :] = sub8 * stride + lax.shift_right_logical(base, 7) * 8
    vec[8:16, :] = jnp.bitwise_and(at - starts, LANES - 1)
    vec[16:24, :] = at
    vec[24:32, :] = at + counts - LANES
    copy = pltpu.make_async_copy(vec, scal, sem.at[len(copies)])
    copy.start()
    start = jnp.zeros((blocks, LANES), F32)
    pos = jnp.zeros((blocks, LANES), F32)
    for o, hot in enumerate(hots):
        inside = dot(hot, before)
        pos = jnp.where(offsets == o, start + inside[:, :LANES], pos)
        start = start + inside[:, LANES:]
    pos_scr[...] = pos.astype(I32)
    f, g = iota((8, 8), 1), jnp.bitwise_and(iota((8, 8), 0), 3)
    plus = ((g == 0) & (f == 0)) | ((g == 1) & (f == 1)) | ((g == 2) & (f == 3)) | ((g == 3) & (f >= 6))
    minus = ((g == 2) & (f == 2)) | ((g == 3) & ((f == 4) | (f == 5)))
    combine = (jnp.where(plus, 1.0, 0.0) - jnp.where(minus, 1.0, 0.0)).astype(BF16)
    copies[1].wait()
    comb[...] = dot(combine, x_ref[...]).astype(BF16)

    lines = iota((LANES, LANES), 0)

    def sort_blocks(i):
        result = []
        for u in range(0, unit, 2):
            b = i * unit + u
            columns = comb[:, pl.ds(pl.multiple_of(b * LANES, 2 * LANES), 2 * LANES)].astype(F32)
            columns = jnp.concatenate([columns[:, :LANES], columns[:, LANES:]], axis=0).astype(BF16)
            hot = [ones_where(pos_scr[pl.ds(b + v, 1), :] == lines) for v in range(2)]
            both = dot_t(columns, jnp.concatenate(hot, axis=0))
            result += [both[:8, :LANES], both[8:, LANES:]]
        return result

    lane = iota((8, LANES), 1)

    def place_blocks(i, values, current):
        current = list(current)
        for u in range(unit):
            b = i * unit + u
            for o in range(NEIGHBOR_TILES):
                turned = pltpu.roll(values[u], scal[8 + o, b], 1)
                merged = jnp.where(lane < scal[16 + o, b], current[o], turned)
                place[pl.ds(pl.multiple_of(scal[o, b], 8), 8), :] = merged
                current[o] = jnp.where(lane < scal[24 + o, b], turned, merged)
        return current

    def step(i, carry):
        values = sort_blocks(i + 1)
        return tuple(place_blocks(i, carry[NEIGHBOR_TILES:], carry[:NEIGHBOR_TILES])) + tuple(values)

    steps = blocks // unit
    current = [jnp.zeros((8, LANES), F32) for _ in range(NEIGHBOR_TILES)]
    values = sort_blocks(0)
    copy.wait()
    carry = lax.fori_loop(0, steps - 1, step, tuple(current) + tuple(values))
    current = place_blocks(steps - 1, carry[NEIGHBOR_TILES:], carry[:NEIGHBOR_TILES])
    pair_lane = jnp.where(iota((8, LANES), 0) < 4, lane, lane + LANES)
    upper = iota((groups // 2, 8, LANES), 1) < 4
    slot = iota((groups // 2, 8, LANES), 0) * (2 * LANES) + pair_lane[None]
    last = blocks - 1

    def length(o):
        return (scal[o, last] - o * stride) * (LANES // 8) + scal[24 + o, last] + LANES

    for o in range(NEIGHBOR_TILES):
        full = lax.shift_right_logical(length(o), 7) * 8 + o * stride
        place[pl.ds(pl.multiple_of(full, 8), 8), :] = current[o]
    for offset, out in zip(sent, outs):
        o = pick(offset)
        tiles = place[pl.ds(pl.multiple_of(o * stride, 8), groups * 8), :]
        tiles = tiles.reshape(groups // 2, 2, 8, LANES)
        both = jnp.where(upper, tiles[:, 0], tiles[:, 1])
        both = jnp.where(slot < length(o), both, 0.0)
        out[...] = both.reshape(groups * 4, LANES).astype(BF16)
    for copy in copies[2:]:
        copy.wait()


def prepare_kernel(total, dest_ref, row_ref, blocks_ref, index_ref, code_ref, *hot_refs):
    blocks = dest_ref.shape[0]
    groups = hot_refs[0].shape[1]
    offsets = offsets_of(dest_ref[...], total)
    index = jnp.zeros((blocks, LANES), I32)
    code = jnp.zeros((blocks, LANES), I32)
    group_id = iota((blocks, groups), 1)
    for o, (mask, hot, inside, count, base) in enumerate(ranks(offsets)):
        base = base.astype(I32)
        rank = base + inside.astype(I32)
        first = lax.shift_right_logical(base, 7)
        index = jnp.where(mask, jnp.bitwise_and(rank, LANES - 1), index)
        code = jnp.where(mask, 2 * o + lax.shift_right_logical(rank, 7) - first, code)
        hot_refs[o][0:blocks, :] = ones_where(group_id == first[:, :groups])
        hot_refs[o][blocks:, :] = ones_where(group_id == first[:, :groups] + 1)
    index_ref[...] = index
    code_ref[...] = code
    row = jnp.concatenate([row_ref[0:1, :], row_ref[1:2, :]], axis=1)
    blocks_ref[...] = ones_where(iota(blocks_ref.shape, 0) == row)


def packed_columns(fields, low):
    lane = iota(fields[0].shape, 1)
    packed = fields[0] if low else pltpu.roll(fields[0], HALO, 1)
    for i in range(1, FIELDS):
        turn = (i * HALO + (0 if low else HALO)) % LANES
        packed = jnp.where(
            lane >= i * HALO, pltpu.roll(fields[i], turn, 1) if turn else fields[i], packed
        )
    return packed


def remap_kernel(came, returns, edges, *rest):
    arrived, rest = rest[: len(came)], rest[len(came) :]
    ptr_hbm, hot_ref, w_ref, ocean_ref, skin_ref, depth_ref, mask_ref = rest[:7]
    forcing_ref, own_ref = rest[7:9]
    message_refs = rest[9 : 9 + len(returns)]
    slots, mapped, shares, homebound, bank, ptr_ref, sem = rest[9 + len(returns) :]
    pointers = pltpu.make_async_copy(ptr_hbm, ptr_ref, sem)
    pointers.start()
    per_step = 8
    size = arrived[0].shape[0]
    for offset, block in zip(came, arrived):
        o = pick(offset)
        slots[pl.ds(pl.multiple_of(o * size, size), size), :] = block[...].astype(F32)
    slots[NEIGHBOR_TILES * size :, :] = jnp.zeros((8, LANES), F32)
    pointers.wait()
    sub = iota((per_step, LANES), 0)

    def forward(step):
        for j in range(per_step):
            k = step * per_step + j
            both = [slots[pl.ds(ptr_ref[w, k] * 4, 8), :] for w in range(2)]
            both = jnp.concatenate(both, axis=0).astype(BF16)
            product = dot_t(both, w_ref[k].reshape(2 * LANES, LANES))
            mapped[pl.ds(k * 8, 8), :] = product[:8, :LANES] + product[8:, LANES:]

    def middle(step):
        rows = pl.ds(step * per_step, per_step)
        u, v, p, h = (mapped[pl.ds(step * per_step * 8 + i, per_step, stride=8), :] for i in range(4))
        speed = jnp.sqrt(u * u + v * v + 1.0)
        forcing_ref[0, rows, :] = 0.2 * speed * u
        forcing_ref[1, rows, :] = 0.2 * speed * v
        forcing_ref[2, rows, :] = 0.5 * p
        return (skin_ref[rows, :] + 0.25 * mask_ref[rows, :].astype(F32) * h).astype(BF16).astype(F32)

    def back(step, sst):
        left = []
        for j in range(per_step):
            only = jnp.where(sub == j, sst, 0.0)
            zero = jnp.zeros_like(only)
            left.append(jnp.concatenate([only, zero], axis=0).astype(BF16))
            left.append(jnp.concatenate([zero, only], axis=0).astype(BF16))
        left = jnp.concatenate(left, axis=1)
        right = w_ref[pl.ds(step * per_step, per_step)].reshape(per_step * 2 * LANES, LANES)
        total = dot(left, right)
        for w in range(2):
            rows = slice((w * steps + step) * per_step, (w * steps + step + 1) * per_step)
            shares[rows, :] = total[w * per_step : (w + 1) * per_step]

    steps = w_ref.shape[0] // per_step
    for i in range(steps):
        forward(i)
    for i in range(steps):
        back(i, middle(i))

    every = shares[...]
    high = every.astype(BF16)
    low = (every - high.astype(F32)).astype(BF16)
    split = jnp.concatenate([high, low], axis=1)
    groups = own_ref.shape[0]
    value = dot(hot_ref[...], split)
    returned = (value[:, :LANES] + value[:, LANES:]).astype(BF16)
    homebound[...] = returned
    own_ref[...] = returned[MIDDLE * groups : (MIDDLE + 1) * groups]
    fields = [ocean_ref[0], ocean_ref[1], ocean_ref[2], mask_ref[...].astype(F32), depth_ref[...]]
    fields += [forcing_ref[0], forcing_ref[1], forcing_ref[2]]
    tall = fields[0].shape[0]
    rows = HALO * FIELDS
    bank[0:rows, :] = jnp.concatenate([x[tall - HALO :] for x in fields], axis=0).astype(BF16)
    bank[rows : 2 * rows, :] = jnp.concatenate([x[:HALO] for x in fields], axis=0).astype(BF16)
    bank[2 * rows : 2 * rows + tall, :] = packed_columns(fields, False).astype(BF16)
    bank[2 * rows + tall : 2 * rows + 2 * tall, :] = packed_columns(fields, True).astype(BF16)
    bank[2 * rows + 2 * tall :, :] = jnp.zeros((rows, LANES), BF16)
    for offset, edge, out in zip(returns, edges, message_refs):
        first = pl.multiple_of(pick(offset) * groups, 16)
        out[0:groups, :] = homebound[pl.ds(first, groups), :]
        first = pl.multiple_of(pick(edge), 16)
        out[groups:, :] = bank[pl.ds(first, rows), :]


def finish_kernel(sources, halos, count_t, count_s, messages, *rest):
    message_refs, rest = rest[:messages], rest[messages:]
    own_ref, index_ref, code_ref = rest[:3]
    hot_refs, rest = rest[3 : 3 + NEIGHBOR_TILES], rest[3 + NEIGHBOR_TILES :]
    ocean_ref, depth_ref, mask_ref, forcing_ref, out_ref, warm_ref, inbox = rest
    t, s = lax.axis_index("tile"), lax.axis_index("sub")
    size = message_refs[0].shape[0]
    groups = own_ref.shape[0]
    for i, ref in enumerate(message_refs):
        inbox[i * size : (i + 1) * size, :] = ref[...]
    blocks = index_ref.shape[0]
    index = index_ref[...]
    code = code_ref[...]
    warm = jnp.zeros((blocks, LANES), F32)
    for o in range(NEIGHBOR_TILES):
        if o == MIDDLE:
            value = own_ref[...]
        else:
            value = inbox[pl.ds(pl.multiple_of(pick(sources[o]) * size, 16), groups), :]
        lines = dot(hot_refs[o][...], value)
        for half in range(2):
            picked = jnp.take_along_axis(lines[half * blocks : (half + 1) * blocks], index, axis=1)
            warm = jnp.where(code == 2 * o + half, picked, warm)
    warm_ref[...] = warm

    tall = depth_ref.shape[0]
    full = tall + 2 * HALO

    def halo(dt, ds):
        ok = jnp.bool_(True)
        if dt == 1:
            ok &= t > 0
        if dt == -1:
            ok &= t < count_t - 1
        if ds == 1:
            ok &= s > 0
        if ds == -1:
            ok &= s < count_s - 1
        rows = tall if dt == 0 else (HALO if ds else HALO * FIELDS)
        first = pl.multiple_of(pick(halos[dt, ds]) * size + groups, 16)
        value = inbox[pl.ds(first, rows), :].astype(F32)
        return jnp.where(ok, value, 0.0)

    from_left = jnp.concatenate([halo(1, 1), halo(0, 1), halo(-1, 1)], axis=0)
    from_right = jnp.concatenate([halo(1, -1), halo(0, -1), halo(-1, -1)], axis=0)
    above, below = halo(1, 0), halo(-1, 0)
    lane = iota((full, LANES), 1)
    inner = [ocean_ref[0], ocean_ref[1], ocean_ref[2], mask_ref[...].astype(F32), depth_ref[...]]
    inner += [forcing_ref[0], forcing_ref[1], forcing_ref[2]]
    wide = []
    for i in range(FIELDS):
        rows = slice(i * HALO, (i + 1) * HALO)
        main = jnp.concatenate([above[rows], inner[i], below[rows]], axis=0)
        turn = (LANES - HALO - i * HALO) % LANES
        left = pltpu.roll(from_left, turn, 1) if turn else from_left
        turn = (LANES - i * HALO) % LANES
        right = pltpu.roll(from_right, turn, 1) if turn else from_right
        side = jnp.where(lane < HALO, right, jnp.where(lane >= LANES - HALO, left, 0.0))
        wide.append(jnp.concatenate([main, side], axis=1))
    eta, east, north, m, depth, stress_x, stress_y, fresh = wide
    row = iota((full, 2 * LANES), 0) + (t * tall - HALO)
    coriolis = 0.1 + 0.2 * (row.astype(F32) + 0.5) / (tall * count_t)

    def dx(a):
        return 0.5 * (pltpu.roll(a, 2 * LANES - 1, 1) - pltpu.roll(a, 1, 1))

    def dy(a):
        return 0.5 * (pltpu.roll(a, full - 1, 0) - pltpu.roll(a, 1, 0))

    for _ in range(SUBS):
        eta = m * (eta - (dx(east) + dy(north)) + fresh)
        new_east = m * (east + coriolis * north - depth * dx(eta) + stress_x)
        north = m * (north - coriolis * east - depth * dy(eta) + stress_y)
        east = new_east
    for i, a in enumerate((eta, east, north)):
        out_ref[i] = a[HALO : HALO + tall, :LANES]


SCHEDULES = {
    (4, 2): (
        [
            [1, 3, 4, 2, 6, 7, 0, 5],
            [7, 2, 1, 5, 3, 6, 4, 0],
            [6, 7, 0, 4, 2, 3, 5, 1],
            [2, 0, 3, 1, 5, 4, 7, 6],
        ],
        [
            [3, 6, 5, 0, 7, 2, 1, 4],
            [2, 3, 1, 4, 6, 7, 0, 5],
            [7, 2, 4, 1, 3, 6, 5, 0],
            [6, 7, 0, 5, 2, 3, 4, 1],
            [1, 0, 3, 2, 5, 4, 7, 6],
        ],
    ),
}


def schedule(count_t, count_s):
    total = count_t * count_s
    if (count_t, count_s) in SCHEDULES:
        return SCHEDULES[count_t, count_s]
    rings = [
        [(i + distance) % total for i in range(total)]
        for distance in range(-MIDDLE, MIDDLE + 1)
        if distance
    ]
    others = []
    for dt in (-1, 1):
        for ds in (-1, 0, 1):
            if MIDDLE < abs(dt * count_s + ds):
                targets = [-1] * total
                for device in range(total):
                    t, s = device // count_s + dt, device % count_s + ds
                    if 0 <= t < count_t and 0 <= s < count_s:
                        targets[device] = t * count_s + s
                others.append(targets)
    return rings, rings + others


def plan(count_t, count_s, groups, tall):
    total = count_t * count_s
    outward, homeward = schedule(count_t, count_s)

    def offset(a, b):
        o = (b - a + MIDDLE) % total
        return o if o < NEIGHBOR_TILES else -1

    def step(a, b):
        dt, ds = b // count_s - a // count_s, b % count_s - a % count_s
        return (dt, ds) if abs(dt) <= 1 and abs(ds) <= 1 else None

    def senders(targets):
        return [targets.index(d) if d in targets else -1 for d in range(total)]

    rows = HALO * FIELDS
    start = {(1, 0): 0, (-1, 0): rows}
    for ds, first in ((1, 2 * rows), (-1, 2 * rows + tall)):
        start[0, ds] = start[-1, ds] = first
        start[1, ds] = first + tall - HALO
    result = {"outward": outward, "homeward": homeward}
    result["sent"] = [[offset(a, b) for a, b in enumerate(p)] for p in outward]
    result["sent"].insert(0, [MIDDLE] * total)
    result["came"] = [[offset(a, b) for b, a in enumerate(senders(p))] for p in outward]
    result["came"].insert(0, [MIDDLE] * total)
    result["returns"] = [
        [max(offset(b, a), 0) if b >= 0 else 0 for a, b in enumerate(p)] for p in homeward
    ]
    result["edges"] = [
        [start[step(a, b)] if b >= 0 and step(a, b) else 0 for a, b in enumerate(p)] for p in homeward
    ]
    sources = [[0] * total for _ in range(NEIGHBOR_TILES)]
    halos = {(dt, ds): [0] * total for dt in (-1, 0, 1) for ds in (-1, 0, 1)}
    for i, p in enumerate(homeward):
        for a, b in enumerate(p):
            if b >= 0:
                if offset(b, a) >= 0:
                    sources[offset(b, a)][b] = i
                if step(a, b):
                    halos[step(a, b)][b] = i
    result["sources"], result["halos"] = sources, halos
    return result


def shards(
    air_exchanges,
    air_destination,
    diagonal_group_pointer,
    interpolation_factors,
    marine_fields,
    skin_warmth_anomaly,
    gravity_bathymetry,
    marine_indicator,
):
    axes = ("tile", "sub")
    count_t, count_s = lax.axis_size("tile"), lax.axis_size("sub")
    total = count_t * count_s
    columns = air_destination.shape[1]
    blocks = columns // LANES
    groups = columns // 2 // LANES
    destination = air_destination.reshape(blocks, LANES)
    vmem = pl.BlockSpec(memory_space=pltpu.VMEM)
    params = pltpu.CompilerParams(vmem_limit_bytes=VMEM_LIMIT)
    hbm = pl.BlockSpec(memory_space=pltpu.HBM)
    pointers = diagonal_group_pointer[0, 0, 0].T
    to_stage = (
        pointers,
        interpolation_factors[0, 0, 0],
        marine_fields[0],
        skin_warmth_anomaly[0],
        gravity_bathymetry[0],
        marine_indicator[0],
    )
    tall = skin_warmth_anomaly.shape[1]
    moves = plan(count_t, count_s, groups, tall)
    sends = len(moves["sent"])
    results = pl.pallas_call(
        functools.partial(route_kernel, moves["sent"], total),
        out_shape=[jax.ShapeDtypeStruct((groups * 4, LANES), BF16)] * sends
        + [jax.ShapeDtypeStruct(a.shape, a.dtype) for a in (destination,) + to_stage],
        in_specs=[hbm] * (2 + len(to_stage)),
        out_specs=[vmem] * (sends + 1 + len(to_stage)),
        scratch_shapes=[
            pltpu.VMEM((8, columns), BF16),
            pltpu.VMEM((8, columns), BF16),
            pltpu.VMEM((NEIGHBOR_TILES * (groups + 1) * 8, LANES), F32),
            pltpu.VMEM((blocks, LANES), I32),
            pltpu.VMEM((32, blocks), I32),
            pltpu.SMEM((32, blocks), I32),
            pltpu.SemaphoreType.DMA((3 + len(to_stage),)),
        ],
        compiler_params=params,
        name="route",
    )(*(pltpu.with_memory_space_constraint(a, pltpu.HBM) for a in (air_exchanges[0], destination) + to_stage))
    destination, rows, weights, ocean, skin, depth, mask = results[sends:]

    def send(array, targets):
        return lax.ppermute(array, axes, [(a, b) for a, b in enumerate(targets) if b >= 0])

    arrived = [results[0]] + [send(a, p) for a, p in zip(results[1:], moves["outward"])]
    prepared = pl.pallas_call(
        functools.partial(prepare_kernel, total),
        out_shape=[jax.ShapeDtypeStruct((NEIGHBOR_TILES * groups, LANES), BF16)]
        + [jax.ShapeDtypeStruct((blocks, LANES), I32)] * 2
        + [jax.ShapeDtypeStruct((2 * blocks, groups), BF16)] * NEIGHBOR_TILES,
        in_specs=[vmem] * 2,
        out_specs=[vmem] * (3 + NEIGHBOR_TILES),
        compiler_params=params,
        cost_estimate=pl.CostEstimate(flops=2 * 15 * LANES**3, bytes_accessed=2**19, transcendentals=0),
        name="prepare",
    )(destination, rows)
    returns = len(moves["returns"])
    message = (groups + HALO * FIELDS, LANES)
    row_blocks = weights.shape[0]
    outs = pl.pallas_call(
        functools.partial(remap_kernel, moves["came"], moves["returns"], moves["edges"]),
        out_shape=[
            jax.ShapeDtypeStruct((3, tall, LANES), F32),
            jax.ShapeDtypeStruct((groups, LANES), BF16),
        ]
        + [jax.ShapeDtypeStruct(message, BF16)] * returns,
        in_specs=[vmem] * sends + [hbm] + [vmem] * 6,
        out_specs=[vmem] * (2 + returns),
        scratch_shapes=[
            pltpu.VMEM((NEIGHBOR_TILES * groups * 4 + 8, LANES), F32),
            pltpu.VMEM((row_blocks * 8, LANES), F32),
            pltpu.VMEM((2 * row_blocks, LANES), F32),
            pltpu.VMEM((NEIGHBOR_TILES * groups, LANES), BF16),
            pltpu.VMEM((3 * HALO * FIELDS + 2 * tall, LANES), BF16),
            pltpu.SMEM(pointers.shape, I32),
            pltpu.SemaphoreType.DMA,
        ],
        compiler_params=params,
        name="remap",
    )(*arrived, pltpu.with_memory_space_constraint(pointers, pltpu.HBM), prepared[0], weights, ocean, skin, depth, mask)
    forcing, own = outs[:2]
    received = [send(a, p) for a, p in zip(outs[2:], moves["homeward"])]
    ocean_out, warm = pl.pallas_call(
        functools.partial(
            finish_kernel, moves["sources"], moves["halos"], count_t, count_s, returns
        ),
        out_shape=[
            jax.ShapeDtypeStruct((3, tall, LANES), F32),
            jax.ShapeDtypeStruct((blocks, LANES), F32),
        ],
        in_specs=[vmem] * (returns + 3 + NEIGHBOR_TILES + 4),
        out_specs=[vmem] * 2,
        scratch_shapes=[pltpu.VMEM((returns * message[0], LANES), BF16)],
        compiler_params=params,
        name="finish",
    )(*received, own, *prepared[1:], ocean, depth, mask, forcing)
    return ocean_out[None], warm.reshape(1, columns)


def solution(mesh):
    return jax.shard_map(
        shards,
        mesh=mesh,
        in_specs=(
            P(("member", "comp"), None, ("tile", "sub")),
            P("comp", ("tile", "sub"), None),
            P("comp", "tile", "sub", None, None),
            P("comp", "tile", "sub", None, None, None, None),
            P(("member", "comp"), None, "tile", "sub"),
            P(("member", "comp"), "tile", "sub"),
            P("comp", "tile", "sub"),
            P("comp", "tile", "sub"),
        ),
        out_specs=(
            P(("member", "comp"), None, "tile", "sub"),
            P(("member", "comp"), ("tile", "sub")),
        ),
        check_vma=False,
    )
```

```python
import functools

import jax
import jax.numpy as jnp
from jax import lax
from jax.experimental import pallas as pl
from jax.experimental.pallas import tpu as pltpu
from jax.sharding import PartitionSpec as P

NEIGHBOR_TILES = 5
MIDDLE = NEIGHBOR_TILES // 2
SUBS = 8
LANES = 128
HALO = 2 * SUBS
FIELDS = 8
F32 = jnp.float32
BF16 = jnp.bfloat16
I32 = jnp.int32
SORT_UNIT = 16
VMEM_LIMIT = 48 * 1024 * 1024


def iota(shape, dim):
    return lax.broadcasted_iota(I32, shape, dim)


def dot(a, b):
    return jnp.dot(a, b, preferred_element_type=F32)


def dot_t(a, b):
    return lax.dot_general(a, b, (((1,), (1,)), ((), ())), preferred_element_type=F32)


def position():
    return lax.axis_index("tile") * lax.axis_size("sub") + lax.axis_index("sub")


def pick(values):
    usual = max(sorted(set(values)), key=values.count)
    mine = position()
    result = jnp.int32(usual)
    for device, value in enumerate(values):
        if value != usual:
            result = jnp.where(mine == device, value, result)
    return result


def ones_where(mask):
    return jnp.where(mask, 1.0, 0.0).astype(BF16)


def offsets_of(destination, total):
    shifted = destination - position() + MIDDLE
    shifted = jnp.where(shifted < 0, shifted + total, shifted)
    return jnp.where(shifted >= total, shifted - total, shifted)


def ranks(offsets):
    rows = offsets.shape[0]
    r, c = iota((LANES, LANES), 0), iota((LANES, LANES), 1)
    before = ones_where(r < c)
    every = jnp.ones((LANES, LANES), BF16)
    earlier = ones_where(iota((rows, rows), 1) < iota((rows, rows), 0))
    result = []
    for o in range(NEIGHBOR_TILES):
        mask = offsets == o
        hot = ones_where(mask)
        inside = dot(hot, before)
        count = dot(hot, every)
        base = dot(earlier, count.astype(BF16))
        result.append((mask, hot, inside, count, base))
    return result


def route_kernel(sent, total, x_hbm, dest_hbm, *rest):
    staged = len(rest) - len(sent) - 8
    sources, rest = rest[: staged // 2], rest[staged // 2 :]
    outs, dest_ref, rest = rest[: len(sent)], rest[len(sent)], rest[len(sent) + 1 :]
    targets, rest = rest[: staged // 2], rest[staged // 2 :]
    x_ref, comb, place, pos_scr, vec, scal, sem = rest
    copies = [
        pltpu.make_async_copy(a, b, sem.at[i])
        for i, (a, b) in enumerate(
            zip((dest_hbm, x_hbm) + tuple(sources), (dest_ref, x_ref) + tuple(targets))
        )
    ]
    for copy in copies:
        copy.start()
    copies[0].wait()
    blocks = dest_ref.shape[0]
    unit = SORT_UNIT
    groups = outs[0].shape[0] // 4
    stride = (groups + 1) * 8
    offsets = offsets_of(dest_ref[...], total)
    ones8 = jnp.ones((8, LANES), BF16)
    sub8 = iota((8, blocks), 0)
    earlier = ones_where(iota((blocks, blocks), 0) < iota((blocks, blocks), 1))
    before = ones_where(iota((LANES, 2 * LANES), 0) < iota((LANES, 2 * LANES), 1))
    hots = [ones_where(offsets == o) for o in range(NEIGHBOR_TILES)]
    counts = jnp.zeros((8, blocks), F32)
    start_t = jnp.zeros((8, blocks), F32)
    starts = jnp.zeros((8, blocks), F32)
    for o, hot in enumerate(hots):
        count_t = dot_t(ones8, hot)
        counts = jnp.where(sub8 == o, count_t, counts)
        starts = jnp.where(sub8 == o, start_t, starts)
        start_t = start_t + count_t
    base = dot(counts.astype(BF16), earlier).astype(I32)
    counts, starts = counts.astype(I32), starts.astype(I32)
    at = jnp.bitwise_and(base, LANES - 1)
    vec[0:8, :] = sub8 * stride + lax.shift_right_logical(base, 7) * 8
    vec[8:16, :] = jnp.bitwise_and(at - starts, LANES - 1)
    vec[16:24, :] = at
    vec[24:32, :] = at + counts - LANES
    copy = pltpu.make_async_copy(vec, scal, sem.at[len(copies)])
    copy.start()
    start = jnp.zeros((blocks, LANES), F32)
    pos = jnp.zeros((blocks, LANES), F32)
    for o, hot in enumerate(hots):
        inside = dot(hot, before)
        pos = jnp.where(offsets == o, start + inside[:, :LANES], pos)
        start = start + inside[:, LANES:]
    pos_scr[...] = pos.astype(I32)
    f, g = iota((8, 8), 1), jnp.bitwise_and(iota((8, 8), 0), 3)
    plus = ((g == 0) & (f == 0)) | ((g == 1) & (f == 1)) | ((g == 2) & (f == 3)) | ((g == 3) & (f >= 6))
    minus = ((g == 2) & (f == 2)) | ((g == 3) & ((f == 4) | (f == 5)))
    combine = (jnp.where(plus, 1.0, 0.0) - jnp.where(minus, 1.0, 0.0)).astype(BF16)
    copies[1].wait()
    comb[...] = dot(combine, x_ref[...]).astype(BF16)

    lines = iota((LANES, LANES), 0)

    def sort_blocks(i):
        result = []
        for u in range(0, unit, 2):
            b = i * unit + u
            columns = comb[:, pl.ds(pl.multiple_of(b * LANES, 2 * LANES), 2 * LANES)].astype(F32)
            columns = jnp.concatenate([columns[:, :LANES], columns[:, LANES:]], axis=0).astype(BF16)
            hot = [ones_where(pos_scr[pl.ds(b + v, 1), :] == lines) for v in range(2)]
            both = dot_t(columns, jnp.concatenate(hot, axis=0))
            result += [both[:8, :LANES], both[8:, LANES:]]
        return result

    lane = iota((8, LANES), 1)

    def place_blocks(i, values, current):
        current = list(current)
        for u in range(unit):
            b = i * unit + u
            for o in range(NEIGHBOR_TILES):
                turned = pltpu.roll(values[u], scal[8 + o, b], 1)
                merged = jnp.where(lane < scal[16 + o, b], current[o], turned)
                place[pl.ds(pl.multiple_of(scal[o, b], 8), 8), :] = merged
                current[o] = jnp.where(lane < scal[24 + o, b], turned, merged)
        return current

    def step(i, carry):
        values = sort_blocks(i + 1)
        return tuple(place_blocks(i, carry[NEIGHBOR_TILES:], carry[:NEIGHBOR_TILES])) + tuple(values)

    steps = blocks // unit
    current = [jnp.zeros((8, LANES), F32) for _ in range(NEIGHBOR_TILES)]
    values = sort_blocks(0)
    copy.wait()
    carry = lax.fori_loop(0, steps - 1, step, tuple(current) + tuple(values))
    current = place_blocks(steps - 1, carry[NEIGHBOR_TILES:], carry[:NEIGHBOR_TILES])
    pair_lane = jnp.where(iota((8, LANES), 0) < 4, lane, lane + LANES)
    upper = iota((groups // 2, 8, LANES), 1) < 4
    slot = iota((groups // 2, 8, LANES), 0) * (2 * LANES) + pair_lane[None]
    last = blocks - 1

    def length(o):
        return (scal[o, last] - o * stride) * (LANES // 8) + scal[24 + o, last] + LANES

    for o in range(NEIGHBOR_TILES):
        full = lax.shift_right_logical(length(o), 7) * 8 + o * stride
        place[pl.ds(pl.multiple_of(full, 8), 8), :] = current[o]
    for offset, out in zip(sent, outs):
        o = pick(offset)
        tiles = place[pl.ds(pl.multiple_of(o * stride, 8), groups * 8), :]
        tiles = tiles.reshape(groups // 2, 2, 8, LANES)
        both = jnp.where(upper, tiles[:, 0], tiles[:, 1])
        both = jnp.where(slot < length(o), both, 0.0)
        out[...] = both.reshape(groups * 4, LANES).astype(BF16)
    for copy in copies[2:]:
        copy.wait()


def prepare_kernel(total, dest_ref, row_ref, blocks_ref, index_ref, code_ref, *hot_refs):
    blocks = dest_ref.shape[0]
    groups = hot_refs[0].shape[1]
    offsets = offsets_of(dest_ref[...], total)
    index = jnp.zeros((blocks, LANES), I32)
    code = jnp.zeros((blocks, LANES), I32)
    group_id = iota((blocks, groups), 1)
    lane = iota((blocks, LANES), 1)
    for o, (mask, hot, inside, count, base) in enumerate(ranks(offsets)):
        base = base.astype(I32)
        rank = base + inside.astype(I32)
        first = lax.shift_right_logical(base, 7)
        index = jnp.where(mask, jnp.bitwise_and(rank, LANES - 1), index)
        code = jnp.where(mask, code + o, code)
        code = jnp.where(lane >= jnp.bitwise_and(base, LANES - 1), code + (8 << o), code)
        hot_refs[o][0:blocks, :] = ones_where(group_id == first[:, :groups])
        hot_refs[o][blocks:, :] = ones_where(group_id == first[:, :groups] + 1)
    index_ref[...] = index
    code_ref[...] = code
    row = jnp.concatenate([row_ref[0:1, :], row_ref[1:2, :]], axis=1)
    blocks_ref[...] = ones_where(iota(blocks_ref.shape, 0) == row)


def packed_columns(fields, low):
    lane = iota(fields[0].shape, 1)
    packed = fields[0] if low else pltpu.roll(fields[0], HALO, 1)
    for i in range(1, FIELDS):
        turn = (i * HALO + (0 if low else HALO)) % LANES
        packed = jnp.where(
            lane >= i * HALO, pltpu.roll(fields[i], turn, 1) if turn else fields[i], packed
        )
    return packed


def remap_kernel(came, returns, edges, *rest):
    arrived, rest = rest[: len(came)], rest[len(came) :]
    ptr_hbm, hot_ref, w_ref, ocean_ref, skin_ref, depth_ref, mask_ref = rest[:7]
    forcing_ref, own_ref = rest[7:9]
    message_refs = rest[9 : 9 + len(returns)]
    slots, mapped, shares, homebound, bank, ptr_ref, sem = rest[9 + len(returns) :]
    pointers = pltpu.make_async_copy(ptr_hbm, ptr_ref, sem)
    pointers.start()
    per_step = 8
    size = arrived[0].shape[0]
    for offset, block in zip(came, arrived):
        o = pick(offset)
        slots[pl.ds(pl.multiple_of(o * size, size), size), :] = block[...].astype(F32)
    slots[NEIGHBOR_TILES * size :, :] = jnp.zeros((8, LANES), F32)
    pointers.wait()
    sub = iota((per_step, LANES), 0)

    def forward(step):
        for j in range(per_step):
            k = step * per_step + j
            both = [slots[pl.ds(ptr_ref[w, k] * 4, 8), :] for w in range(2)]
            both = jnp.concatenate(both, axis=0).astype(BF16)
            product = dot_t(both, w_ref[k].reshape(2 * LANES, LANES))
            mapped[pl.ds(k * 8, 8), :] = product[:8, :LANES] + product[8:, LANES:]

    def middle(step):
        rows = pl.ds(step * per_step, per_step)
        u, v, p, h = (mapped[pl.ds(step * per_step * 8 + i, per_step, stride=8), :] for i in range(4))
        speed = jnp.sqrt(u * u + v * v + 1.0)
        forcing_ref[0, rows, :] = 0.2 * speed * u
        forcing_ref[1, rows, :] = 0.2 * speed * v
        forcing_ref[2, rows, :] = 0.5 * p
        return (skin_ref[rows, :] + 0.25 * mask_ref[rows, :].astype(F32) * h).astype(BF16).astype(F32)

    def back(step, sst):
        left = []
        for j in range(per_step):
            only = jnp.where(sub == j, sst, 0.0)
            zero = jnp.zeros_like(only)
            left.append(jnp.concatenate([only, zero], axis=0).astype(BF16))
            left.append(jnp.concatenate([zero, only], axis=0).astype(BF16))
        left = jnp.concatenate(left, axis=1)
        right = w_ref[pl.ds(step * per_step, per_step)].reshape(per_step * 2 * LANES, LANES)
        total = dot(left, right)
        for w in range(2):
            rows = slice((w * steps + step) * per_step, (w * steps + step + 1) * per_step)
            shares[rows, :] = total[w * per_step : (w + 1) * per_step]

    steps = w_ref.shape[0] // per_step
    for i in range(steps):
        forward(i)
    for i in range(steps):
        back(i, middle(i))

    every = shares[...]
    high = every.astype(BF16)
    low = (every - high.astype(F32)).astype(BF16)
    split = jnp.concatenate([high, low], axis=1)
    groups = own_ref.shape[0]
    value = dot(hot_ref[...], split)
    returned = (value[:, :LANES] + value[:, LANES:]).astype(BF16)
    homebound[...] = returned
    own_ref[...] = returned[MIDDLE * groups : (MIDDLE + 1) * groups]
    fields = [ocean_ref[0], ocean_ref[1], ocean_ref[2], mask_ref[...].astype(F32), depth_ref[...]]
    fields += [forcing_ref[0], forcing_ref[1], forcing_ref[2]]
    tall = fields[0].shape[0]
    rows = HALO * FIELDS
    bank[0:rows, :] = jnp.concatenate([x[tall - HALO :] for x in fields], axis=0).astype(BF16)
    bank[rows : 2 * rows, :] = jnp.concatenate([x[:HALO] for x in fields], axis=0).astype(BF16)
    bank[2 * rows : 2 * rows + tall, :] = packed_columns(fields, False).astype(BF16)
    bank[2 * rows + tall : 2 * rows + 2 * tall, :] = packed_columns(fields, True).astype(BF16)
    bank[2 * rows + 2 * tall :, :] = jnp.zeros((rows, LANES), BF16)
    for offset, edge, out in zip(returns, edges, message_refs):
        first = pl.multiple_of(pick(offset) * groups, 16)
        out[0:groups, :] = homebound[pl.ds(first, groups), :]
        first = pl.multiple_of(pick(edge), 16)
        out[groups:, :] = bank[pl.ds(first, rows), :]


def finish_kernel(sources, halos, count_t, count_s, messages, *rest):
    message_refs, rest = rest[:messages], rest[messages:]
    own_ref, index_ref, code_ref = rest[:3]
    hot_refs, rest = rest[3 : 3 + NEIGHBOR_TILES], rest[3 + NEIGHBOR_TILES :]
    ocean_ref, depth_ref, mask_ref, forcing_ref, out_ref, warm_ref, inbox, shifted = rest
    t, s = lax.axis_index("tile"), lax.axis_index("sub")
    size = message_refs[0].shape[0]
    groups = own_ref.shape[0]
    for i, ref in enumerate(message_refs):
        inbox[i * size : (i + 1) * size, :] = ref[...]
    blocks = index_ref.shape[0]
    index = index_ref[...]
    code = code_ref[...]
    warm = jnp.zeros((blocks, LANES), F32)
    for o in range(NEIGHBOR_TILES):
        if o == MIDDLE:
            value = own_ref[...]
        else:
            value = inbox[pl.ds(pl.multiple_of(pick(sources[o]) * size, 16), groups), :]
        lines = dot(hot_refs[o][...], value)
        upper = jnp.bitwise_and(code, 8 << o) != 0
        lines = jnp.where(upper, lines[:blocks], lines[blocks:])
        picked = jnp.take_along_axis(lines, index, axis=1)
        warm = jnp.where(jnp.bitwise_and(code, 7) == o, picked, warm)
    warm_ref[...] = warm

    tall = depth_ref.shape[0]
    full = tall + 2 * HALO

    def halo(dt, ds):
        ok = jnp.bool_(True)
        if dt == 1:
            ok &= t > 0
        if dt == -1:
            ok &= t < count_t - 1
        if ds == 1:
            ok &= s > 0
        if ds == -1:
            ok &= s < count_s - 1
        rows = tall if dt == 0 else (HALO if ds else HALO * FIELDS)
        first = pl.multiple_of(pick(halos[dt, ds]) * size + groups, 16)
        value = inbox[pl.ds(first, rows), :].astype(F32)
        return jnp.where(ok, value, 0.0)

    from_left = jnp.concatenate([halo(1, 1), halo(0, 1), halo(-1, 1)], axis=0)
    from_right = jnp.concatenate([halo(1, -1), halo(0, -1), halo(-1, -1)], axis=0)
    above, below = halo(1, 0), halo(-1, 0)
    lane = iota((full, LANES), 1)
    inner = [ocean_ref[0], ocean_ref[1], ocean_ref[2], mask_ref[...].astype(F32), depth_ref[...]]
    inner += [forcing_ref[0], forcing_ref[1], forcing_ref[2]]
    wide = []
    for i in range(FIELDS):
        rows = slice(i * HALO, (i + 1) * HALO)
        main = jnp.concatenate([above[rows], inner[i], below[rows]], axis=0)
        turn = (LANES - HALO - i * HALO) % LANES
        left = pltpu.roll(from_left, turn, 1) if turn else from_left
        turn = (LANES - i * HALO) % LANES
        right = pltpu.roll(from_right, turn, 1) if turn else from_right
        side = jnp.where(lane < HALO, right, jnp.where(lane >= LANES - HALO, left, 0.0))
        wide.append([main, side])
    eta, east, north, m, depth, stress_x, stress_y, fresh = wide
    row = iota((full, LANES), 0) + (t * tall - HALO)
    coriolis = 0.1 + 0.2 * (row.astype(F32) + 0.5) / (tall * count_t)

    both = range(2)
    half_m = [0.5 * m[i] for i in both]
    half_d = [half_m[i] * depth[i] for i in both]
    turning = [m[i] * coriolis for i in both]
    fresh = [m[i] * fresh[i] for i in both]
    stress_x = [m[i] * stress_x[i] for i in both]
    stress_y = [m[i] * stress_y[i] for i in both]
    shifted[:, 0:8, :] = jnp.zeros((4, 8, LANES), F32)
    shifted[:, 8 + full :, :] = jnp.zeros((4, 8, LANES), F32)

    def across(a):
        ahead = [pltpu.roll(a[i], LANES - 1, 1) for i in both]
        behind = [pltpu.roll(a[i], 1, 1) for i in both]
        columns = lane[: a[0].shape[0]]
        return [
            jnp.where(columns == LANES - 1, ahead[1 - i], ahead[i])
            - jnp.where(columns == 0, behind[1 - i], behind[i])
            for i in both
        ]

    def along(a, first, rows, place):
        result = []
        for i in both:
            shifted[place + i, 8 + first : 8 + first + a[i].shape[0], :] = a[i]
            result.append(
                shifted[place + i, 9 + rows.start : 9 + rows.stop, :]
                - shifted[place + i, 7 + rows.start : 7 + rows.stop, :]
            )
        return result

    first, last = 0, full
    out_east, out_north = across(east), along(north, 0, slice(0, full), 0)
    eta, east, north = ([m[i] * a[i] for i in both] for a in (eta, east, north))
    for step in range(1, SUBS + 1):
        if step > 1:
            out_east, out_north = across(east), along(north, first, slice(first, last), 0)
        eta = [eta[i] + fresh[i] - half_m[i] * (out_east[i] + out_north[i]) for i in both]
        below_first = 2 * step // 8 * 8
        slope_y = along(eta, first, slice(below_first, full - below_first), 2)
        if below_first > first:
            cut = slice(below_first - first, full - below_first - first)
            eta, east, north, turning, stress_x, stress_y, half_d, fresh, half_m = (
                [x[cut] for x in a]
                for a in (eta, east, north, turning, stress_x, stress_y, half_d, fresh, half_m)
            )
            first, last = below_first, full - below_first
        slope_x = across(eta)
        new_east = [
            east[i] + turning[i] * north[i] + stress_x[i] - half_d[i] * slope_x[i] for i in both
        ]
        north = [
            north[i] - turning[i] * east[i] + stress_y[i] - half_d[i] * slope_y[i] for i in both
        ]
        east = new_east
    for i, a in enumerate((eta, east, north)):
        out_ref[i] = a[0][HALO - first : HALO - first + tall]


SCHEDULES = {
    (4, 2): (
        [
            [1, 3, 4, 2, 6, 7, 0, 5],
            [7, 2, 1, 5, 3, 6, 4, 0],
            [6, 7, 0, 4, 2, 3, 5, 1],
            [2, 0, 3, 1, 5, 4, 7, 6],
        ],
        [
            [3, 6, 5, 0, 7, 2, 1, 4],
            [2, 3, 1, 4, 6, 7, 0, 5],
            [7, 2, 4, 1, 3, 6, 5, 0],
            [6, 7, 0, 5, 2, 3, 4, 1],
            [1, 0, 3, 2, 5, 4, 7, 6],
        ],
    ),
}


def schedule(count_t, count_s):
    total = count_t * count_s
    if (count_t, count_s) in SCHEDULES:
        return SCHEDULES[count_t, count_s]
    rings = [
        [(i + distance) % total for i in range(total)]
        for distance in range(-MIDDLE, MIDDLE + 1)
        if distance
    ]
    others = []
    for dt in (-1, 1):
        for ds in (-1, 0, 1):
            if MIDDLE < abs(dt * count_s + ds):
                targets = [-1] * total
                for device in range(total):
                    t, s = device // count_s + dt, device % count_s + ds
                    if 0 <= t < count_t and 0 <= s < count_s:
                        targets[device] = t * count_s + s
                others.append(targets)
    return rings, rings + others


def plan(count_t, count_s, groups, tall):
    total = count_t * count_s
    outward, homeward = schedule(count_t, count_s)

    def offset(a, b):
        o = (b - a + MIDDLE) % total
        return o if o < NEIGHBOR_TILES else -1

    def step(a, b):
        dt, ds = b // count_s - a // count_s, b % count_s - a % count_s
        return (dt, ds) if abs(dt) <= 1 and abs(ds) <= 1 else None

    def senders(targets):
        return [targets.index(d) if d in targets else -1 for d in range(total)]

    rows = HALO * FIELDS
    start = {(1, 0): 0, (-1, 0): rows}
    for ds, first in ((1, 2 * rows), (-1, 2 * rows + tall)):
        start[0, ds] = start[-1, ds] = first
        start[1, ds] = first + tall - HALO
    result = {"outward": outward, "homeward": homeward}
    result["sent"] = [[offset(a, b) for a, b in enumerate(p)] for p in outward]
    result["sent"].insert(0, [MIDDLE] * total)
    result["came"] = [[offset(a, b) for b, a in enumerate(senders(p))] for p in outward]
    result["came"].insert(0, [MIDDLE] * total)
    result["returns"] = [
        [max(offset(b, a), 0) if b >= 0 else 0 for a, b in enumerate(p)] for p in homeward
    ]
    result["edges"] = [
        [start[step(a, b)] if b >= 0 and step(a, b) else 0 for a, b in enumerate(p)] for p in homeward
    ]
    sources = [[0] * total for _ in range(NEIGHBOR_TILES)]
    halos = {(dt, ds): [0] * total for dt in (-1, 0, 1) for ds in (-1, 0, 1)}
    for i, p in enumerate(homeward):
        for a, b in enumerate(p):
            if b >= 0:
                if offset(b, a) >= 0:
                    sources[offset(b, a)][b] = i
                if step(a, b):
                    halos[step(a, b)][b] = i
    result["sources"], result["halos"] = sources, halos
    return result


def shards(
    air_exchanges,
    air_destination,
    diagonal_group_pointer,
    interpolation_factors,
    marine_fields,
    skin_warmth_anomaly,
    gravity_bathymetry,
    marine_indicator,
):
    axes = ("tile", "sub")
    count_t, count_s = lax.axis_size("tile"), lax.axis_size("sub")
    total = count_t * count_s
    columns = air_destination.shape[1]
    blocks = columns // LANES
    groups = columns // 2 // LANES
    destination = air_destination.reshape(blocks, LANES)
    vmem = pl.BlockSpec(memory_space=pltpu.VMEM)
    params = pltpu.CompilerParams(vmem_limit_bytes=VMEM_LIMIT)
    hbm = pl.BlockSpec(memory_space=pltpu.HBM)
    pointers = diagonal_group_pointer[0, 0, 0].T
    to_stage = (
        pointers,
        interpolation_factors[0, 0, 0],
        marine_fields[0],
        skin_warmth_anomaly[0],
        gravity_bathymetry[0],
        marine_indicator[0],
    )
    tall = skin_warmth_anomaly.shape[1]
    moves = plan(count_t, count_s, groups, tall)
    sends = len(moves["sent"])
    results = pl.pallas_call(
        functools.partial(route_kernel, moves["sent"], total),
        out_shape=[jax.ShapeDtypeStruct((groups * 4, LANES), BF16)] * sends
        + [jax.ShapeDtypeStruct(a.shape, a.dtype) for a in (destination,) + to_stage],
        in_specs=[hbm] * (2 + len(to_stage)),
        out_specs=[vmem] * (sends + 1 + len(to_stage)),
        scratch_shapes=[
            pltpu.VMEM((8, columns), BF16),
            pltpu.VMEM((8, columns), BF16),
            pltpu.VMEM((NEIGHBOR_TILES * (groups + 1) * 8, LANES), F32),
            pltpu.VMEM((blocks, LANES), I32),
            pltpu.VMEM((32, blocks), I32),
            pltpu.SMEM((32, blocks), I32),
            pltpu.SemaphoreType.DMA((3 + len(to_stage),)),
        ],
        compiler_params=params,
        name="route",
    )(*(pltpu.with_memory_space_constraint(a, pltpu.HBM) for a in (air_exchanges[0], destination) + to_stage))
    destination, rows, weights, ocean, skin, depth, mask = results[sends:]

    def send(array, targets):
        return lax.ppermute(array, axes, [(a, b) for a, b in enumerate(targets) if b >= 0])

    arrived = [results[0]] + [send(a, p) for a, p in zip(results[1:], moves["outward"])]
    prepared = pl.pallas_call(
        functools.partial(prepare_kernel, total),
        out_shape=[jax.ShapeDtypeStruct((NEIGHBOR_TILES * groups, LANES), BF16)]
        + [jax.ShapeDtypeStruct((blocks, LANES), I32)] * 2
        + [jax.ShapeDtypeStruct((2 * blocks, groups), BF16)] * NEIGHBOR_TILES,
        in_specs=[vmem] * 2,
        out_specs=[vmem] * (3 + NEIGHBOR_TILES),
        compiler_params=params,
        cost_estimate=pl.CostEstimate(flops=2 * 15 * LANES**3, bytes_accessed=2**19, transcendentals=0),
        name="prepare",
    )(destination, rows)
    returns = len(moves["returns"])
    message = (groups + HALO * FIELDS, LANES)
    row_blocks = weights.shape[0]
    outs = pl.pallas_call(
        functools.partial(remap_kernel, moves["came"], moves["returns"], moves["edges"]),
        out_shape=[
            jax.ShapeDtypeStruct((3, tall, LANES), F32),
            jax.ShapeDtypeStruct((groups, LANES), BF16),
        ]
        + [jax.ShapeDtypeStruct(message, BF16)] * returns,
        in_specs=[vmem] * sends + [hbm] + [vmem] * 6,
        out_specs=[vmem] * (2 + returns),
        scratch_shapes=[
            pltpu.VMEM((NEIGHBOR_TILES * groups * 4 + 8, LANES), F32),
            pltpu.VMEM((row_blocks * 8, LANES), F32),
            pltpu.VMEM((2 * row_blocks, LANES), F32),
            pltpu.VMEM((NEIGHBOR_TILES * groups, LANES), BF16),
            pltpu.VMEM((3 * HALO * FIELDS + 2 * tall, LANES), BF16),
            pltpu.SMEM(pointers.shape, I32),
            pltpu.SemaphoreType.DMA,
        ],
        compiler_params=params,
        name="remap",
    )(*arrived, pltpu.with_memory_space_constraint(pointers, pltpu.HBM), prepared[0], weights, ocean, skin, depth, mask)
    forcing, own = outs[:2]
    received = [send(a, p) for a, p in zip(outs[2:], moves["homeward"])]
    ocean_out, warm = pl.pallas_call(
        functools.partial(
            finish_kernel, moves["sources"], moves["halos"], count_t, count_s, returns
        ),
        out_shape=[
            jax.ShapeDtypeStruct((3, tall, LANES), F32),
            jax.ShapeDtypeStruct((blocks, LANES), F32),
        ],
        in_specs=[vmem] * (returns + 3 + NEIGHBOR_TILES + 4),
        out_specs=[vmem] * 2,
        scratch_shapes=[
            pltpu.VMEM((returns * message[0], LANES), BF16),
            pltpu.VMEM((4, tall + 2 * HALO + 16, LANES), F32),
        ],
        compiler_params=params,
        name="finish",
    )(*received, own, *prepared[1:], ocean, depth, mask, forcing)
    return ocean_out[None], warm.reshape(1, columns)


def solution(mesh):
    return jax.shard_map(
        shards,
        mesh=mesh,
        in_specs=(
            P(("member", "comp"), None, ("tile", "sub")),
            P("comp", ("tile", "sub"), None),
            P("comp", "tile", "sub", None, None),
            P("comp", "tile", "sub", None, None, None, None),
            P(("member", "comp"), None, "tile", "sub"),
            P(("member", "comp"), "tile", "sub"),
            P("comp", "tile", "sub"),
            P("comp", "tile", "sub"),
        ),
        out_specs=(
            P(("member", "comp"), None, "tile", "sub"),
            P(("member", "comp"), ("tile", "sub")),
        ),
        check_vma=False,
    )
```

```python
import functools

import jax
import jax.numpy as jnp
from jax import lax
from jax.experimental import pallas as pl
from jax.experimental.pallas import tpu as pltpu
from jax.sharding import PartitionSpec as P

NEIGHBOR_TILES = 5
MIDDLE = NEIGHBOR_TILES // 2
SUBS = 8
LANES = 128
HALO = 2 * SUBS
FIELDS = 8
F32 = jnp.float32
BF16 = jnp.bfloat16
I32 = jnp.int32
SORT_UNIT = 16
VMEM_LIMIT = 48 * 1024 * 1024


def iota(shape, dim):
    return lax.broadcasted_iota(I32, shape, dim)


def dot(a, b):
    return jnp.dot(a, b, preferred_element_type=F32)


def dot_t(a, b):
    return lax.dot_general(a, b, (((1,), (1,)), ((), ())), preferred_element_type=F32)


def position():
    return lax.axis_index("tile") * lax.axis_size("sub") + lax.axis_index("sub")


def pick(values):
    usual = max(sorted(set(values)), key=values.count)
    mine = position()
    result = jnp.int32(usual)
    for device, value in enumerate(values):
        if value != usual:
            result = jnp.where(mine == device, value, result)
    return result


def ones_where(mask):
    return jnp.where(mask, 1.0, 0.0).astype(BF16)


def offsets_of(destination, total):
    shifted = destination - position() + MIDDLE
    shifted = jnp.where(shifted < 0, shifted + total, shifted)
    return jnp.where(shifted >= total, shifted - total, shifted)


def ranks(offsets):
    rows = offsets.shape[0]
    r, c = iota((LANES, LANES), 0), iota((LANES, LANES), 1)
    before = ones_where(r < c)
    every = jnp.ones((LANES, LANES), BF16)
    earlier = ones_where(iota((rows, rows), 1) < iota((rows, rows), 0))
    result = []
    for o in range(NEIGHBOR_TILES):
        mask = offsets == o
        hot = ones_where(mask)
        inside = dot(hot, before)
        count = dot(hot, every)
        base = dot(earlier, count.astype(BF16))
        result.append((mask, hot, inside, count, base))
    return result


def route_kernel(sent, total, x_hbm, dest_hbm, *rest):
    staged = len(rest) - len(sent) - 8
    sources, rest = rest[: staged // 2], rest[staged // 2 :]
    outs, dest_ref, rest = rest[: len(sent)], rest[len(sent)], rest[len(sent) + 1 :]
    targets, rest = rest[: staged // 2], rest[staged // 2 :]
    x_ref, comb, place, pos_scr, vec, scal, sem = rest
    copies = [
        pltpu.make_async_copy(a, b, sem.at[i])
        for i, (a, b) in enumerate(
            zip((dest_hbm, x_hbm) + tuple(sources), (dest_ref, x_ref) + tuple(targets))
        )
    ]
    for copy in copies:
        copy.start()
    copies[0].wait()
    blocks = dest_ref.shape[0]
    unit = SORT_UNIT
    groups = outs[0].shape[0] // 4
    stride = (groups + 1) * 8
    offsets = offsets_of(dest_ref[...], total)
    ones8 = jnp.ones((8, LANES), BF16)
    sub8 = iota((8, blocks), 0)
    earlier = ones_where(iota((blocks, blocks), 0) < iota((blocks, blocks), 1))
    before = ones_where(iota((LANES, 2 * LANES), 0) < iota((LANES, 2 * LANES), 1))
    hots = [ones_where(offsets == o) for o in range(NEIGHBOR_TILES)]
    counts = jnp.zeros((8, blocks), F32)
    start_t = jnp.zeros((8, blocks), F32)
    starts = jnp.zeros((8, blocks), F32)
    for o, hot in enumerate(hots):
        count_t = dot_t(ones8, hot)
        counts = jnp.where(sub8 == o, count_t, counts)
        starts = jnp.where(sub8 == o, start_t, starts)
        start_t = start_t + count_t
    base = dot(counts.astype(BF16), earlier).astype(I32)
    counts, starts = counts.astype(I32), starts.astype(I32)
    at = jnp.bitwise_and(base, LANES - 1)
    vec[0:8, :] = sub8 * stride + lax.shift_right_logical(base, 7) * 8
    vec[8:16, :] = jnp.bitwise_and(at - starts, LANES - 1)
    vec[16:24, :] = at
    vec[24:32, :] = at + counts - LANES
    copy = pltpu.make_async_copy(vec, scal, sem.at[len(copies)])
    copy.start()
    start = jnp.zeros((blocks, LANES), F32)
    pos = jnp.zeros((blocks, LANES), F32)
    for o, hot in enumerate(hots):
        inside = dot(hot, before)
        pos = jnp.where(offsets == o, start + inside[:, :LANES], pos)
        start = start + inside[:, LANES:]
    pos_scr[...] = pos.astype(I32)
    f, g = iota((8, 8), 1), jnp.bitwise_and(iota((8, 8), 0), 3)
    plus = ((g == 0) & (f == 0)) | ((g == 1) & (f == 1)) | ((g == 2) & (f == 3)) | ((g == 3) & (f >= 6))
    minus = ((g == 2) & (f == 2)) | ((g == 3) & ((f == 4) | (f == 5)))
    combine = (jnp.where(plus, 1.0, 0.0) - jnp.where(minus, 1.0, 0.0)).astype(BF16)
    copies[1].wait()
    comb[...] = dot(combine, x_ref[...]).astype(BF16)

    lines = iota((LANES, LANES), 0)

    def sort_blocks(i):
        result = []
        for u in range(0, unit, 2):
            b = i * unit + u
            columns = comb[:, pl.ds(pl.multiple_of(b * LANES, 2 * LANES), 2 * LANES)].astype(F32)
            columns = jnp.concatenate([columns[:, :LANES], columns[:, LANES:]], axis=0).astype(BF16)
            hot = [ones_where(pos_scr[pl.ds(b + v, 1), :] == lines) for v in range(2)]
            both = dot_t(columns, jnp.concatenate(hot, axis=0))
            result += [both[:8, :LANES], both[8:, LANES:]]
        return result

    lane = iota((8, LANES), 1)

    def place_blocks(i, values, current):
        current = list(current)
        for u in range(unit):
            b = i * unit + u
            for o in range(NEIGHBOR_TILES):
                turned = pltpu.roll(values[u], scal[8 + o, b], 1)
                merged = jnp.where(lane < scal[16 + o, b], current[o], turned)
                place[pl.ds(pl.multiple_of(scal[o, b], 8), 8), :] = merged
                current[o] = jnp.where(lane < scal[24 + o, b], turned, merged)
        return current

    def step(i, carry):
        values = sort_blocks(i + 1)
        return tuple(place_blocks(i, carry[NEIGHBOR_TILES:], carry[:NEIGHBOR_TILES])) + tuple(values)

    steps = blocks // unit
    current = [jnp.zeros((8, LANES), F32) for _ in range(NEIGHBOR_TILES)]
    values = sort_blocks(0)
    copy.wait()
    carry = lax.fori_loop(0, steps - 1, step, tuple(current) + tuple(values))
    current = place_blocks(steps - 1, carry[NEIGHBOR_TILES:], carry[:NEIGHBOR_TILES])
    pair_lane = jnp.where(iota((8, LANES), 0) < 4, lane, lane + LANES)
    upper = iota((groups // 2, 8, LANES), 1) < 4
    slot = iota((groups // 2, 8, LANES), 0) * (2 * LANES) + pair_lane[None]
    last = blocks - 1

    def length(o):
        return (scal[o, last] - o * stride) * (LANES // 8) + scal[24 + o, last] + LANES

    for o in range(NEIGHBOR_TILES):
        full = lax.shift_right_logical(length(o), 7) * 8 + o * stride
        place[pl.ds(pl.multiple_of(full, 8), 8), :] = current[o]
    for offset, out in zip(sent, outs):
        o = pick(offset)
        tiles = place[pl.ds(pl.multiple_of(o * stride, 8), groups * 8), :]
        tiles = tiles.reshape(groups // 2, 2, 8, LANES)
        both = jnp.where(upper, tiles[:, 0], tiles[:, 1])
        both = jnp.where(slot < length(o), both, 0.0)
        out[...] = both.reshape(groups * 4, LANES).astype(BF16)
    for copy in copies[2:]:
        copy.wait()


def prepare_kernel(
    total, dest_ref, row_ref, ocean_ref, depth_ref, mask_ref,
    blocks_ref, edge_rows, edge_columns, index_ref, code_ref, *hot_refs
):
    blocks = dest_ref.shape[0]
    groups = hot_refs[0].shape[1]
    offsets = offsets_of(dest_ref[...], total)
    index = jnp.zeros((blocks, LANES), I32)
    code = jnp.zeros((blocks, LANES), I32)
    group_id = iota((blocks, groups), 1)
    lane = iota((blocks, LANES), 1)
    for o, (mask, hot, inside, count, base) in enumerate(ranks(offsets)):
        base = base.astype(I32)
        rank = base + inside.astype(I32)
        first = lax.shift_right_logical(base, 7)
        index = jnp.where(mask, jnp.bitwise_and(rank, LANES - 1), index)
        code = jnp.where(mask, code + o, code)
        code = jnp.where(lane >= jnp.bitwise_and(base, LANES - 1), code + (8 << o), code)
        hot_refs[o][0:blocks, :] = ones_where(group_id == first[:, :groups])
        hot_refs[o][blocks:, :] = ones_where(group_id == first[:, :groups] + 1)
    index_ref[...] = index
    code_ref[...] = code
    row = jnp.concatenate([row_ref[0:1, :], row_ref[1:2, :]], axis=1)
    blocks_ref[...] = ones_where(iota(blocks_ref.shape, 0) == row)
    fields = [ocean_ref[0], ocean_ref[1], ocean_ref[2], mask_ref[...].astype(F32), depth_ref[...]]
    for i, low in enumerate((False, True)):
        edge_rows[i] = packed_rows(fields, low).astype(BF16)
        edge_columns[i] = packed_columns(fields, low, 0).astype(BF16)


def packed_columns(fields, low, start):
    lane = iota(fields[0].shape, 1)
    packed = None
    for i, field in enumerate(fields, start):
        turn = (i * HALO + (0 if low else HALO)) % LANES
        turned = pltpu.roll(field, turn, 1) if turn else field
        packed = turned if packed is None else jnp.where(lane >= i * HALO, turned, packed)
    return packed


def packed_rows(fields, low):
    tall = fields[0].shape[0]
    span = slice(0, HALO) if low else slice(tall - HALO, tall)
    return jnp.concatenate([x[span] for x in fields], axis=0)


def remap_kernel(came, returns, edges, *rest):
    arrived, rest = rest[: len(came)], rest[len(came) :]
    ptr_hbm, hot_ref, edge_rows, edge_columns, w_ref, skin_ref, mask_ref = rest[:7]
    forcing_ref, own_ref = rest[7:9]
    message_refs = rest[9 : 9 + len(returns)]
    slots, mapped, shares, homebound, bank, ptr_ref, sem = rest[9 + len(returns) :]
    pointers = pltpu.make_async_copy(ptr_hbm, ptr_ref, sem)
    pointers.start()
    per_step = 8
    size = arrived[0].shape[0]
    for offset, block in zip(came, arrived):
        o = pick(offset)
        slots[pl.ds(pl.multiple_of(o * size, size), size), :] = block[...].astype(F32)
    slots[NEIGHBOR_TILES * size :, :] = jnp.zeros((8, LANES), F32)
    pointers.wait()
    sub = iota((per_step, LANES), 0)

    def forward(step):
        for j in range(per_step):
            k = step * per_step + j
            both = [slots[pl.ds(ptr_ref[w, k] * 4, 8), :] for w in range(2)]
            both = jnp.concatenate(both, axis=0).astype(BF16)
            product = dot_t(both, w_ref[k].reshape(2 * LANES, LANES))
            mapped[pl.ds(k * 8, 8), :] = product[:8, :LANES] + product[8:, LANES:]

    def middle(step):
        rows = pl.ds(step * per_step, per_step)
        u, v, p, h = (mapped[pl.ds(step * per_step * 8 + i, per_step, stride=8), :] for i in range(4))
        speed = jnp.sqrt(u * u + v * v + 1.0)
        forcing_ref[0, rows, :] = 0.2 * speed * u
        forcing_ref[1, rows, :] = 0.2 * speed * v
        forcing_ref[2, rows, :] = 0.5 * p
        return (skin_ref[rows, :] + 0.25 * mask_ref[rows, :].astype(F32) * h).astype(BF16).astype(F32)

    def back(step, sst):
        left = []
        for j in range(per_step):
            only = jnp.where(sub == j, sst, 0.0)
            zero = jnp.zeros_like(only)
            left.append(jnp.concatenate([only, zero], axis=0).astype(BF16))
            left.append(jnp.concatenate([zero, only], axis=0).astype(BF16))
        left = jnp.concatenate(left, axis=1)
        right = w_ref[pl.ds(step * per_step, per_step)].reshape(per_step * 2 * LANES, LANES)
        total = dot(left, right)
        for w in range(2):
            rows = slice((w * steps + step) * per_step, (w * steps + step + 1) * per_step)
            shares[rows, :] = total[w * per_step : (w + 1) * per_step]

    steps = w_ref.shape[0] // per_step
    for i in range(steps):
        forward(i)
    for i in range(steps):
        back(i, middle(i))

    every = shares[...]
    high = every.astype(BF16)
    low = (every - high.astype(F32)).astype(BF16)
    split = jnp.concatenate([high, low], axis=1)
    groups = own_ref.shape[0]
    value = dot(hot_ref[...], split)
    returned = (value[:, :LANES] + value[:, LANES:]).astype(BF16)
    homebound[...] = returned
    own_ref[...] = returned[MIDDLE * groups : (MIDDLE + 1) * groups]
    fields = [forcing_ref[0], forcing_ref[1], forcing_ref[2]]
    tall = fields[0].shape[0]
    rows = HALO * FIELDS
    still = HALO * (FIELDS - len(fields))
    lane = iota((tall, LANES), 1)
    for i, low in enumerate((False, True)):
        bank[i * rows : i * rows + still, :] = edge_rows[i]
        bank[i * rows + still : (i + 1) * rows, :] = packed_rows(fields, low).astype(BF16)
        columns = packed_columns(fields, low, FIELDS - len(fields))
        columns = jnp.where(lane < still, edge_columns[i].astype(F32), columns)
        bank[2 * rows + i * tall : 2 * rows + (i + 1) * tall, :] = columns.astype(BF16)
    bank[2 * rows + 2 * tall :, :] = jnp.zeros((rows, LANES), BF16)
    for offset, edge, out in zip(returns, edges, message_refs):
        first = pl.multiple_of(pick(offset) * groups, 16)
        out[0:groups, :] = homebound[pl.ds(first, groups), :]
        first = pl.multiple_of(pick(edge), 16)
        out[groups:, :] = bank[pl.ds(first, rows), :]


def finish_kernel(sources, halos, count_t, count_s, messages, *rest):
    message_refs, rest = rest[:messages], rest[messages:]
    own_ref, index_ref, code_ref = rest[:3]
    hot_refs, rest = rest[3 : 3 + NEIGHBOR_TILES], rest[3 + NEIGHBOR_TILES :]
    ocean_ref, depth_ref, mask_ref, forcing_ref, out_ref, warm_ref, inbox, shifted = rest
    t, s = lax.axis_index("tile"), lax.axis_index("sub")
    size = message_refs[0].shape[0]
    groups = own_ref.shape[0]
    for i, ref in enumerate(message_refs):
        inbox[i * size : (i + 1) * size, :] = ref[...]
    blocks = index_ref.shape[0]
    index = index_ref[...]
    code = code_ref[...]
    warm = jnp.zeros((blocks, LANES), F32)
    for o in range(NEIGHBOR_TILES):
        if o == MIDDLE:
            value = own_ref[...]
        else:
            value = inbox[pl.ds(pl.multiple_of(pick(sources[o]) * size, 16), groups), :]
        lines = dot(hot_refs[o][...], value)
        upper = jnp.bitwise_and(code, 8 << o) != 0
        lines = jnp.where(upper, lines[:blocks], lines[blocks:])
        picked = jnp.take_along_axis(lines, index, axis=1)
        warm = jnp.where(jnp.bitwise_and(code, 7) == o, picked, warm)
    warm_ref[...] = warm

    tall = depth_ref.shape[0]
    full = tall + 2 * HALO

    def halo(dt, ds):
        ok = jnp.bool_(True)
        if dt == 1:
            ok &= t > 0
        if dt == -1:
            ok &= t < count_t - 1
        if ds == 1:
            ok &= s > 0
        if ds == -1:
            ok &= s < count_s - 1
        rows = tall if dt == 0 else (HALO if ds else HALO * FIELDS)
        first = pl.multiple_of(pick(halos[dt, ds]) * size + groups, 16)
        value = inbox[pl.ds(first, rows), :].astype(F32)
        return jnp.where(ok, value, 0.0)

    from_left = jnp.concatenate([halo(1, 1), halo(0, 1), halo(-1, 1)], axis=0)
    from_right = jnp.concatenate([halo(1, -1), halo(0, -1), halo(-1, -1)], axis=0)
    above, below = halo(1, 0), halo(-1, 0)
    lane = iota((full, LANES), 1)
    inner = [ocean_ref[0], ocean_ref[1], ocean_ref[2], mask_ref[...].astype(F32), depth_ref[...]]
    inner += [forcing_ref[0], forcing_ref[1], forcing_ref[2]]
    wide = []
    for i in range(FIELDS):
        rows = slice(i * HALO, (i + 1) * HALO)
        main = jnp.concatenate([above[rows], inner[i], below[rows]], axis=0)
        turn = (LANES - HALO - i * HALO) % LANES
        left = pltpu.roll(from_left, turn, 1) if turn else from_left
        turn = (LANES - i * HALO) % LANES
        right = pltpu.roll(from_right, turn, 1) if turn else from_right
        side = jnp.where(lane < HALO, right, jnp.where(lane >= LANES - HALO, left, 0.0))
        wide.append([main, side])
    eta, east, north, m, depth, stress_x, stress_y, fresh = wide
    row = iota((full, LANES), 0) + (t * tall - HALO)
    coriolis = 0.1 + 0.2 * (row.astype(F32) + 0.5) / (tall * count_t)

    both = range(2)
    half_m = [0.5 * m[i] for i in both]
    half_d = [half_m[i] * depth[i] for i in both]
    turning = [m[i] * coriolis for i in both]
    fresh = [m[i] * fresh[i] for i in both]
    stress_x = [m[i] * stress_x[i] for i in both]
    stress_y = [m[i] * stress_y[i] for i in both]
    shifted[:, 0:8, :] = jnp.zeros((4, 8, LANES), F32)
    shifted[:, 8 + full :, :] = jnp.zeros((4, 8, LANES), F32)

    def across(a):
        ahead = [pltpu.roll(a[i], LANES - 1, 1) for i in both]
        behind = [pltpu.roll(a[i], 1, 1) for i in both]
        columns = lane[: a[0].shape[0]]
        return [
            jnp.where(columns == LANES - 1, ahead[1 - i], ahead[i])
            - jnp.where(columns == 0, behind[1 - i], behind[i])
            for i in both
        ]

    def along(a, first, rows, place):
        result = []
        for i in both:
            shifted[place + i, 8 + first : 8 + first + a[i].shape[0], :] = a[i]
            result.append(
                shifted[place + i, 9 + rows.start : 9 + rows.stop, :]
                - shifted[place + i, 7 + rows.start : 7 + rows.stop, :]
            )
        return result

    first, last = 0, full
    out_east, out_north = across(east), along(north, 0, slice(0, full), 0)
    eta, east, north = ([m[i] * a[i] for i in both] for a in (eta, east, north))
    for step in range(1, SUBS + 1):
        if step > 1:
            out_east, out_north = across(east), along(north, first, slice(first, last), 0)
        eta = [eta[i] + fresh[i] - half_m[i] * (out_east[i] + out_north[i]) for i in both]
        below_first = 2 * step // 8 * 8
        slope_y = along(eta, first, slice(below_first, full - below_first), 2)
        if below_first > first:
            cut = slice(below_first - first, full - below_first - first)
            eta, east, north, turning, stress_x, stress_y, half_d, fresh, half_m = (
                [x[cut] for x in a]
                for a in (eta, east, north, turning, stress_x, stress_y, half_d, fresh, half_m)
            )
            first, last = below_first, full - below_first
        slope_x = across(eta)
        new_east = [
            east[i] + turning[i] * north[i] + stress_x[i] - half_d[i] * slope_x[i] for i in both
        ]
        north = [
            north[i] - turning[i] * east[i] + stress_y[i] - half_d[i] * slope_y[i] for i in both
        ]
        east = new_east
    for i, a in enumerate((eta, east, north)):
        out_ref[i] = a[0][HALO - first : HALO - first + tall]


SCHEDULES = {
    (4, 2): (
        [
            [2, 3, 4, 1, 6, 7, 0, 5],
            [7, 2, 1, 5, 3, 6, 4, 0],
            [6, 7, 0, 4, 2, 3, 5, 1],
            [1, 0, 3, 2, 5, 4, 7, 6],
        ],
        [
            [3, 6, 5, 0, 7, 2, 1, 4],
            [2, 3, 4, 1, 6, 7, 0, 5],
            [7, 2, 1, 4, 3, 6, 5, 0],
            [6, 7, 0, 5, 2, 3, 4, 1],
            [1, 0, 3, 2, 5, 4, 7, 6],
        ],
    ),
}


def schedule(count_t, count_s):
    total = count_t * count_s
    if (count_t, count_s) in SCHEDULES:
        return SCHEDULES[count_t, count_s]
    rings = [
        [(i + distance) % total for i in range(total)]
        for distance in range(-MIDDLE, MIDDLE + 1)
        if distance
    ]
    others = []
    for dt in (-1, 1):
        for ds in (-1, 0, 1):
            if MIDDLE < abs(dt * count_s + ds):
                targets = [-1] * total
                for device in range(total):
                    t, s = device // count_s + dt, device % count_s + ds
                    if 0 <= t < count_t and 0 <= s < count_s:
                        targets[device] = t * count_s + s
                others.append(targets)
    return rings, rings + others


def plan(count_t, count_s, groups, tall):
    total = count_t * count_s
    outward, homeward = schedule(count_t, count_s)

    def offset(a, b):
        o = (b - a + MIDDLE) % total
        return o if o < NEIGHBOR_TILES else -1

    def step(a, b):
        dt, ds = b // count_s - a // count_s, b % count_s - a % count_s
        return (dt, ds) if abs(dt) <= 1 and abs(ds) <= 1 else None

    def senders(targets):
        return [targets.index(d) if d in targets else -1 for d in range(total)]

    rows = HALO * FIELDS
    start = {(1, 0): 0, (-1, 0): rows}
    for ds, first in ((1, 2 * rows), (-1, 2 * rows + tall)):
        start[0, ds] = start[-1, ds] = first
        start[1, ds] = first + tall - HALO
    result = {"outward": outward, "homeward": homeward}
    result["sent"] = [[offset(a, b) for a, b in enumerate(p)] for p in outward]
    result["sent"].insert(0, [MIDDLE] * total)
    result["came"] = [[offset(a, b) for b, a in enumerate(senders(p))] for p in outward]
    result["came"].insert(0, [MIDDLE] * total)
    result["returns"] = [
        [max(offset(b, a), 0) if b >= 0 else 0 for a, b in enumerate(p)] for p in homeward
    ]
    result["edges"] = [
        [start[step(a, b)] if b >= 0 and step(a, b) else 0 for a, b in enumerate(p)] for p in homeward
    ]
    sources = [[0] * total for _ in range(NEIGHBOR_TILES)]
    halos = {(dt, ds): [0] * total for dt in (-1, 0, 1) for ds in (-1, 0, 1)}
    for i, p in enumerate(homeward):
        for a, b in enumerate(p):
            if b >= 0:
                if offset(b, a) >= 0:
                    sources[offset(b, a)][b] = i
                if step(a, b):
                    halos[step(a, b)][b] = i
    result["sources"], result["halos"] = sources, halos
    return result


def shards(
    air_exchanges,
    air_destination,
    diagonal_group_pointer,
    interpolation_factors,
    marine_fields,
    skin_warmth_anomaly,
    gravity_bathymetry,
    marine_indicator,
):
    axes = ("tile", "sub")
    count_t, count_s = lax.axis_size("tile"), lax.axis_size("sub")
    total = count_t * count_s
    columns = air_destination.shape[1]
    blocks = columns // LANES
    groups = columns // 2 // LANES
    destination = air_destination.reshape(blocks, LANES)
    vmem = pl.BlockSpec(memory_space=pltpu.VMEM)
    params = pltpu.CompilerParams(vmem_limit_bytes=VMEM_LIMIT)
    hbm = pl.BlockSpec(memory_space=pltpu.HBM)
    pointers = diagonal_group_pointer[0, 0, 0].T
    to_stage = (
        pointers,
        interpolation_factors[0, 0, 0],
        marine_fields[0],
        skin_warmth_anomaly[0],
        gravity_bathymetry[0],
        marine_indicator[0],
    )
    tall = skin_warmth_anomaly.shape[1]
    moves = plan(count_t, count_s, groups, tall)
    sends = len(moves["sent"])
    results = pl.pallas_call(
        functools.partial(route_kernel, moves["sent"], total),
        out_shape=[jax.ShapeDtypeStruct((groups * 4, LANES), BF16)] * sends
        + [jax.ShapeDtypeStruct(a.shape, a.dtype) for a in (destination,) + to_stage],
        in_specs=[hbm] * (2 + len(to_stage)),
        out_specs=[vmem] * (sends + 1 + len(to_stage)),
        scratch_shapes=[
            pltpu.VMEM((8, columns), BF16),
            pltpu.VMEM((8, columns), BF16),
            pltpu.VMEM((NEIGHBOR_TILES * (groups + 1) * 8, LANES), F32),
            pltpu.VMEM((blocks, LANES), I32),
            pltpu.VMEM((32, blocks), I32),
            pltpu.SMEM((32, blocks), I32),
            pltpu.SemaphoreType.DMA((3 + len(to_stage),)),
        ],
        compiler_params=params,
        name="route",
    )(*(pltpu.with_memory_space_constraint(a, pltpu.HBM) for a in (air_exchanges[0], destination) + to_stage))
    destination, rows, weights, ocean, skin, depth, mask = results[sends:]

    def send(array, targets):
        return lax.ppermute(array, axes, [(a, b) for a, b in enumerate(targets) if b >= 0])

    arrived = [results[0]] + [send(a, p) for a, p in zip(results[1:], moves["outward"])]
    prepared = pl.pallas_call(
        functools.partial(prepare_kernel, total),
        out_shape=[
            jax.ShapeDtypeStruct((NEIGHBOR_TILES * groups, LANES), BF16),
            jax.ShapeDtypeStruct((2, HALO * (FIELDS - 3), LANES), BF16),
            jax.ShapeDtypeStruct((2, tall, LANES), BF16),
        ]
        + [jax.ShapeDtypeStruct((blocks, LANES), I32)] * 2
        + [jax.ShapeDtypeStruct((2 * blocks, groups), BF16)] * NEIGHBOR_TILES,
        in_specs=[vmem] * 5,
        out_specs=[vmem] * (5 + NEIGHBOR_TILES),
        compiler_params=params,
        cost_estimate=pl.CostEstimate(flops=2 * 15 * LANES**3, bytes_accessed=2**19, transcendentals=0),
        name="prepare",
    )(destination, rows, ocean, depth, mask)
    returns = len(moves["returns"])
    message = (groups + HALO * FIELDS, LANES)
    row_blocks = weights.shape[0]
    outs = pl.pallas_call(
        functools.partial(remap_kernel, moves["came"], moves["returns"], moves["edges"]),
        out_shape=[
            jax.ShapeDtypeStruct((3, tall, LANES), F32),
            jax.ShapeDtypeStruct((groups, LANES), BF16),
        ]
        + [jax.ShapeDtypeStruct(message, BF16)] * returns,
        in_specs=[vmem] * sends + [hbm] + [vmem] * 6,
        out_specs=[vmem] * (2 + returns),
        scratch_shapes=[
            pltpu.VMEM((NEIGHBOR_TILES * groups * 4 + 8, LANES), F32),
            pltpu.VMEM((row_blocks * 8, LANES), F32),
            pltpu.VMEM((2 * row_blocks, LANES), F32),
            pltpu.VMEM((NEIGHBOR_TILES * groups, LANES), BF16),
            pltpu.VMEM((3 * HALO * FIELDS + 2 * tall, LANES), BF16),
            pltpu.SMEM(pointers.shape, I32),
            pltpu.SemaphoreType.DMA,
        ],
        compiler_params=params,
        name="remap",
    )(*arrived, pltpu.with_memory_space_constraint(pointers, pltpu.HBM), *prepared[:3], weights, skin, mask)
    forcing, own = outs[:2]
    received = [send(a, p) for a, p in zip(outs[2:], moves["homeward"])]
    ocean_out, warm = pl.pallas_call(
        functools.partial(
            finish_kernel, moves["sources"], moves["halos"], count_t, count_s, returns
        ),
        out_shape=[
            jax.ShapeDtypeStruct((3, tall, LANES), F32),
            jax.ShapeDtypeStruct((blocks, LANES), F32),
        ],
        in_specs=[vmem] * (returns + 3 + NEIGHBOR_TILES + 4),
        out_specs=[vmem] * 2,
        scratch_shapes=[
            pltpu.VMEM((returns * message[0], LANES), BF16),
            pltpu.VMEM((4, tall + 2 * HALO + 16, LANES), F32),
        ],
        compiler_params=params,
        name="finish",
    )(*received, own, *prepared[3:], ocean, depth, mask, forcing)
    return ocean_out[None], warm.reshape(1, columns)


def solution(mesh):
    return jax.shard_map(
        shards,
        mesh=mesh,
        in_specs=(
            P(("member", "comp"), None, ("tile", "sub")),
            P("comp", ("tile", "sub"), None),
            P("comp", "tile", "sub", None, None),
            P("comp", "tile", "sub", None, None, None, None),
            P(("member", "comp"), None, "tile", "sub"),
            P(("member", "comp"), "tile", "sub"),
            P("comp", "tile", "sub"),
            P("comp", "tile", "sub"),
        ),
        out_specs=(
            P(("member", "comp"), None, "tile", "sub"),
            P(("member", "comp"), ("tile", "sub")),
        ),
        check_vma=False,
    )
```

```python
import functools

import jax
import jax.numpy as jnp
from jax import lax
from jax.experimental import pallas as pl
from jax.experimental.pallas import tpu as pltpu
from jax.sharding import PartitionSpec as P

NEIGHBOR_TILES = 5
MIDDLE = NEIGHBOR_TILES // 2
SUBS = 8
LANES = 128
HALO = 2 * SUBS
FIELDS = 8
F32 = jnp.float32
BF16 = jnp.bfloat16
I32 = jnp.int32
SORT_UNIT = 16
VMEM_LIMIT = 48 * 1024 * 1024


def iota(shape, dim):
    return lax.broadcasted_iota(I32, shape, dim)


def dot(a, b):
    return jnp.dot(a, b, preferred_element_type=F32)


def dot_t(a, b):
    return lax.dot_general(a, b, (((1,), (1,)), ((), ())), preferred_element_type=F32)


def position():
    return lax.axis_index("tile") * lax.axis_size("sub") + lax.axis_index("sub")


def pick(values):
    usual = max(sorted(set(values)), key=values.count)
    mine = position()
    result = jnp.int32(usual)
    for device, value in enumerate(values):
        if value != usual:
            result = jnp.where(mine == device, value, result)
    return result


def ones_where(mask):
    return jnp.where(mask, 1.0, 0.0).astype(BF16)


def offsets_of(destination, total):
    shifted = destination - position() + MIDDLE
    shifted = jnp.where(shifted < 0, shifted + total, shifted)
    return jnp.where(shifted >= total, shifted - total, shifted)


def ranks(offsets):
    rows = offsets.shape[0]
    r, c = iota((LANES, LANES), 0), iota((LANES, LANES), 1)
    before = ones_where(r < c)
    every = jnp.ones((LANES, LANES), BF16)
    earlier = ones_where(iota((rows, rows), 1) < iota((rows, rows), 0))
    result = []
    for o in range(NEIGHBOR_TILES):
        mask = offsets == o
        hot = ones_where(mask)
        inside = dot(hot, before)
        count = dot(hot, every)
        base = dot(earlier, count.astype(BF16))
        result.append((mask, hot, inside, count, base))
    return result


def route_kernel(sent, total, x_hbm, dest_hbm, *rest):
    staged = len(rest) - len(sent) - 8
    sources, rest = rest[: staged // 2], rest[staged // 2 :]
    outs, dest_ref, rest = rest[: len(sent)], rest[len(sent)], rest[len(sent) + 1 :]
    targets, rest = rest[: staged // 2], rest[staged // 2 :]
    x_ref, comb, place, pos_scr, vec, scal, sem = rest
    copies = [
        pltpu.make_async_copy(a, b, sem.at[i])
        for i, (a, b) in enumerate(
            zip((dest_hbm, x_hbm) + tuple(sources), (dest_ref, x_ref) + tuple(targets))
        )
    ]
    for copy in copies:
        copy.start()
    copies[0].wait()
    blocks = dest_ref.shape[0]
    unit = SORT_UNIT
    groups = outs[0].shape[0] // 4
    stride = (groups + 1) * 8
    offsets = offsets_of(dest_ref[...], total)
    ones8 = jnp.ones((8, LANES), BF16)
    sub8 = iota((8, blocks), 0)
    earlier = ones_where(iota((blocks, blocks), 0) < iota((blocks, blocks), 1))
    before = ones_where(iota((LANES, 2 * LANES), 0) < iota((LANES, 2 * LANES), 1))
    hots = [ones_where(offsets == o) for o in range(NEIGHBOR_TILES)]
    counts = jnp.zeros((8, blocks), F32)
    start_t = jnp.zeros((8, blocks), F32)
    starts = jnp.zeros((8, blocks), F32)
    for o, hot in enumerate(hots):
        count_t = dot_t(ones8, hot)
        counts = jnp.where(sub8 == o, count_t, counts)
        starts = jnp.where(sub8 == o, start_t, starts)
        start_t = start_t + count_t
    base = dot(counts.astype(BF16), earlier).astype(I32)
    counts, starts = counts.astype(I32), starts.astype(I32)
    at = jnp.bitwise_and(base, LANES - 1)
    vec[0:8, :] = sub8 * stride + lax.shift_right_logical(base, 7) * 8
    vec[8:16, :] = jnp.bitwise_and(at - starts, LANES - 1)
    vec[16:24, :] = at
    vec[24:32, :] = at + counts - LANES
    copy = pltpu.make_async_copy(vec, scal, sem.at[len(copies)])
    copy.start()
    start = jnp.zeros((blocks, LANES), F32)
    pos = jnp.zeros((blocks, LANES), F32)
    for o, hot in enumerate(hots):
        inside = dot(hot, before)
        pos = jnp.where(offsets == o, start + inside[:, :LANES], pos)
        start = start + inside[:, LANES:]
    pos_scr[...] = pos.astype(I32)
    f, g = iota((8, 8), 1), jnp.bitwise_and(iota((8, 8), 0), 3)
    plus = ((g == 0) & (f == 0)) | ((g == 1) & (f == 1)) | ((g == 2) & (f == 3)) | ((g == 3) & (f >= 6))
    minus = ((g == 2) & (f == 2)) | ((g == 3) & ((f == 4) | (f == 5)))
    combine = (jnp.where(plus, 1.0, 0.0) - jnp.where(minus, 1.0, 0.0)).astype(BF16)
    copies[1].wait()
    comb[...] = dot(combine, x_ref[...]).astype(BF16)

    lines = iota((LANES, LANES), 0)

    def sort_blocks(i):
        result = []
        for u in range(0, unit, 2):
            b = i * unit + u
            columns = comb[:, pl.ds(pl.multiple_of(b * LANES, 2 * LANES), 2 * LANES)].astype(F32)
            columns = jnp.concatenate([columns[:, :LANES], columns[:, LANES:]], axis=0).astype(BF16)
            hot = [ones_where(pos_scr[pl.ds(b + v, 1), :] == lines) for v in range(2)]
            both = dot_t(columns, jnp.concatenate(hot, axis=0))
            result += [both[:8, :LANES], both[8:, LANES:]]
        return result

    lane = iota((8, LANES), 1)

    def place_blocks(i, values, current):
        current = list(current)
        for u in range(unit):
            b = i * unit + u
            for o in range(NEIGHBOR_TILES):
                turned = pltpu.roll(values[u], scal[8 + o, b], 1)
                merged = jnp.where(lane < scal[16 + o, b], current[o], turned)
                place[pl.ds(pl.multiple_of(scal[o, b], 8), 8), :] = merged
                current[o] = jnp.where(lane < scal[24 + o, b], turned, merged)
        return current

    def step(i, carry):
        values = sort_blocks(i + 1)
        return tuple(place_blocks(i, carry[NEIGHBOR_TILES:], carry[:NEIGHBOR_TILES])) + tuple(values)

    steps = blocks // unit
    current = [jnp.zeros((8, LANES), F32) for _ in range(NEIGHBOR_TILES)]
    values = sort_blocks(0)
    copy.wait()
    carry = lax.fori_loop(0, steps - 1, step, tuple(current) + tuple(values))
    current = place_blocks(steps - 1, carry[NEIGHBOR_TILES:], carry[:NEIGHBOR_TILES])
    pair_lane = jnp.where(iota((8, LANES), 0) < 4, lane, lane + LANES)
    upper = iota((groups // 2, 8, LANES), 1) < 4
    slot = iota((groups // 2, 8, LANES), 0) * (2 * LANES) + pair_lane[None]
    last = blocks - 1

    def length(o):
        return (scal[o, last] - o * stride) * (LANES // 8) + scal[24 + o, last] + LANES

    for o in range(NEIGHBOR_TILES):
        full = lax.shift_right_logical(length(o), 7) * 8 + o * stride
        place[pl.ds(pl.multiple_of(full, 8), 8), :] = current[o]
    for offset, out in zip(sent, outs):
        o = pick(offset)
        tiles = place[pl.ds(pl.multiple_of(o * stride, 8), groups * 8), :]
        tiles = tiles.reshape(groups // 2, 2, 8, LANES)
        both = jnp.where(upper, tiles[:, 0], tiles[:, 1])
        both = jnp.where(slot < length(o), both, 0.0)
        out[...] = both.reshape(groups * 4, LANES).astype(BF16)
    for copy in copies[2:]:
        copy.wait()


def prepare_kernel(
    total, dest_ref, row_ref, ocean_ref, depth_ref, mask_ref,
    blocks_ref, edge_rows, edge_columns, index_ref, code_ref, *hot_refs
):
    blocks = dest_ref.shape[0]
    groups = hot_refs[0].shape[1]
    offsets = offsets_of(dest_ref[...], total)
    index = jnp.zeros((blocks, LANES), I32)
    code = jnp.zeros((blocks, LANES), I32)
    group_id = iota((blocks, groups), 1)
    lane = iota((blocks, LANES), 1)
    for o, (mask, hot, inside, count, base) in enumerate(ranks(offsets)):
        base = base.astype(I32)
        rank = base + inside.astype(I32)
        first = lax.shift_right_logical(base, 7)
        index = jnp.where(mask, jnp.bitwise_and(rank, LANES - 1), index)
        code = jnp.where(mask, code + o, code)
        code = jnp.where(lane >= jnp.bitwise_and(base, LANES - 1), code + (8 << o), code)
        hot_refs[o][0:blocks, :] = ones_where(group_id == first[:, :groups])
        hot_refs[o][blocks:, :] = ones_where(group_id == first[:, :groups] + 1)
    index_ref[...] = index
    code_ref[...] = code
    row = jnp.concatenate([row_ref[0:1, :], row_ref[1:2, :]], axis=1)
    blocks_ref[...] = ones_where(iota(blocks_ref.shape, 0) == row)
    fields = [ocean_ref[0], ocean_ref[1], ocean_ref[2], mask_ref[...].astype(F32), depth_ref[...]]
    for i, low in enumerate((False, True)):
        edge_rows[i] = packed_rows(fields, low).astype(BF16)
        edge_columns[i] = packed_columns(fields, low, 0).astype(BF16)


def packed_columns(fields, low, start):
    lane = iota(fields[0].shape, 1)
    packed = None
    for i, field in enumerate(fields, start):
        turn = (i * HALO + (0 if low else HALO)) % LANES
        turned = pltpu.roll(field, turn, 1) if turn else field
        packed = turned if packed is None else jnp.where(lane >= i * HALO, turned, packed)
    return packed


def packed_rows(fields, low):
    tall = fields[0].shape[0]
    span = slice(0, HALO) if low else slice(tall - HALO, tall)
    return jnp.concatenate([x[span] for x in fields], axis=0)


def remap_kernel(came, returns, edges, *rest):
    arrived, rest = rest[: len(came)], rest[len(came) :]
    ptr_hbm, hot_ref, edge_rows, edge_columns, w_ref, skin_ref, mask_ref = rest[:7]
    forcing_ref, own_ref = rest[7:9]
    message_refs = rest[9 : 9 + len(returns)]
    slots, mapped, shares, homebound, bank, ptr_ref, sem = rest[9 + len(returns) :]
    pointers = pltpu.make_async_copy(ptr_hbm, ptr_ref, sem)
    pointers.start()
    per_step = 8
    size = arrived[0].shape[0]
    for offset, block in zip(came, arrived):
        o = pick(offset)
        slots[pl.ds(pl.multiple_of(o * size, size), size), :] = block[...].astype(F32)
    slots[NEIGHBOR_TILES * size :, :] = jnp.zeros((8, LANES), F32)
    pointers.wait()
    sub = iota((per_step, LANES), 0)

    def forward(step):
        for j in range(per_step):
            k = step * per_step + j
            both = [slots[pl.ds(ptr_ref[w, k] * 4, 8), :] for w in range(2)]
            both = jnp.concatenate(both, axis=0).astype(BF16)
            product = dot_t(both, w_ref[k].reshape(2 * LANES, LANES))
            mapped[pl.ds(k * 8, 8), :] = product[:8, :LANES] + product[8:, LANES:]

    def middle(step):
        rows = pl.ds(step * per_step, per_step)
        u, v, p, h = (mapped[pl.ds(step * per_step * 8 + i, per_step, stride=8), :] for i in range(4))
        speed = jnp.sqrt(u * u + v * v + 1.0)
        forcing_ref[0, rows, :] = 0.2 * speed * u
        forcing_ref[1, rows, :] = 0.2 * speed * v
        forcing_ref[2, rows, :] = 0.5 * p
        return (skin_ref[rows, :] + 0.25 * mask_ref[rows, :].astype(F32) * h).astype(BF16).astype(F32)

    def back(step, sst):
        left = []
        for j in range(per_step):
            only = jnp.where(sub == j, sst, 0.0)
            zero = jnp.zeros_like(only)
            left.append(jnp.concatenate([only, zero], axis=0).astype(BF16))
            left.append(jnp.concatenate([zero, only], axis=0).astype(BF16))
        left = jnp.concatenate(left, axis=1)
        right = w_ref[pl.ds(step * per_step, per_step)].reshape(per_step * 2 * LANES, LANES)
        total = dot(left, right)
        for w in range(2):
            rows = slice((w * steps + step) * per_step, (w * steps + step + 1) * per_step)
            shares[rows, :] = total[w * per_step : (w + 1) * per_step]

    steps = w_ref.shape[0] // per_step
    for i in range(steps):
        forward(i)
    for i in range(steps):
        back(i, middle(i))

    every = shares[...]
    high = every.astype(BF16)
    low = (every - high.astype(F32)).astype(BF16)
    split = jnp.concatenate([high, low], axis=1)
    groups = own_ref.shape[0]
    value = dot(hot_ref[...], split)
    returned = (value[:, :LANES] + value[:, LANES:]).astype(BF16)
    homebound[...] = returned
    own_ref[...] = returned[MIDDLE * groups : (MIDDLE + 1) * groups]
    fields = [forcing_ref[0], forcing_ref[1], forcing_ref[2]]
    tall = fields[0].shape[0]
    rows = HALO * FIELDS
    still = HALO * (FIELDS - len(fields))
    lane = iota((tall, LANES), 1)
    for i, low in enumerate((False, True)):
        bank[i * rows : i * rows + still, :] = edge_rows[i]
        bank[i * rows + still : (i + 1) * rows, :] = packed_rows(fields, low).astype(BF16)
        columns = packed_columns(fields, low, FIELDS - len(fields))
        columns = jnp.where(lane < still, edge_columns[i].astype(F32), columns)
        bank[2 * rows + i * tall : 2 * rows + (i + 1) * tall, :] = columns.astype(BF16)
    bank[2 * rows + 2 * tall :, :] = jnp.zeros((rows, LANES), BF16)
    for offset, edge, out in zip(returns, edges, message_refs):
        first = pl.multiple_of(pick(offset) * groups, 16)
        out[0:groups, :] = homebound[pl.ds(first, groups), :]
        first = pl.multiple_of(pick(edge), 16)
        out[groups:, :] = bank[pl.ds(first, rows), :]


def finish_kernel(sources, halos, count_t, count_s, messages, *rest):
    message_refs, rest = rest[:messages], rest[messages:]
    own_ref, index_ref, code_ref = rest[:3]
    hot_refs, rest = rest[3 : 3 + NEIGHBOR_TILES], rest[3 + NEIGHBOR_TILES :]
    ocean_ref, depth_ref, mask_ref, forcing_ref, out_ref, warm_ref, inbox, shifted = rest
    t, s = lax.axis_index("tile"), lax.axis_index("sub")
    size = message_refs[0].shape[0]
    groups = own_ref.shape[0]
    for i, ref in enumerate(message_refs):
        inbox[i * size : (i + 1) * size, :] = ref[...]
    blocks = index_ref.shape[0]
    index = index_ref[...]
    code = code_ref[...]
    warm = jnp.zeros((blocks, LANES), F32)

    def warmth(o, warm):
        if o == MIDDLE:
            value = own_ref[...]
        else:
            value = inbox[pl.ds(pl.multiple_of(pick(sources[o]) * size, 16), groups), :]
        lines = dot(hot_refs[o][...], value)
        upper = jnp.bitwise_and(code, 8 << o) != 0
        lines = jnp.where(upper, lines[:blocks], lines[blocks:])
        picked = jnp.take_along_axis(lines, index, axis=1)
        return jnp.where(jnp.bitwise_and(code, 7) == o, picked, warm)

    tall = depth_ref.shape[0]
    full = tall + 2 * HALO

    def halo(dt, ds):
        ok = jnp.bool_(True)
        if dt == 1:
            ok &= t > 0
        if dt == -1:
            ok &= t < count_t - 1
        if ds == 1:
            ok &= s > 0
        if ds == -1:
            ok &= s < count_s - 1
        rows = tall if dt == 0 else (HALO if ds else HALO * FIELDS)
        first = pl.multiple_of(pick(halos[dt, ds]) * size + groups, 16)
        value = inbox[pl.ds(first, rows), :].astype(F32)
        return jnp.where(ok, value, 0.0)

    from_left = jnp.concatenate([halo(1, 1), halo(0, 1), halo(-1, 1)], axis=0)
    from_right = jnp.concatenate([halo(1, -1), halo(0, -1), halo(-1, -1)], axis=0)
    above, below = halo(1, 0), halo(-1, 0)
    lane = iota((full, LANES), 1)
    inner = [ocean_ref[0], ocean_ref[1], ocean_ref[2], mask_ref[...].astype(F32), depth_ref[...]]
    inner += [forcing_ref[0], forcing_ref[1], forcing_ref[2]]
    wide = []
    for i in range(FIELDS):
        rows = slice(i * HALO, (i + 1) * HALO)
        main = jnp.concatenate([above[rows], inner[i], below[rows]], axis=0)
        turn = (LANES - HALO - i * HALO) % LANES
        left = pltpu.roll(from_left, turn, 1) if turn else from_left
        turn = (LANES - i * HALO) % LANES
        right = pltpu.roll(from_right, turn, 1) if turn else from_right
        side = jnp.where(lane < HALO, right, jnp.where(lane >= LANES - HALO, left, 0.0))
        wide.append([main, side])
    eta, east, north, m, depth, stress_x, stress_y, fresh = wide
    row = iota((full, LANES), 0) + (t * tall - HALO)
    coriolis = 0.1 + 0.2 * (row.astype(F32) + 0.5) / (tall * count_t)

    both = range(2)
    half_m = [0.5 * m[i] for i in both]
    half_d = [half_m[i] * depth[i] for i in both]
    turning = [m[i] * coriolis for i in both]
    fresh = [m[i] * fresh[i] for i in both]
    stress_x = [m[i] * stress_x[i] for i in both]
    stress_y = [m[i] * stress_y[i] for i in both]
    shifted[:, 0:8, :] = jnp.zeros((4, 8, LANES), F32)
    shifted[:, 8 + full :, :] = jnp.zeros((4, 8, LANES), F32)

    def across(a):
        ahead = [pltpu.roll(a[i], LANES - 1, 1) for i in both]
        behind = [pltpu.roll(a[i], 1, 1) for i in both]
        columns = lane[: a[0].shape[0]]
        return [
            jnp.where(columns == LANES - 1, ahead[1 - i], ahead[i])
            - jnp.where(columns == 0, behind[1 - i], behind[i])
            for i in both
        ]

    def along(a, first, rows, place):
        result = []
        for i in both:
            shifted[place + i, 8 + first : 8 + first + a[i].shape[0], :] = a[i]
            result.append(
                shifted[place + i, 9 + rows.start : 9 + rows.stop, :]
                - shifted[place + i, 7 + rows.start : 7 + rows.stop, :]
            )
        return result

    first, last = 0, full
    out_east, out_north = across(east), along(north, 0, slice(0, full), 0)
    eta, east, north = ([m[i] * a[i] for i in both] for a in (eta, east, north))
    for step in range(1, SUBS + 1):
        if step > 1:
            out_east, out_north = across(east), along(north, first, slice(first, last), 0)
        eta = [eta[i] + fresh[i] - half_m[i] * (out_east[i] + out_north[i]) for i in both]
        below_first = 2 * step // 8 * 8
        slope_y = along(eta, first, slice(below_first, full - below_first), 2)
        if below_first > first:
            cut = slice(below_first - first, full - below_first - first)
            eta, east, north, turning, stress_x, stress_y, half_d, fresh, half_m = (
                [x[cut] for x in a]
                for a in (eta, east, north, turning, stress_x, stress_y, half_d, fresh, half_m)
            )
            first, last = below_first, full - below_first
        slope_x = across(eta)
        if step <= NEIGHBOR_TILES:
            warm = warmth(step - 1, warm)
        new_east = [
            east[i] + turning[i] * north[i] + stress_x[i] - half_d[i] * slope_x[i] for i in both
        ]
        north = [
            north[i] - turning[i] * east[i] + stress_y[i] - half_d[i] * slope_y[i] for i in both
        ]
        east = new_east
    warm_ref[...] = warm
    for i, a in enumerate((eta, east, north)):
        out_ref[i] = a[0][HALO - first : HALO - first + tall]


SCHEDULES = {
    (4, 2): (
        [
            [2, 3, 4, 1, 6, 7, 0, 5],
            [7, 2, 1, 5, 3, 6, 4, 0],
            [6, 7, 0, 4, 2, 3, 5, 1],
            [1, 0, 3, 2, 5, 4, 7, 6],
        ],
        [
            [3, 6, 5, 0, 7, 2, 1, 4],
            [2, 3, 4, 1, 6, 7, 0, 5],
            [7, 2, 1, 4, 3, 6, 5, 0],
            [6, 7, 0, 5, 2, 3, 4, 1],
            [1, 0, 3, 2, 5, 4, 7, 6],
        ],
    ),
}


def schedule(count_t, count_s):
    total = count_t * count_s
    if (count_t, count_s) in SCHEDULES:
        return SCHEDULES[count_t, count_s]
    rings = [
        [(i + distance) % total for i in range(total)]
        for distance in range(-MIDDLE, MIDDLE + 1)
        if distance
    ]
    others = []
    for dt in (-1, 1):
        for ds in (-1, 0, 1):
            if MIDDLE < abs(dt * count_s + ds):
                targets = [-1] * total
                for device in range(total):
                    t, s = device // count_s + dt, device % count_s + ds
                    if 0 <= t < count_t and 0 <= s < count_s:
                        targets[device] = t * count_s + s
                others.append(targets)
    return rings, rings + others


def plan(count_t, count_s, groups, tall):
    total = count_t * count_s
    outward, homeward = schedule(count_t, count_s)

    def offset(a, b):
        o = (b - a + MIDDLE) % total
        return o if o < NEIGHBOR_TILES else -1

    def step(a, b):
        dt, ds = b // count_s - a // count_s, b % count_s - a % count_s
        return (dt, ds) if abs(dt) <= 1 and abs(ds) <= 1 else None

    def senders(targets):
        return [targets.index(d) if d in targets else -1 for d in range(total)]

    rows = HALO * FIELDS
    start = {(1, 0): 0, (-1, 0): rows}
    for ds, first in ((1, 2 * rows), (-1, 2 * rows + tall)):
        start[0, ds] = start[-1, ds] = first
        start[1, ds] = first + tall - HALO
    result = {"outward": outward, "homeward": homeward}
    result["sent"] = [[offset(a, b) for a, b in enumerate(p)] for p in outward]
    result["sent"].insert(0, [MIDDLE] * total)
    result["came"] = [[offset(a, b) for b, a in enumerate(senders(p))] for p in outward]
    result["came"].insert(0, [MIDDLE] * total)
    result["returns"] = [
        [max(offset(b, a), 0) if b >= 0 else 0 for a, b in enumerate(p)] for p in homeward
    ]
    result["edges"] = [
        [start[step(a, b)] if b >= 0 and step(a, b) else 0 for a, b in enumerate(p)] for p in homeward
    ]
    sources = [[0] * total for _ in range(NEIGHBOR_TILES)]
    halos = {(dt, ds): [0] * total for dt in (-1, 0, 1) for ds in (-1, 0, 1)}
    for i, p in enumerate(homeward):
        for a, b in enumerate(p):
            if b >= 0:
                if offset(b, a) >= 0:
                    sources[offset(b, a)][b] = i
                if step(a, b):
                    halos[step(a, b)][b] = i
    result["sources"], result["halos"] = sources, halos
    return result


def shards(
    air_exchanges,
    air_destination,
    diagonal_group_pointer,
    interpolation_factors,
    marine_fields,
    skin_warmth_anomaly,
    gravity_bathymetry,
    marine_indicator,
):
    axes = ("tile", "sub")
    count_t, count_s = lax.axis_size("tile"), lax.axis_size("sub")
    total = count_t * count_s
    columns = air_destination.shape[1]
    blocks = columns // LANES
    groups = columns // 2 // LANES
    destination = air_destination.reshape(blocks, LANES)
    vmem = pl.BlockSpec(memory_space=pltpu.VMEM)
    params = pltpu.CompilerParams(vmem_limit_bytes=VMEM_LIMIT)
    hbm = pl.BlockSpec(memory_space=pltpu.HBM)
    pointers = diagonal_group_pointer[0, 0, 0].T
    to_stage = (
        pointers,
        interpolation_factors[0, 0, 0],
        marine_fields[0],
        skin_warmth_anomaly[0],
        gravity_bathymetry[0],
        marine_indicator[0],
    )
    tall = skin_warmth_anomaly.shape[1]
    moves = plan(count_t, count_s, groups, tall)
    sends = len(moves["sent"])
    results = pl.pallas_call(
        functools.partial(route_kernel, moves["sent"], total),
        out_shape=[jax.ShapeDtypeStruct((groups * 4, LANES), BF16)] * sends
        + [jax.ShapeDtypeStruct(a.shape, a.dtype) for a in (destination,) + to_stage],
        in_specs=[hbm] * (2 + len(to_stage)),
        out_specs=[vmem] * (sends + 1 + len(to_stage)),
        scratch_shapes=[
            pltpu.VMEM((8, columns), BF16),
            pltpu.VMEM((8, columns), BF16),
            pltpu.VMEM((NEIGHBOR_TILES * (groups + 1) * 8, LANES), F32),
            pltpu.VMEM((blocks, LANES), I32),
            pltpu.VMEM((32, blocks), I32),
            pltpu.SMEM((32, blocks), I32),
            pltpu.SemaphoreType.DMA((3 + len(to_stage),)),
        ],
        compiler_params=params,
        name="route",
    )(*(pltpu.with_memory_space_constraint(a, pltpu.HBM) for a in (air_exchanges[0], destination) + to_stage))
    destination, rows, weights, ocean, skin, depth, mask = results[sends:]

    def send(array, targets):
        return lax.ppermute(array, axes, [(a, b) for a, b in enumerate(targets) if b >= 0])

    arrived = [results[0]] + [send(a, p) for a, p in zip(results[1:], moves["outward"])]
    prepared = pl.pallas_call(
        functools.partial(prepare_kernel, total),
        out_shape=[
            jax.ShapeDtypeStruct((NEIGHBOR_TILES * groups, LANES), BF16),
            jax.ShapeDtypeStruct((2, HALO * (FIELDS - 3), LANES), BF16),
            jax.ShapeDtypeStruct((2, tall, LANES), BF16),
        ]
        + [jax.ShapeDtypeStruct((blocks, LANES), I32)] * 2
        + [jax.ShapeDtypeStruct((2 * blocks, groups), BF16)] * NEIGHBOR_TILES,
        in_specs=[vmem] * 5,
        out_specs=[vmem] * (5 + NEIGHBOR_TILES),
        compiler_params=params,
        cost_estimate=pl.CostEstimate(flops=2 * 15 * LANES**3, bytes_accessed=2**19, transcendentals=0),
        name="prepare",
    )(destination, rows, ocean, depth, mask)
    returns = len(moves["returns"])
    message = (groups + HALO * FIELDS, LANES)
    row_blocks = weights.shape[0]
    outs = pl.pallas_call(
        functools.partial(remap_kernel, moves["came"], moves["returns"], moves["edges"]),
        out_shape=[
            jax.ShapeDtypeStruct((3, tall, LANES), F32),
            jax.ShapeDtypeStruct((groups, LANES), BF16),
        ]
        + [jax.ShapeDtypeStruct(message, BF16)] * returns,
        in_specs=[vmem] * sends + [hbm] + [vmem] * 6,
        out_specs=[vmem] * (2 + returns),
        scratch_shapes=[
            pltpu.VMEM((NEIGHBOR_TILES * groups * 4 + 8, LANES), F32),
            pltpu.VMEM((row_blocks * 8, LANES), F32),
            pltpu.VMEM((2 * row_blocks, LANES), F32),
            pltpu.VMEM((NEIGHBOR_TILES * groups, LANES), BF16),
            pltpu.VMEM((3 * HALO * FIELDS + 2 * tall, LANES), BF16),
            pltpu.SMEM(pointers.shape, I32),
            pltpu.SemaphoreType.DMA,
        ],
        compiler_params=params,
        name="remap",
    )(*arrived, pltpu.with_memory_space_constraint(pointers, pltpu.HBM), *prepared[:3], weights, skin, mask)
    forcing, own = outs[:2]
    received = [send(a, p) for a, p in zip(outs[2:], moves["homeward"])]
    ocean_out, warm = pl.pallas_call(
        functools.partial(
            finish_kernel, moves["sources"], moves["halos"], count_t, count_s, returns
        ),
        out_shape=[
            jax.ShapeDtypeStruct((3, tall, LANES), F32),
            jax.ShapeDtypeStruct((blocks, LANES), F32),
        ],
        in_specs=[vmem] * (returns + 3 + NEIGHBOR_TILES + 4),
        out_specs=[vmem] * 2,
        scratch_shapes=[
            pltpu.VMEM((returns * message[0], LANES), BF16),
            pltpu.VMEM((4, tall + 2 * HALO + 16, LANES), F32),
        ],
        compiler_params=params,
        name="finish",
    )(*received, own, *prepared[3:], ocean, depth, mask, forcing)
    return ocean_out[None], warm.reshape(1, columns)


def solution(mesh):
    return jax.shard_map(
        shards,
        mesh=mesh,
        in_specs=(
            P(("member", "comp"), None, ("tile", "sub")),
            P("comp", ("tile", "sub"), None),
            P("comp", "tile", "sub", None, None),
            P("comp", "tile", "sub", None, None, None, None),
            P(("member", "comp"), None, "tile", "sub"),
            P(("member", "comp"), "tile", "sub"),
            P("comp", "tile", "sub"),
            P("comp", "tile", "sub"),
        ),
        out_specs=(
            P(("member", "comp"), None, "tile", "sub"),
            P(("member", "comp"), ("tile", "sub")),
        ),
        check_vma=False,
    )
```

```python
import functools

import jax
import jax.numpy as jnp
from jax import lax
from jax.experimental import pallas as pl
from jax.experimental.pallas import tpu as pltpu
from jax.sharding import PartitionSpec as P

NEIGHBOR_TILES = 5
MIDDLE = NEIGHBOR_TILES // 2
SUBS = 8
LANES = 128
HALO = 2 * SUBS
FIELDS = 8
F32 = jnp.float32
BF16 = jnp.bfloat16
I32 = jnp.int32
SORT_UNIT = 16
VMEM_LIMIT = 48 * 1024 * 1024


def iota(shape, dim):
    return lax.broadcasted_iota(I32, shape, dim)


def dot(a, b):
    return jnp.dot(a, b, preferred_element_type=F32)


def dot_t(a, b):
    return lax.dot_general(a, b, (((1,), (1,)), ((), ())), preferred_element_type=F32)


def position():
    return lax.axis_index("tile") * lax.axis_size("sub") + lax.axis_index("sub")


def pick(values):
    usual = max(sorted(set(values)), key=values.count)
    mine = position()
    result = jnp.int32(usual)
    for device, value in enumerate(values):
        if value != usual:
            result = jnp.where(mine == device, value, result)
    return result


def ones_where(mask):
    return jnp.where(mask, 1.0, 0.0).astype(BF16)


def offsets_of(destination, total):
    shifted = destination - position() + MIDDLE
    shifted = jnp.where(shifted < 0, shifted + total, shifted)
    return jnp.where(shifted >= total, shifted - total, shifted)


def ranks(offsets):
    rows = offsets.shape[0]
    r, c = iota((LANES, LANES), 0), iota((LANES, LANES), 1)
    before = ones_where(r < c)
    every = jnp.ones((LANES, LANES), BF16)
    earlier = ones_where(iota((rows, rows), 1) < iota((rows, rows), 0))
    result = []
    for o in range(NEIGHBOR_TILES):
        mask = offsets == o
        hot = ones_where(mask)
        inside = dot(hot, before)
        count = dot(hot, every)
        base = dot(earlier, count.astype(BF16))
        result.append((mask, hot, inside, count, base))
    return result


def route_kernel(sent, total, x_hbm, dest_hbm, *rest):
    staged = len(rest) - len(sent) - 8
    sources, rest = rest[: staged // 2], rest[staged // 2 :]
    outs, dest_ref, rest = rest[: len(sent)], rest[len(sent)], rest[len(sent) + 1 :]
    targets, rest = rest[: staged // 2], rest[staged // 2 :]
    x_ref, comb, place, pos_scr, vec, scal, sem = rest
    copies = [
        pltpu.make_async_copy(a, b, sem.at[i])
        for i, (a, b) in enumerate(
            zip((dest_hbm, x_hbm) + tuple(sources), (dest_ref, x_ref) + tuple(targets))
        )
    ]
    for copy in copies:
        copy.start()
    copies[0].wait()
    blocks = dest_ref.shape[0]
    unit = SORT_UNIT
    groups = outs[0].shape[0] // 4
    stride = (groups + 1) * 8
    offsets = offsets_of(dest_ref[...], total)
    ones8 = jnp.ones((8, LANES), BF16)
    sub8 = iota((8, blocks), 0)
    earlier = ones_where(iota((blocks, blocks), 0) < iota((blocks, blocks), 1))
    before = ones_where(iota((LANES, 2 * LANES), 0) < iota((LANES, 2 * LANES), 1))
    hots = [ones_where(offsets == o) for o in range(NEIGHBOR_TILES)]
    counts = jnp.zeros((8, blocks), F32)
    start_t = jnp.zeros((8, blocks), F32)
    starts = jnp.zeros((8, blocks), F32)
    for o, hot in enumerate(hots):
        count_t = dot_t(ones8, hot)
        counts = jnp.where(sub8 == o, count_t, counts)
        starts = jnp.where(sub8 == o, start_t, starts)
        start_t = start_t + count_t
    base = dot(counts.astype(BF16), earlier).astype(I32)
    counts, starts = counts.astype(I32), starts.astype(I32)
    at = jnp.bitwise_and(base, LANES - 1)
    vec[0:8, :] = sub8 * stride + lax.shift_right_logical(base, 7) * 8
    vec[8:16, :] = jnp.bitwise_and(at - starts, LANES - 1)
    vec[16:24, :] = at
    vec[24:32, :] = at + counts - LANES
    copy = pltpu.make_async_copy(vec, scal, sem.at[len(copies)])
    copy.start()
    start = jnp.zeros((blocks, LANES), F32)
    pos = jnp.zeros((blocks, LANES), F32)
    for o, hot in enumerate(hots):
        inside = dot(hot, before)
        pos = jnp.where(offsets == o, start + inside[:, :LANES], pos)
        start = start + inside[:, LANES:]
    pos_scr[...] = pos.astype(I32)
    f, g = iota((8, 8), 1), jnp.bitwise_and(iota((8, 8), 0), 3)
    plus = ((g == 0) & (f == 0)) | ((g == 1) & (f == 1)) | ((g == 2) & (f == 3)) | ((g == 3) & (f >= 6))
    minus = ((g == 2) & (f == 2)) | ((g == 3) & ((f == 4) | (f == 5)))
    combine = (jnp.where(plus, 1.0, 0.0) - jnp.where(minus, 1.0, 0.0)).astype(BF16)
    copies[1].wait()
    comb[...] = dot(combine, x_ref[...]).astype(BF16)

    lines = iota((LANES, LANES), 0)

    def sort_blocks(i):
        result = []
        for u in range(0, unit, 2):
            b = i * unit + u
            columns = comb[:, pl.ds(pl.multiple_of(b * LANES, 2 * LANES), 2 * LANES)].astype(F32)
            columns = jnp.concatenate([columns[:, :LANES], columns[:, LANES:]], axis=0).astype(BF16)
            hot = [ones_where(pos_scr[pl.ds(b + v, 1), :] == lines) for v in range(2)]
            both = dot_t(columns, jnp.concatenate(hot, axis=0))
            result += [both[:8, :LANES], both[8:, LANES:]]
        return result

    lane = iota((8, LANES), 1)

    def place_blocks(i, values, current):
        current = list(current)
        for u in range(unit):
            b = i * unit + u
            for o in range(NEIGHBOR_TILES):
                turned = pltpu.roll(values[u], scal[8 + o, b], 1)
                merged = jnp.where(lane < scal[16 + o, b], current[o], turned)
                place[pl.ds(pl.multiple_of(scal[o, b], 8), 8), :] = merged
                current[o] = jnp.where(lane < scal[24 + o, b], turned, merged)
        return current

    def step(i, carry):
        values = sort_blocks(i + 1)
        return tuple(place_blocks(i, carry[NEIGHBOR_TILES:], carry[:NEIGHBOR_TILES])) + tuple(values)

    steps = blocks // unit
    current = [jnp.zeros((8, LANES), F32) for _ in range(NEIGHBOR_TILES)]
    values = sort_blocks(0)
    copy.wait()
    carry = lax.fori_loop(0, steps - 1, step, tuple(current) + tuple(values))
    current = place_blocks(steps - 1, carry[NEIGHBOR_TILES:], carry[:NEIGHBOR_TILES])
    pair_lane = jnp.where(iota((8, LANES), 0) < 4, lane, lane + LANES)
    upper = iota((groups // 2, 8, LANES), 1) < 4
    slot = iota((groups // 2, 8, LANES), 0) * (2 * LANES) + pair_lane[None]
    last = blocks - 1

    def length(o):
        return (scal[o, last] - o * stride) * (LANES // 8) + scal[24 + o, last] + LANES

    for o in range(NEIGHBOR_TILES):
        full = lax.shift_right_logical(length(o), 7) * 8 + o * stride
        place[pl.ds(pl.multiple_of(full, 8), 8), :] = current[o]
    for offset, out in zip(sent, outs):
        o = pick(offset)
        tiles = place[pl.ds(pl.multiple_of(o * stride, 8), groups * 8), :]
        tiles = tiles.reshape(groups // 2, 2, 8, LANES)
        both = jnp.where(upper, tiles[:, 0], tiles[:, 1])
        both = jnp.where(slot < length(o), both, 0.0)
        out[...] = both.reshape(groups * 4, LANES).astype(BF16)
    for copy in copies[2:]:
        copy.wait()


def prepare_kernel(
    total, dest_ref, row_ref, ocean_ref, depth_ref, mask_ref,
    blocks_ref, edge_rows, edge_columns, index_ref, code_ref, *hot_refs
):
    blocks = dest_ref.shape[0]
    groups = hot_refs[0].shape[1]
    offsets = offsets_of(dest_ref[...], total)
    index = jnp.zeros((blocks, LANES), I32)
    code = jnp.zeros((blocks, LANES), I32)
    group_id = iota((blocks, groups), 1)
    lane = iota((blocks, LANES), 1)
    for o, (mask, hot, inside, count, base) in enumerate(ranks(offsets)):
        base = base.astype(I32)
        rank = base + inside.astype(I32)
        first = lax.shift_right_logical(base, 7)
        index = jnp.where(mask, jnp.bitwise_and(rank, LANES - 1), index)
        code = jnp.where(mask, code + o, code)
        code = jnp.where(lane >= jnp.bitwise_and(base, LANES - 1), code + (8 << o), code)
        hot_refs[o][0:blocks, :] = ones_where(group_id == first[:, :groups])
        hot_refs[o][blocks:, :] = ones_where(group_id == first[:, :groups] + 1)
    index_ref[...] = index
    code_ref[...] = code
    row = jnp.concatenate([row_ref[0:1, :], row_ref[1:2, :]], axis=1)
    blocks_ref[...] = ones_where(iota(blocks_ref.shape, 0) == row)
    fields = [ocean_ref[0], ocean_ref[1], ocean_ref[2], mask_ref[...].astype(F32), depth_ref[...]]
    for i, low in enumerate((False, True)):
        edge_rows[i] = packed_rows(fields, low).astype(BF16)
        edge_columns[i] = packed_columns(fields, low, 0).astype(BF16)


def packed_columns(fields, low, start):
    lane = iota(fields[0].shape, 1)
    packed = None
    for i, field in enumerate(fields, start):
        turn = (i * HALO + (0 if low else HALO)) % LANES
        turned = pltpu.roll(field, turn, 1) if turn else field
        packed = turned if packed is None else jnp.where(lane >= i * HALO, turned, packed)
    return packed


def packed_rows(fields, low):
    tall = fields[0].shape[0]
    span = slice(0, HALO) if low else slice(tall - HALO, tall)
    return jnp.concatenate([x[span] for x in fields], axis=0)


def remap_kernel(came, returns, edges, *rest):
    arrived, rest = rest[: len(came)], rest[len(came) :]
    ptr_vmem, hot_ref, edge_rows, edge_columns, w_ref, skin_ref, mask_ref = rest[:7]
    forcing_ref, own_ref = rest[7:9]
    message_refs = rest[9 : 9 + len(returns)]
    slots, mapped, shares, homebound, bank, ptr_ref, sem = rest[9 + len(returns) :]
    pointers = pltpu.make_async_copy(ptr_vmem, ptr_ref, sem)
    pointers.start()
    per_step = 8
    size = arrived[0].shape[0]
    for offset, block in zip(came, arrived):
        o = pick(offset)
        slots[pl.ds(pl.multiple_of(o * size, size), size), :] = block[...].astype(F32)
    slots[NEIGHBOR_TILES * size :, :] = jnp.zeros((8, LANES), F32)
    pointers.wait()
    sub = iota((per_step, LANES), 0)

    def forward(step):
        for j in range(per_step):
            k = step * per_step + j
            both = [slots[pl.ds(ptr_ref[w, k] * 4, 8), :] for w in range(2)]
            both = jnp.concatenate(both, axis=0).astype(BF16)
            product = dot_t(both, w_ref[k].reshape(2 * LANES, LANES))
            mapped[pl.ds(k * 8, 8), :] = product[:8, :LANES] + product[8:, LANES:]

    def middle(step):
        rows = pl.ds(step * per_step, per_step)
        u, v, p, h = (mapped[pl.ds(step * per_step * 8 + i, per_step, stride=8), :] for i in range(4))
        speed = jnp.sqrt(u * u + v * v + 1.0)
        forcing_ref[0, rows, :] = 0.2 * speed * u
        forcing_ref[1, rows, :] = 0.2 * speed * v
        forcing_ref[2, rows, :] = 0.5 * p
        return (skin_ref[rows, :] + 0.25 * mask_ref[rows, :].astype(F32) * h).astype(BF16).astype(F32)

    def back(step, sst):
        left = []
        for j in range(per_step):
            only = jnp.where(sub == j, sst, 0.0)
            zero = jnp.zeros_like(only)
            left.append(jnp.concatenate([only, zero], axis=0).astype(BF16))
            left.append(jnp.concatenate([zero, only], axis=0).astype(BF16))
        left = jnp.concatenate(left, axis=1)
        right = w_ref[pl.ds(step * per_step, per_step)].reshape(per_step * 2 * LANES, LANES)
        total = dot(left, right)
        for w in range(2):
            rows = slice((w * steps + step) * per_step, (w * steps + step + 1) * per_step)
            shares[rows, :] = total[w * per_step : (w + 1) * per_step]

    steps = w_ref.shape[0] // per_step
    for i in range(steps):
        forward(i)
    for i in range(steps):
        back(i, middle(i))

    every = shares[...]
    high = every.astype(BF16)
    low = (every - high.astype(F32)).astype(BF16)
    split = jnp.concatenate([high, low], axis=1)
    groups = own_ref.shape[0]
    value = dot(hot_ref[...], split)
    returned = (value[:, :LANES] + value[:, LANES:]).astype(BF16)
    homebound[...] = returned
    own_ref[...] = returned[MIDDLE * groups : (MIDDLE + 1) * groups]
    fields = [forcing_ref[0], forcing_ref[1], forcing_ref[2]]
    tall = fields[0].shape[0]
    rows = HALO * FIELDS
    still = HALO * (FIELDS - len(fields))
    lane = iota((tall, LANES), 1)
    for i, low in enumerate((False, True)):
        bank[i * rows : i * rows + still, :] = edge_rows[i]
        bank[i * rows + still : (i + 1) * rows, :] = packed_rows(fields, low).astype(BF16)
        columns = packed_columns(fields, low, FIELDS - len(fields))
        columns = jnp.where(lane < still, edge_columns[i].astype(F32), columns)
        bank[2 * rows + i * tall : 2 * rows + (i + 1) * tall, :] = columns.astype(BF16)
    bank[2 * rows + 2 * tall :, :] = jnp.zeros((rows, LANES), BF16)
    for offset, edge, out in zip(returns, edges, message_refs):
        first = pl.multiple_of(pick(offset) * groups, 16)
        out[0:groups, :] = homebound[pl.ds(first, groups), :]
        first = pl.multiple_of(pick(edge), 16)
        out[groups:, :] = bank[pl.ds(first, rows), :]


def finish_kernel(sources, halos, count_t, count_s, messages, *rest):
    message_refs, rest = rest[:messages], rest[messages:]
    own_ref, index_ref, code_ref = rest[:3]
    hot_refs, rest = rest[3 : 3 + NEIGHBOR_TILES], rest[3 + NEIGHBOR_TILES :]
    ocean_ref, depth_ref, mask_ref, forcing_ref, out_ref, warm_ref, inbox, shifted = rest
    t, s = lax.axis_index("tile"), lax.axis_index("sub")
    size = message_refs[0].shape[0]
    groups = own_ref.shape[0]
    for i, ref in enumerate(message_refs):
        inbox[i * size : (i + 1) * size, :] = ref[...]
    blocks = index_ref.shape[0]
    index = index_ref[...]
    code = code_ref[...]
    warm = jnp.zeros((blocks, LANES), F32)

    def warmth(o, warm):
        if o == MIDDLE:
            value = own_ref[...]
        else:
            value = inbox[pl.ds(pl.multiple_of(pick(sources[o]) * size, 16), groups), :]
        lines = dot(hot_refs[o][...], value)
        upper = jnp.bitwise_and(code, 8 << o) != 0
        lines = jnp.where(upper, lines[:blocks], lines[blocks:])
        picked = jnp.take_along_axis(lines, index, axis=1)
        return jnp.where(jnp.bitwise_and(code, 7) == o, picked, warm)

    tall = depth_ref.shape[0]
    full = tall + 2 * HALO

    def halo(dt, ds):
        ok = jnp.bool_(True)
        if dt == 1:
            ok &= t > 0
        if dt == -1:
            ok &= t < count_t - 1
        if ds == 1:
            ok &= s > 0
        if ds == -1:
            ok &= s < count_s - 1
        rows = tall if dt == 0 else (HALO if ds else HALO * FIELDS)
        first = pl.multiple_of(pick(halos[dt, ds]) * size + groups, 16)
        value = inbox[pl.ds(first, rows), :].astype(F32)
        return jnp.where(ok, value, 0.0)

    from_left = jnp.concatenate([halo(1, 1), halo(0, 1), halo(-1, 1)], axis=0)
    from_right = jnp.concatenate([halo(1, -1), halo(0, -1), halo(-1, -1)], axis=0)
    above, below = halo(1, 0), halo(-1, 0)
    lane = iota((full, LANES), 1)
    inner = [ocean_ref[0], ocean_ref[1], ocean_ref[2], mask_ref[...].astype(F32), depth_ref[...]]
    inner += [forcing_ref[0], forcing_ref[1], forcing_ref[2]]
    wide = []
    for i in range(FIELDS):
        rows = slice(i * HALO, (i + 1) * HALO)
        main = jnp.concatenate([above[rows], inner[i], below[rows]], axis=0)
        turn = (LANES - HALO - i * HALO) % LANES
        left = pltpu.roll(from_left, turn, 1) if turn else from_left
        turn = (LANES - i * HALO) % LANES
        right = pltpu.roll(from_right, turn, 1) if turn else from_right
        side = jnp.where(lane < HALO, right, jnp.where(lane >= LANES - HALO, left, 0.0))
        wide.append([main, side])
    eta, east, north, m, depth, stress_x, stress_y, fresh = wide
    row = iota((full, LANES), 0) + (t * tall - HALO)
    coriolis = 0.1 + 0.2 * (row.astype(F32) + 0.5) / (tall * count_t)

    both = range(2)
    half_m = [0.5 * m[i] for i in both]
    half_d = [half_m[i] * depth[i] for i in both]
    turning = [m[i] * coriolis for i in both]
    fresh = [m[i] * fresh[i] for i in both]
    stress_x = [m[i] * stress_x[i] for i in both]
    stress_y = [m[i] * stress_y[i] for i in both]
    shifted[:, 0:8, :] = jnp.zeros((4, 8, LANES), F32)
    shifted[:, 8 + full :, :] = jnp.zeros((4, 8, LANES), F32)

    def across(a):
        ahead = [pltpu.roll(a[i], LANES - 1, 1) for i in both]
        behind = [pltpu.roll(a[i], 1, 1) for i in both]
        columns = lane[: a[0].shape[0]]
        return [
            jnp.where(columns == LANES - 1, ahead[1 - i], ahead[i])
            - jnp.where(columns == 0, behind[1 - i], behind[i])
            for i in both
        ]

    def along(a, first, rows, place):
        result = []
        for i in both:
            shifted[place + i, 8 + first : 8 + first + a[i].shape[0], :] = a[i]
            result.append(
                shifted[place + i, 9 + rows.start : 9 + rows.stop, :]
                - shifted[place + i, 7 + rows.start : 7 + rows.stop, :]
            )
        return result

    first, last = 0, full
    out_east, out_north = across(east), along(north, 0, slice(0, full), 0)
    eta, east, north = ([m[i] * a[i] for i in both] for a in (eta, east, north))
    for step in range(1, SUBS + 1):
        if step > 1:
            out_east, out_north = across(east), along(north, first, slice(first, last), 0)
        eta = [eta[i] + fresh[i] - half_m[i] * (out_east[i] + out_north[i]) for i in both]
        below_first = 2 * step // 8 * 8
        slope_y = along(eta, first, slice(below_first, full - below_first), 2)
        if below_first > first:
            cut = slice(below_first - first, full - below_first - first)
            eta, east, north, turning, stress_x, stress_y, half_d, fresh, half_m = (
                [x[cut] for x in a]
                for a in (eta, east, north, turning, stress_x, stress_y, half_d, fresh, half_m)
            )
            first, last = below_first, full - below_first
        slope_x = across(eta)
        if step <= NEIGHBOR_TILES:
            warm = warmth(step - 1, warm)
        new_east = [
            east[i] + turning[i] * north[i] + stress_x[i] - half_d[i] * slope_x[i] for i in both
        ]
        north = [
            north[i] - turning[i] * east[i] + stress_y[i] - half_d[i] * slope_y[i] for i in both
        ]
        east = new_east
    warm_ref[...] = warm
    for i, a in enumerate((eta, east, north)):
        out_ref[i] = a[0][HALO - first : HALO - first + tall]


SCHEDULES = {
    (4, 2): (
        [
            [2, 3, 4, 1, 6, 7, 0, 5],
            [7, 2, 1, 5, 3, 6, 4, 0],
            [6, 7, 0, 4, 2, 3, 5, 1],
            [1, 0, 3, 2, 5, 4, 7, 6],
        ],
        [
            [3, 6, 5, 0, 7, 2, 1, 4],
            [2, 3, 4, 1, 6, 7, 0, 5],
            [7, 2, 1, 4, 3, 6, 5, 0],
            [6, 7, 0, 5, 2, 3, 4, 1],
            [1, 0, 3, 2, 5, 4, 7, 6],
        ],
    ),
}


def schedule(count_t, count_s):
    total = count_t * count_s
    if (count_t, count_s) in SCHEDULES:
        return SCHEDULES[count_t, count_s]
    rings = [
        [(i + distance) % total for i in range(total)]
        for distance in range(-MIDDLE, MIDDLE + 1)
        if distance
    ]
    others = []
    for dt in (-1, 1):
        for ds in (-1, 0, 1):
            if MIDDLE < abs(dt * count_s + ds):
                targets = [-1] * total
                for device in range(total):
                    t, s = device // count_s + dt, device % count_s + ds
                    if 0 <= t < count_t and 0 <= s < count_s:
                        targets[device] = t * count_s + s
                others.append(targets)
    return rings, rings + others


def plan(count_t, count_s, groups, tall):
    total = count_t * count_s
    outward, homeward = schedule(count_t, count_s)

    def offset(a, b):
        o = (b - a + MIDDLE) % total
        return o if o < NEIGHBOR_TILES else -1

    def step(a, b):
        dt, ds = b // count_s - a // count_s, b % count_s - a % count_s
        return (dt, ds) if abs(dt) <= 1 and abs(ds) <= 1 else None

    def senders(targets):
        return [targets.index(d) if d in targets else -1 for d in range(total)]

    rows = HALO * FIELDS
    start = {(1, 0): 0, (-1, 0): rows}
    for ds, first in ((1, 2 * rows), (-1, 2 * rows + tall)):
        start[0, ds] = start[-1, ds] = first
        start[1, ds] = first + tall - HALO
    result = {"outward": outward, "homeward": homeward}
    result["sent"] = [[offset(a, b) for a, b in enumerate(p)] for p in outward]
    result["sent"].insert(0, [MIDDLE] * total)
    result["came"] = [[offset(a, b) for b, a in enumerate(senders(p))] for p in outward]
    result["came"].insert(0, [MIDDLE] * total)
    result["returns"] = [
        [max(offset(b, a), 0) if b >= 0 else 0 for a, b in enumerate(p)] for p in homeward
    ]
    result["edges"] = [
        [start[step(a, b)] if b >= 0 and step(a, b) else 0 for a, b in enumerate(p)] for p in homeward
    ]
    sources = [[0] * total for _ in range(NEIGHBOR_TILES)]
    halos = {(dt, ds): [0] * total for dt in (-1, 0, 1) for ds in (-1, 0, 1)}
    for i, p in enumerate(homeward):
        for a, b in enumerate(p):
            if b >= 0:
                if offset(b, a) >= 0:
                    sources[offset(b, a)][b] = i
                if step(a, b):
                    halos[step(a, b)][b] = i
    result["sources"], result["halos"] = sources, halos
    return result


def shards(
    air_exchanges,
    air_destination,
    diagonal_group_pointer,
    interpolation_factors,
    marine_fields,
    skin_warmth_anomaly,
    gravity_bathymetry,
    marine_indicator,
):
    axes = ("tile", "sub")
    count_t, count_s = lax.axis_size("tile"), lax.axis_size("sub")
    total = count_t * count_s
    columns = air_destination.shape[1]
    blocks = columns // LANES
    groups = columns // 2 // LANES
    destination = air_destination.reshape(blocks, LANES)
    vmem = pl.BlockSpec(memory_space=pltpu.VMEM)
    params = pltpu.CompilerParams(vmem_limit_bytes=VMEM_LIMIT)
    hbm = pl.BlockSpec(memory_space=pltpu.HBM)
    pointers = diagonal_group_pointer[0, 0, 0].T
    to_stage = (
        pointers,
        interpolation_factors[0, 0, 0],
        marine_fields[0],
        skin_warmth_anomaly[0],
        gravity_bathymetry[0],
        marine_indicator[0],
    )
    tall = skin_warmth_anomaly.shape[1]
    moves = plan(count_t, count_s, groups, tall)
    sends = len(moves["sent"])
    results = pl.pallas_call(
        functools.partial(route_kernel, moves["sent"], total),
        out_shape=[jax.ShapeDtypeStruct((groups * 4, LANES), BF16)] * sends
        + [jax.ShapeDtypeStruct(a.shape, a.dtype) for a in (destination,) + to_stage],
        in_specs=[hbm] * (2 + len(to_stage)),
        out_specs=[vmem] * (sends + 1 + len(to_stage)),
        scratch_shapes=[
            pltpu.VMEM((8, columns), BF16),
            pltpu.VMEM((8, columns), BF16),
            pltpu.VMEM((NEIGHBOR_TILES * (groups + 1) * 8, LANES), F32),
            pltpu.VMEM((blocks, LANES), I32),
            pltpu.VMEM((32, blocks), I32),
            pltpu.SMEM((32, blocks), I32),
            pltpu.SemaphoreType.DMA((3 + len(to_stage),)),
        ],
        compiler_params=params,
        name="route",
    )(*(pltpu.with_memory_space_constraint(a, pltpu.HBM) for a in (air_exchanges[0], destination) + to_stage))
    destination, rows, weights, ocean, skin, depth, mask = results[sends:]

    def send(array, targets):
        return lax.ppermute(array, axes, [(a, b) for a, b in enumerate(targets) if b >= 0])

    arrived = [results[0]] + [send(a, p) for a, p in zip(results[1:], moves["outward"])]
    prepared = pl.pallas_call(
        functools.partial(prepare_kernel, total),
        out_shape=[
            jax.ShapeDtypeStruct((NEIGHBOR_TILES * groups, LANES), BF16),
            jax.ShapeDtypeStruct((2, HALO * (FIELDS - 3), LANES), BF16),
            jax.ShapeDtypeStruct((2, tall, LANES), BF16),
        ]
        + [jax.ShapeDtypeStruct((blocks, LANES), I32)] * 2
        + [jax.ShapeDtypeStruct((2 * blocks, groups), BF16)] * NEIGHBOR_TILES,
        in_specs=[vmem] * 5,
        out_specs=[vmem] * (5 + NEIGHBOR_TILES),
        compiler_params=params,
        cost_estimate=pl.CostEstimate(flops=2 * 15 * LANES**3, bytes_accessed=2**19, transcendentals=0),
        name="prepare",
    )(destination, rows, ocean, depth, mask)
    returns = len(moves["returns"])
    message = (groups + HALO * FIELDS, LANES)
    row_blocks = weights.shape[0]
    outs = pl.pallas_call(
        functools.partial(remap_kernel, moves["came"], moves["returns"], moves["edges"]),
        out_shape=[
            jax.ShapeDtypeStruct((3, tall, LANES), F32),
            jax.ShapeDtypeStruct((groups, LANES), BF16),
        ]
        + [jax.ShapeDtypeStruct(message, BF16)] * returns,
        in_specs=[vmem] * (sends + 7),
        out_specs=[vmem] * (2 + returns),
        scratch_shapes=[
            pltpu.VMEM((NEIGHBOR_TILES * groups * 4 + 8, LANES), F32),
            pltpu.VMEM((row_blocks * 8, LANES), F32),
            pltpu.VMEM((2 * row_blocks, LANES), F32),
            pltpu.VMEM((NEIGHBOR_TILES * groups, LANES), BF16),
            pltpu.VMEM((3 * HALO * FIELDS + 2 * tall, LANES), BF16),
            pltpu.SMEM(pointers.shape, I32),
            pltpu.SemaphoreType.DMA,
        ],
        compiler_params=params,
        name="remap",
    )(*arrived, rows, *prepared[:3], weights, skin, mask)
    forcing, own = outs[:2]
    received = [send(a, p) for a, p in zip(outs[2:], moves["homeward"])]
    ocean_out, warm = pl.pallas_call(
        functools.partial(
            finish_kernel, moves["sources"], moves["halos"], count_t, count_s, returns
        ),
        out_shape=[
            jax.ShapeDtypeStruct((3, tall, LANES), F32),
            jax.ShapeDtypeStruct((blocks, LANES), F32),
        ],
        in_specs=[vmem] * (returns + 3 + NEIGHBOR_TILES + 4),
        out_specs=[vmem] * 2,
        scratch_shapes=[
            pltpu.VMEM((returns * message[0], LANES), BF16),
            pltpu.VMEM((4, tall + 2 * HALO + 16, LANES), F32),
        ],
        compiler_params=params,
        name="finish",
    )(*received, own, *prepared[3:], ocean, depth, mask, forcing)
    return ocean_out[None], warm.reshape(1, columns)


def solution(mesh):
    return jax.shard_map(
        shards,
        mesh=mesh,
        in_specs=(
            P(("member", "comp"), None, ("tile", "sub")),
            P("comp", ("tile", "sub"), None),
            P("comp", "tile", "sub", None, None),
            P("comp", "tile", "sub", None, None, None, None),
            P(("member", "comp"), None, "tile", "sub"),
            P(("member", "comp"), "tile", "sub"),
            P("comp", "tile", "sub"),
            P("comp", "tile", "sub"),
        ),
        out_specs=(
            P(("member", "comp"), None, "tile", "sub"),
            P(("member", "comp"), ("tile", "sub")),
        ),
        check_vma=False,
    )
```

```python
import functools

import jax
import jax.numpy as jnp
from jax import lax
from jax.experimental import pallas as pl
from jax.experimental.pallas import tpu as pltpu
from jax.sharding import PartitionSpec as P

NEIGHBOR_TILES = 5
MIDDLE = NEIGHBOR_TILES // 2
SUBS = 8
LANES = 128
HALO = 2 * SUBS
FIELDS = 8
F32 = jnp.float32
BF16 = jnp.bfloat16
I32 = jnp.int32
SORT_UNIT = 16
VMEM_LIMIT = 48 * 1024 * 1024


def iota(shape, dim):
    return lax.broadcasted_iota(I32, shape, dim)


def dot(a, b):
    return jnp.dot(a, b, preferred_element_type=F32)


def dot_t(a, b):
    return lax.dot_general(a, b, (((1,), (1,)), ((), ())), preferred_element_type=F32)


def position():
    return lax.axis_index("tile") * lax.axis_size("sub") + lax.axis_index("sub")


def pick(values):
    usual = max(sorted(set(values)), key=values.count)
    mine = position()
    result = jnp.int32(usual)
    for device, value in enumerate(values):
        if value != usual:
            result = jnp.where(mine == device, value, result)
    return result


def ones_where(mask):
    return jnp.where(mask, 1.0, 0.0).astype(BF16)


def offsets_of(destination, total):
    shifted = destination - position() + MIDDLE
    shifted = jnp.where(shifted < 0, shifted + total, shifted)
    return jnp.where(shifted >= total, shifted - total, shifted)


def ranks(offsets):
    rows = offsets.shape[0]
    r, c = iota((LANES, LANES), 0), iota((LANES, LANES), 1)
    before = ones_where(r < c)
    every = jnp.ones((LANES, LANES), BF16)
    earlier = ones_where(iota((rows, rows), 1) < iota((rows, rows), 0))
    result = []
    for o in range(NEIGHBOR_TILES):
        mask = offsets == o
        hot = ones_where(mask)
        inside = dot(hot, before)
        count = dot(hot, every)
        base = dot(earlier, count.astype(BF16))
        result.append((mask, hot, inside, count, base))
    return result


def route_kernel(sent, total, x_hbm, dest_hbm, *rest):
    staged = len(rest) - len(sent) - 8
    sources, rest = rest[: staged // 2], rest[staged // 2 :]
    outs, dest_ref, rest = rest[: len(sent)], rest[len(sent)], rest[len(sent) + 1 :]
    targets, rest = rest[: staged // 2], rest[staged // 2 :]
    x_ref, comb, place, pos_scr, vec, scal, sem = rest
    copies = [
        pltpu.make_async_copy(a, b, sem.at[i])
        for i, (a, b) in enumerate(
            zip((dest_hbm, x_hbm) + tuple(sources), (dest_ref, x_ref) + tuple(targets))
        )
    ]
    for copy in copies:
        copy.start()
    copies[0].wait()
    blocks = dest_ref.shape[0]
    unit = SORT_UNIT
    groups = outs[0].shape[0] // 4
    stride = (groups + 1) * 8
    offsets = offsets_of(dest_ref[...], total)
    ones8 = jnp.ones((8, LANES), BF16)
    sub8 = iota((8, blocks), 0)
    earlier = ones_where(iota((blocks, blocks), 0) < iota((blocks, blocks), 1))
    before = ones_where(iota((LANES, 2 * LANES), 0) < iota((LANES, 2 * LANES), 1))
    hots = [ones_where(offsets == o) for o in range(NEIGHBOR_TILES)]
    counts = jnp.zeros((8, blocks), F32)
    start_t = jnp.zeros((8, blocks), F32)
    starts = jnp.zeros((8, blocks), F32)
    for o, hot in enumerate(hots):
        count_t = dot_t(ones8, hot)
        counts = jnp.where(sub8 == o, count_t, counts)
        starts = jnp.where(sub8 == o, start_t, starts)
        start_t = start_t + count_t
    base = dot(counts.astype(BF16), earlier).astype(I32)
    counts, starts = counts.astype(I32), starts.astype(I32)
    at = jnp.bitwise_and(base, LANES - 1)
    vec[0:8, :] = sub8 * stride + lax.shift_right_logical(base, 7) * 8
    vec[8:16, :] = jnp.bitwise_and(at - starts, LANES - 1)
    vec[16:24, :] = at
    vec[24:32, :] = at + counts - LANES
    copy = pltpu.make_async_copy(vec, scal, sem.at[len(copies)])
    copy.start()
    start = jnp.zeros((blocks, LANES), F32)
    pos = jnp.zeros((blocks, LANES), F32)
    for o, hot in enumerate(hots):
        inside = dot(hot, before)
        pos = jnp.where(offsets == o, start + inside[:, :LANES], pos)
        start = start + inside[:, LANES:]
    pos_scr[...] = pos.astype(I32)
    f, g = iota((8, 8), 1), jnp.bitwise_and(iota((8, 8), 0), 3)
    plus = ((g == 0) & (f == 0)) | ((g == 1) & (f == 1)) | ((g == 2) & (f == 3)) | ((g == 3) & (f >= 6))
    minus = ((g == 2) & (f == 2)) | ((g == 3) & ((f == 4) | (f == 5)))
    combine = (jnp.where(plus, 1.0, 0.0) - jnp.where(minus, 1.0, 0.0)).astype(BF16)
    copies[1].wait()
    comb[...] = dot(combine, x_ref[...]).astype(BF16)

    lines = iota((LANES, LANES), 0)

    def sort_blocks(i):
        result = []
        for u in range(0, unit, 2):
            b = i * unit + u
            columns = comb[:, pl.ds(pl.multiple_of(b * LANES, 2 * LANES), 2 * LANES)].astype(F32)
            columns = jnp.concatenate([columns[:, :LANES], columns[:, LANES:]], axis=0).astype(BF16)
            hot = [ones_where(pos_scr[pl.ds(b + v, 1), :] == lines) for v in range(2)]
            both = dot_t(columns, jnp.concatenate(hot, axis=0))
            result += [both[:8, :LANES], both[8:, LANES:]]
        return result

    lane = iota((8, LANES), 1)

    def place_blocks(i, values, current):
        current = list(current)
        for u in range(unit):
            b = i * unit + u
            for o in range(NEIGHBOR_TILES):
                turned = pltpu.roll(values[u], scal[8 + o, b], 1)
                merged = jnp.where(lane < scal[16 + o, b], current[o], turned)
                place[pl.ds(pl.multiple_of(scal[o, b], 8), 8), :] = merged
                current[o] = jnp.where(lane < scal[24 + o, b], turned, merged)
        return current

    def step(i, carry):
        values = sort_blocks(i + 1)
        return tuple(place_blocks(i, carry[NEIGHBOR_TILES:], carry[:NEIGHBOR_TILES])) + tuple(values)

    steps = blocks // unit
    current = [jnp.zeros((8, LANES), F32) for _ in range(NEIGHBOR_TILES)]
    values = sort_blocks(0)
    copy.wait()
    carry = lax.fori_loop(0, steps - 1, step, tuple(current) + tuple(values))
    current = place_blocks(steps - 1, carry[NEIGHBOR_TILES:], carry[:NEIGHBOR_TILES])
    pair_lane = jnp.where(iota((8, LANES), 0) < 4, lane, lane + LANES)
    upper = iota((groups // 2, 8, LANES), 1) < 4
    slot = iota((groups // 2, 8, LANES), 0) * (2 * LANES) + pair_lane[None]
    last = blocks - 1

    def length(o):
        return (scal[o, last] - o * stride) * (LANES // 8) + scal[24 + o, last] + LANES

    for o in range(NEIGHBOR_TILES):
        full = lax.shift_right_logical(length(o), 7) * 8 + o * stride
        place[pl.ds(pl.multiple_of(full, 8), 8), :] = current[o]
    for offset, out in zip(sent, outs):
        o = pick(offset)
        tiles = place[pl.ds(pl.multiple_of(o * stride, 8), groups * 8), :]
        tiles = tiles.reshape(groups // 2, 2, 8, LANES)
        both = jnp.where(upper, tiles[:, 0], tiles[:, 1])
        both = jnp.where(slot < length(o), both, 0.0)
        out[...] = both.reshape(groups * 4, LANES).astype(BF16)
    for copy in copies[2:]:
        copy.wait()


def prepare_kernel(
    total, dest_ref, row_ref, ocean_ref, depth_ref, mask_ref,
    blocks_ref, edge_rows, edge_columns, index_ref, code_ref, *hot_refs
):
    blocks = dest_ref.shape[0]
    groups = hot_refs[0].shape[1]
    offsets = offsets_of(dest_ref[...], total)
    index = jnp.zeros((blocks, LANES), I32)
    code = jnp.zeros((blocks, LANES), I32)
    group_id = iota((blocks, groups), 1)
    lane = iota((blocks, LANES), 1)
    for o, (mask, hot, inside, count, base) in enumerate(ranks(offsets)):
        base = base.astype(I32)
        rank = base + inside.astype(I32)
        first = lax.shift_right_logical(base, 7)
        index = jnp.where(mask, jnp.bitwise_and(rank, LANES - 1), index)
        code = jnp.where(mask, code + o, code)
        code = jnp.where(lane >= jnp.bitwise_and(base, LANES - 1), code + (8 << o), code)
        hot_refs[o][0:blocks, :] = ones_where(group_id == first[:, :groups])
        hot_refs[o][blocks:, :] = ones_where(group_id == first[:, :groups] + 1)
    index_ref[...] = index
    code_ref[...] = code
    row = jnp.concatenate([row_ref[0:1, :], row_ref[1:2, :]], axis=1)
    blocks_ref[...] = ones_where(iota(blocks_ref.shape, 0) == row)
    fields = [ocean_ref[0], ocean_ref[1], ocean_ref[2], mask_ref[...].astype(F32), depth_ref[...]]
    for i, low in enumerate((False, True)):
        edge_rows[i] = packed_rows(fields, low).astype(BF16)
        edge_columns[i] = packed_columns(fields, low, 0).astype(BF16)


def packed_columns(fields, low, start):
    lane = iota(fields[0].shape, 1)
    packed = None
    for i, field in enumerate(fields, start):
        turn = (i * HALO + (0 if low else HALO)) % LANES
        turned = pltpu.roll(field, turn, 1) if turn else field
        packed = turned if packed is None else jnp.where(lane >= i * HALO, turned, packed)
    return packed


def packed_rows(fields, low):
    tall = fields[0].shape[0]
    span = slice(0, HALO) if low else slice(tall - HALO, tall)
    return jnp.concatenate([x[span] for x in fields], axis=0)


def remap_kernel(came, returns, edges, *rest):
    arrived, rest = rest[: len(came)], rest[len(came) :]
    ptr_vmem, hot_ref, edge_rows, edge_columns, w_ref, skin_ref, mask_ref = rest[:7]
    forcing_ref, own_ref = rest[7:9]
    message_refs = rest[9 : 9 + len(returns)]
    slots, mapped, shares, homebound, bank, ptr_ref, sem = rest[9 + len(returns) :]
    pointers = pltpu.make_async_copy(ptr_vmem, ptr_ref, sem)
    pointers.start()
    per_step = 8
    size = arrived[0].shape[0]
    for offset, block in zip(came, arrived):
        o = pick(offset)
        slots[pl.ds(pl.multiple_of(o * size, size), size), :] = block[...].astype(F32)
    slots[NEIGHBOR_TILES * size :, :] = jnp.zeros((8, LANES), F32)
    rows = HALO * FIELDS
    for i in range(2):
        bank[i * rows : i * rows + edge_rows.shape[1], :] = edge_rows[i]
    bank[bank.shape[0] - rows :, :] = jnp.zeros((rows, LANES), BF16)
    pointers.wait()
    sub = iota((per_step, LANES), 0)

    def forward(step):
        for j in range(per_step):
            k = step * per_step + j
            both = [slots[pl.ds(ptr_ref[w, k] * 4, 8), :] for w in range(2)]
            both = jnp.concatenate(both, axis=0).astype(BF16)
            product = dot_t(both, w_ref[k].reshape(2 * LANES, LANES))
            mapped[pl.ds(k * 8, 8), :] = product[:8, :LANES] + product[8:, LANES:]

    def middle(step):
        rows = pl.ds(step * per_step, per_step)
        u, v, p, h = (mapped[pl.ds(step * per_step * 8 + i, per_step, stride=8), :] for i in range(4))
        speed = jnp.sqrt(u * u + v * v + 1.0)
        forcing_ref[0, rows, :] = 0.2 * speed * u
        forcing_ref[1, rows, :] = 0.2 * speed * v
        forcing_ref[2, rows, :] = 0.5 * p
        return (skin_ref[rows, :] + 0.25 * mask_ref[rows, :].astype(F32) * h).astype(BF16).astype(F32)

    def back(step, sst):
        left = []
        for j in range(per_step):
            only = jnp.where(sub == j, sst, 0.0)
            zero = jnp.zeros_like(only)
            left.append(jnp.concatenate([only, zero], axis=0).astype(BF16))
            left.append(jnp.concatenate([zero, only], axis=0).astype(BF16))
        left = jnp.concatenate(left, axis=1)
        right = w_ref[pl.ds(step * per_step, per_step)].reshape(per_step * 2 * LANES, LANES)
        total = dot(left, right)
        for w in range(2):
            rows = slice((w * steps + step) * per_step, (w * steps + step + 1) * per_step)
            shares[rows, :] = total[w * per_step : (w + 1) * per_step]

    steps = w_ref.shape[0] // per_step
    for i in range(steps):
        forward(i)
    for i in range(steps):
        back(i, middle(i))

    every = shares[...]
    high = every.astype(BF16)
    low = (every - high.astype(F32)).astype(BF16)
    split = jnp.concatenate([high, low], axis=1)
    groups = own_ref.shape[0]
    value = dot(hot_ref[...], split)
    returned = (value[:, :LANES] + value[:, LANES:]).astype(BF16)
    homebound[...] = returned
    own_ref[...] = returned[MIDDLE * groups : (MIDDLE + 1) * groups]
    fields = [forcing_ref[0], forcing_ref[1], forcing_ref[2]]
    tall = fields[0].shape[0]
    rows = HALO * FIELDS
    still = HALO * (FIELDS - len(fields))
    lane = iota((tall, LANES), 1)
    for i, low in enumerate((False, True)):
        bank[i * rows + still : (i + 1) * rows, :] = packed_rows(fields, low).astype(BF16)
        columns = packed_columns(fields, low, FIELDS - len(fields))
        columns = jnp.where(lane < still, edge_columns[i].astype(F32), columns)
        bank[2 * rows + i * tall : 2 * rows + (i + 1) * tall, :] = columns.astype(BF16)
    for offset, edge, out in zip(returns, edges, message_refs):
        first = pl.multiple_of(pick(offset) * groups, 16)
        out[0:groups, :] = homebound[pl.ds(first, groups), :]
        first = pl.multiple_of(pick(edge), 16)
        out[groups:, :] = bank[pl.ds(first, rows), :]


def finish_kernel(sources, halos, count_t, count_s, messages, *rest):
    message_refs, rest = rest[:messages], rest[messages:]
    own_ref, index_ref, code_ref = rest[:3]
    hot_refs, rest = rest[3 : 3 + NEIGHBOR_TILES], rest[3 + NEIGHBOR_TILES :]
    ocean_ref, depth_ref, mask_ref, forcing_ref, out_ref, warm_ref, inbox, shifted = rest
    t, s = lax.axis_index("tile"), lax.axis_index("sub")
    size = message_refs[0].shape[0]
    groups = own_ref.shape[0]
    for i, ref in enumerate(message_refs):
        inbox[i * size : (i + 1) * size, :] = ref[...]
    blocks = index_ref.shape[0]
    index = index_ref[...]
    code = code_ref[...]
    warm = jnp.zeros((blocks, LANES), F32)

    def warmth(o, warm):
        if o == MIDDLE:
            value = own_ref[...]
        else:
            value = inbox[pl.ds(pl.multiple_of(pick(sources[o]) * size, 16), groups), :]
        lines = dot(hot_refs[o][...], value)
        upper = jnp.bitwise_and(code, 8 << o) != 0
        lines = jnp.where(upper, lines[:blocks], lines[blocks:])
        picked = jnp.take_along_axis(lines, index, axis=1)
        return jnp.where(jnp.bitwise_and(code, 7) == o, picked, warm)

    tall = depth_ref.shape[0]
    full = tall + 2 * HALO

    def halo(dt, ds):
        ok = jnp.bool_(True)
        if dt == 1:
            ok &= t > 0
        if dt == -1:
            ok &= t < count_t - 1
        if ds == 1:
            ok &= s > 0
        if ds == -1:
            ok &= s < count_s - 1
        rows = tall if dt == 0 else (HALO if ds else HALO * FIELDS)
        first = pl.multiple_of(pick(halos[dt, ds]) * size + groups, 16)
        value = inbox[pl.ds(first, rows), :].astype(F32)
        return jnp.where(ok, value, 0.0)

    from_left = jnp.concatenate([halo(1, 1), halo(0, 1), halo(-1, 1)], axis=0)
    from_right = jnp.concatenate([halo(1, -1), halo(0, -1), halo(-1, -1)], axis=0)
    above, below = halo(1, 0), halo(-1, 0)
    lane = iota((full, LANES), 1)
    inner = [ocean_ref[0], ocean_ref[1], ocean_ref[2], mask_ref[...].astype(F32), depth_ref[...]]
    inner += [forcing_ref[0], forcing_ref[1], forcing_ref[2]]
    wide = []
    for i in range(FIELDS):
        rows = slice(i * HALO, (i + 1) * HALO)
        main = jnp.concatenate([above[rows], inner[i], below[rows]], axis=0)
        turn = (LANES - HALO - i * HALO) % LANES
        left = pltpu.roll(from_left, turn, 1) if turn else from_left
        turn = (LANES - i * HALO) % LANES
        right = pltpu.roll(from_right, turn, 1) if turn else from_right
        side = jnp.where(lane < HALO, right, jnp.where(lane >= LANES - HALO, left, 0.0))
        wide.append([main, side])
    eta, east, north, m, depth, stress_x, stress_y, fresh = wide
    row = iota((full, LANES), 0) + (t * tall - HALO)
    coriolis = 0.1 + 0.2 * (row.astype(F32) + 0.5) / (tall * count_t)

    both = range(2)
    half_m = [0.5 * m[i] for i in both]
    half_d = [half_m[i] * depth[i] for i in both]
    turning = [m[i] * coriolis for i in both]
    fresh = [m[i] * fresh[i] for i in both]
    stress_x = [m[i] * stress_x[i] for i in both]
    stress_y = [m[i] * stress_y[i] for i in both]
    shifted[:, 0:8, :] = jnp.zeros((4, 8, LANES), F32)
    shifted[:, 8 + full :, :] = jnp.zeros((4, 8, LANES), F32)

    def across(a):
        ahead = [pltpu.roll(a[i], LANES - 1, 1) for i in both]
        behind = [pltpu.roll(a[i], 1, 1) for i in both]
        columns = lane[: a[0].shape[0]]
        return [
            jnp.where(columns == LANES - 1, ahead[1 - i], ahead[i])
            - jnp.where(columns == 0, behind[1 - i], behind[i])
            for i in both
        ]

    def along(a, first, rows, place):
        result = []
        for i in both:
            shifted[place + i, 8 + first : 8 + first + a[i].shape[0], :] = a[i]
            result.append(
                shifted[place + i, 9 + rows.start : 9 + rows.stop, :]
                - shifted[place + i, 7 + rows.start : 7 + rows.stop, :]
            )
        return result

    first, last = 0, full
    out_east, out_north = across(east), along(north, 0, slice(0, full), 0)
    eta, east, north = ([m[i] * a[i] for i in both] for a in (eta, east, north))
    for step in range(1, SUBS + 1):
        if step > 1:
            out_east, out_north = across(east), along(north, first, slice(first, last), 0)
        eta = [eta[i] + fresh[i] - half_m[i] * (out_east[i] + out_north[i]) for i in both]
        below_first = 2 * step // 8 * 8
        slope_y = along(eta, first, slice(below_first, full - below_first), 2)
        if below_first > first:
            cut = slice(below_first - first, full - below_first - first)
            eta, east, north, turning, stress_x, stress_y, half_d, fresh, half_m = (
                [x[cut] for x in a]
                for a in (eta, east, north, turning, stress_x, stress_y, half_d, fresh, half_m)
            )
            first, last = below_first, full - below_first
        slope_x = across(eta)
        if step <= NEIGHBOR_TILES:
            warm = warmth(step - 1, warm)
        new_east = [
            east[i] + turning[i] * north[i] + stress_x[i] - half_d[i] * slope_x[i] for i in both
        ]
        north = [
            north[i] - turning[i] * east[i] + stress_y[i] - half_d[i] * slope_y[i] for i in both
        ]
        east = new_east
    warm_ref[...] = warm
    for i, a in enumerate((eta, east, north)):
        out_ref[i] = a[0][HALO - first : HALO - first + tall]


SCHEDULES = {
    (4, 2): (
        [
            [2, 3, 4, 1, 6, 7, 0, 5],
            [7, 2, 1, 5, 3, 6, 4, 0],
            [6, 7, 0, 4, 2, 3, 5, 1],
            [1, 0, 3, 2, 5, 4, 7, 6],
        ],
        [
            [3, 6, 5, 0, 7, 2, 1, 4],
            [2, 3, 4, 1, 6, 7, 0, 5],
            [7, 2, 1, 4, 3, 6, 5, 0],
            [6, 7, 0, 5, 2, 3, 4, 1],
            [1, 0, 3, 2, 5, 4, 7, 6],
        ],
    ),
}


def schedule(count_t, count_s):
    total = count_t * count_s
    if (count_t, count_s) in SCHEDULES:
        return SCHEDULES[count_t, count_s]
    rings = [
        [(i + distance) % total for i in range(total)]
        for distance in range(-MIDDLE, MIDDLE + 1)
        if distance
    ]
    others = []
    for dt in (-1, 1):
        for ds in (-1, 0, 1):
            if MIDDLE < abs(dt * count_s + ds):
                targets = [-1] * total
                for device in range(total):
                    t, s = device // count_s + dt, device % count_s + ds
                    if 0 <= t < count_t and 0 <= s < count_s:
                        targets[device] = t * count_s + s
                others.append(targets)
    return rings, rings + others


def plan(count_t, count_s, groups, tall):
    total = count_t * count_s
    outward, homeward = schedule(count_t, count_s)

    def offset(a, b):
        o = (b - a + MIDDLE) % total
        return o if o < NEIGHBOR_TILES else -1

    def step(a, b):
        dt, ds = b // count_s - a // count_s, b % count_s - a % count_s
        return (dt, ds) if abs(dt) <= 1 and abs(ds) <= 1 else None

    def senders(targets):
        return [targets.index(d) if d in targets else -1 for d in range(total)]

    rows = HALO * FIELDS
    start = {(1, 0): 0, (-1, 0): rows}
    for ds, first in ((1, 2 * rows), (-1, 2 * rows + tall)):
        start[0, ds] = start[-1, ds] = first
        start[1, ds] = first + tall - HALO
    result = {"outward": outward, "homeward": homeward}
    result["sent"] = [[offset(a, b) for a, b in enumerate(p)] for p in outward]
    result["sent"].insert(0, [MIDDLE] * total)
    result["came"] = [[offset(a, b) for b, a in enumerate(senders(p))] for p in outward]
    result["came"].insert(0, [MIDDLE] * total)
    result["returns"] = [
        [max(offset(b, a), 0) if b >= 0 else 0 for a, b in enumerate(p)] for p in homeward
    ]
    result["edges"] = [
        [start[step(a, b)] if b >= 0 and step(a, b) else 0 for a, b in enumerate(p)] for p in homeward
    ]
    sources = [[0] * total for _ in range(NEIGHBOR_TILES)]
    halos = {(dt, ds): [0] * total for dt in (-1, 0, 1) for ds in (-1, 0, 1)}
    for i, p in enumerate(homeward):
        for a, b in enumerate(p):
            if b >= 0:
                if offset(b, a) >= 0:
                    sources[offset(b, a)][b] = i
                if step(a, b):
                    halos[step(a, b)][b] = i
    result["sources"], result["halos"] = sources, halos
    return result


def shards(
    air_exchanges,
    air_destination,
    diagonal_group_pointer,
    interpolation_factors,
    marine_fields,
    skin_warmth_anomaly,
    gravity_bathymetry,
    marine_indicator,
):
    axes = ("tile", "sub")
    count_t, count_s = lax.axis_size("tile"), lax.axis_size("sub")
    total = count_t * count_s
    columns = air_destination.shape[1]
    blocks = columns // LANES
    groups = columns // 2 // LANES
    destination = air_destination.reshape(blocks, LANES)
    vmem = pl.BlockSpec(memory_space=pltpu.VMEM)
    params = pltpu.CompilerParams(vmem_limit_bytes=VMEM_LIMIT)
    hbm = pl.BlockSpec(memory_space=pltpu.HBM)
    pointers = diagonal_group_pointer[0, 0, 0].T
    to_stage = (
        pointers,
        interpolation_factors[0, 0, 0],
        marine_fields[0],
        skin_warmth_anomaly[0],
        gravity_bathymetry[0],
        marine_indicator[0],
    )
    tall = skin_warmth_anomaly.shape[1]
    moves = plan(count_t, count_s, groups, tall)
    sends = len(moves["sent"])
    results = pl.pallas_call(
        functools.partial(route_kernel, moves["sent"], total),
        out_shape=[jax.ShapeDtypeStruct((groups * 4, LANES), BF16)] * sends
        + [jax.ShapeDtypeStruct(a.shape, a.dtype) for a in (destination,) + to_stage],
        in_specs=[hbm] * (2 + len(to_stage)),
        out_specs=[vmem] * (sends + 1 + len(to_stage)),
        scratch_shapes=[
            pltpu.VMEM((8, columns), BF16),
            pltpu.VMEM((8, columns), BF16),
            pltpu.VMEM((NEIGHBOR_TILES * (groups + 1) * 8, LANES), F32),
            pltpu.VMEM((blocks, LANES), I32),
            pltpu.VMEM((32, blocks), I32),
            pltpu.SMEM((32, blocks), I32),
            pltpu.SemaphoreType.DMA((3 + len(to_stage),)),
        ],
        compiler_params=params,
        name="route",
    )(*(pltpu.with_memory_space_constraint(a, pltpu.HBM) for a in (air_exchanges[0], destination) + to_stage))
    destination, rows, weights, ocean, skin, depth, mask = results[sends:]

    def send(array, targets):
        return lax.ppermute(array, axes, [(a, b) for a, b in enumerate(targets) if b >= 0])

    arrived = [results[0]] + [send(a, p) for a, p in zip(results[1:], moves["outward"])]
    prepared = pl.pallas_call(
        functools.partial(prepare_kernel, total),
        out_shape=[
            jax.ShapeDtypeStruct((NEIGHBOR_TILES * groups, LANES), BF16),
            jax.ShapeDtypeStruct((2, HALO * (FIELDS - 3), LANES), BF16),
            jax.ShapeDtypeStruct((2, tall, LANES), BF16),
        ]
        + [jax.ShapeDtypeStruct((blocks, LANES), I32)] * 2
        + [jax.ShapeDtypeStruct((2 * blocks, groups), BF16)] * NEIGHBOR_TILES,
        in_specs=[vmem] * 5,
        out_specs=[vmem] * (5 + NEIGHBOR_TILES),
        compiler_params=params,
        cost_estimate=pl.CostEstimate(flops=2 * 15 * LANES**3, bytes_accessed=2**19, transcendentals=0),
        name="prepare",
    )(destination, rows, ocean, depth, mask)
    returns = len(moves["returns"])
    message = (groups + HALO * FIELDS, LANES)
    row_blocks = weights.shape[0]
    outs = pl.pallas_call(
        functools.partial(remap_kernel, moves["came"], moves["returns"], moves["edges"]),
        out_shape=[
            jax.ShapeDtypeStruct((3, tall, LANES), F32),
            jax.ShapeDtypeStruct((groups, LANES), BF16),
        ]
        + [jax.ShapeDtypeStruct(message, BF16)] * returns,
        in_specs=[vmem] * (sends + 7),
        out_specs=[vmem] * (2 + returns),
        scratch_shapes=[
            pltpu.VMEM((NEIGHBOR_TILES * groups * 4 + 8, LANES), F32),
            pltpu.VMEM((row_blocks * 8, LANES), F32),
            pltpu.VMEM((2 * row_blocks, LANES), F32),
            pltpu.VMEM((NEIGHBOR_TILES * groups, LANES), BF16),
            pltpu.VMEM((3 * HALO * FIELDS + 2 * tall, LANES), BF16),
            pltpu.SMEM(pointers.shape, I32),
            pltpu.SemaphoreType.DMA,
        ],
        compiler_params=params,
        name="remap",
    )(*arrived, rows, *prepared[:3], weights, skin, mask)
    forcing, own = outs[:2]
    received = [send(a, p) for a, p in zip(outs[2:], moves["homeward"])]
    ocean_out, warm = pl.pallas_call(
        functools.partial(
            finish_kernel, moves["sources"], moves["halos"], count_t, count_s, returns
        ),
        out_shape=[
            jax.ShapeDtypeStruct((3, tall, LANES), F32),
            jax.ShapeDtypeStruct((blocks, LANES), F32),
        ],
        in_specs=[vmem] * (returns + 3 + NEIGHBOR_TILES + 4),
        out_specs=[vmem] * 2,
        scratch_shapes=[
            pltpu.VMEM((returns * message[0], LANES), BF16),
            pltpu.VMEM((4, tall + 2 * HALO + 16, LANES), F32),
        ],
        compiler_params=params,
        name="finish",
    )(*received, own, *prepared[3:], ocean, depth, mask, forcing)
    return ocean_out[None], warm.reshape(1, columns)


def solution(mesh):
    return jax.shard_map(
        shards,
        mesh=mesh,
        in_specs=(
            P(("member", "comp"), None, ("tile", "sub")),
            P("comp", ("tile", "sub"), None),
            P("comp", "tile", "sub", None, None),
            P("comp", "tile", "sub", None, None, None, None),
            P(("member", "comp"), None, "tile", "sub"),
            P(("member", "comp"), "tile", "sub"),
            P("comp", "tile", "sub"),
            P("comp", "tile", "sub"),
        ),
        out_specs=(
            P(("member", "comp"), None, "tile", "sub"),
            P(("member", "comp"), ("tile", "sub")),
        ),
        check_vma=False,
    )
```
